256 devices in a mesh: dp: 4 (over x), table: 32 (over y, z), col: 2 (over core).
Axes of the slice: x: 4, y: 4, z: 8, core: 2. Of those that a mesh axis runs over, the one named last changes fastest.
Arguments:
- table: float32 [131072, 768], P(('dp', 'table'), 'col'), may hold values from -6 to 6
- accum: float32 [131072], P(('dp', 'table')), may hold values from 0.05 to 0.5
- serve_rows: int32 [128, 512], P(('dp', 'table')), may hold values from 0 to 1023, as said below
- seed_slot: int32 [1024], P(('dp', 'table')), may hold values from 0 to 511
- hop1_slot: int32 [1024, 15], P(('dp', 'table')), may hold values from 0 to 511
- hop2_slot: int32 [1024, 15, 10], P(('dp', 'table')), may hold values from 0 to 511
- hop1_rel: int32 [1024, 15], P(('dp', 'table')), may hold values from 0 to 1
- hop2_rel: int32 [1024, 15, 10], P(('dp', 'table')), may hold values from 0 to 1
- cotangent: bfloat16 [1024, 1024], P(('dp', 'table')), may hold values from -24 to 24
- w_first: bfloat16 [3, 768, 1024], P(None, 'col'), may hold values from -0.5 to 0.5
- w_second: bfloat16 [3, 1024, 1024], replicated, may hold values from -0.109375 to 0.109375
Outputs:
- new_table: float32 [131072, 768], P(('dp', 'table'), 'col')
- new_accum: float32 [131072], P(('dp', 'table'))
- grad_first: float32 [3, 768, 1024], P(None, 'col', ('dp', 'table'))
- grad_second: float32 [3, 1024, 1024], P(None, 'col', ('dp', 'table'))
The draws below stay inside these ranges and needn't reach their ends.
Inputs may be any that keep to these rules, and one draw needn't show every extreme that they name: `serve_rows`: the 4 entries of one owner for one fetching index are distinct rows.
All inputs are finite; a program needn't handle non-finite values.
Results may differ from the reference program's by a relative error of at most 0.0065.
Values may be sent and summed in bfloat16 or wider, within the bound.
No kernel may reach another device: no remote copies, remote signals or barrier semaphores. Data moves between devices by JAX's collectives and lax.ppermute only.
A program may use at most 128 MiB of HBM per device.

```python
import math
import jax
import jax.numpy as jnp
from jax import lax

D = 768
HID = 1024
REL = 2
F1 = 15
F2 = 10
SEEDS_DEV = 8
ROWS_DEV = 1024
SLOTS_DEV = 512
SEEDS = 1024
TABLE_ROWS = 131072
N_DP = 4
N_TABLE = 32


def draw_serve_rows(key, part):
    key = jax.random.fold_in(key, 7)
    owners = N_DP * N_TABLE
    per_owner = SLOTS_DEV // owners
    scores = jax.random.randint(key, (owners * owners, ROWS_DEV), 0, 2 ** 30 // ROWS_DEV) * ROWS_DEV
    scores = scores + jnp.arange(ROWS_DEV, dtype=jnp.int32)[None, :]
    picked = jnp.argsort(scores, axis=-1)[:, :per_owner]
    return picked.astype(jnp.int32).reshape(owners, SLOTS_DEV)


def scaled_rows(entries, spread):
    position = jnp.arange(D, dtype=jnp.float32) / (D - 1.0)
    factor = jnp.exp(jnp.log(spread) * (position - 0.5))
    return entries * factor[None, :, None] * ((1.0 + REL) * D) ** (-0.5)


def draw_w_first(key, part):
    key = jax.random.fold_in(key, 11)
    shape = (1 + REL, D, HID)
    entries = jax.random.truncated_normal(key, -6.0, 6.0, shape, jnp.float32)
    return scaled_rows(entries, 4.0).astype(jnp.bfloat16)


def set_ends(values, key, low, high):
    extent = values.shape
    place = [jax.random.randint(jax.random.fold_in(key, axis), (), 0, extent[axis]) for axis in range(len(extent))]
    values = values.at[tuple(place)].set(low)
    longest = extent.index(max(extent))
    place[longest] = (place[longest] + 1) % extent[longest]
    return values.at[tuple(place)].set(high)


def strengthened(result, rng, source, target, blocks, factor):
    owner, partner = [(jnp.arange(result.shape[axis_at]) // (result.shape[axis_at] // blocks)).reshape([-1 if axis == axis_at else 1 for axis in range(result.ndim)]) for axis_at in (source, target)]
    chosen = jax.random.permutation(rng, blocks)[partner]
    strong = (owner == chosen) | (owner == (partner + blocks // 2) % blocks)
    return jnp.where(strong, factor * result, result)


def steps_of(key, dims, cuts, least, high):
    loudness, own = 1.0, jax.random.fold_in(key, 6)
    for dim, blocks in cuts:
        steps = jnp.exp(jax.random.uniform(jax.random.fold_in(own, dim), (blocks,), jnp.float32, least / len(cuts), high / len(cuts)))
        loudness = loudness * jnp.repeat(steps, dims[dim] // blocks).reshape([-1 if axis == dim else 1 for axis in range(len(dims))])
    return loudness


def bell_draw(rng, shape, width, bound, cuts=(), held_as=jnp.bfloat16):
    result = jax.random.normal(rng, shape, jnp.float32) * width
    if len(cuts) > 0:
        result = steps_of(rng, shape, cuts, -0.22, 0.18) * result
    return jnp.clip(result, min=-bound, max=bound).astype(held_as)


def noise_with(rng, extent, deviation, limit, split, heavy, kind=jnp.bfloat16):
    result = deviation * jax.random.normal(rng, extent, jnp.float32)
    if split:
        result = result * steps_of(rng, extent, split, -0.22, 0.18)
    return jnp.clip(strengthened(result, jax.random.fold_in(rng, 3), *heavy), -limit, limit).astype(kind)


def setup_inputs(seed: int = 0) -> dict:
    key_list = jax.random.split(jax.random.key(seed), 12)
    return {
        "table": bell_draw(key_list[0], (TABLE_ROWS, D), 1.0, 6.0, ((0, 128), (1, 2)), jnp.float32),
        "accum": jnp.clip(jnp.exp(math.log(0.5) - 2.3025851 * jax.random.uniform(key_list[1], (TABLE_ROWS,), jnp.float32) ** steps_of(key_list[1], (TABLE_ROWS,), ((0, 128),), -0.2, 0.2)), 0.05, 0.5),
        "serve_rows": draw_serve_rows(jax.random.fold_in(key_list[11], 71), 0),
        "seed_slot": set_ends(jax.random.randint(key_list[3], (SEEDS,), 0, SLOTS_DEV), jax.random.fold_in(key_list[3], 1), 0, SLOTS_DEV - 1).astype(jnp.int32),
        "hop1_slot": set_ends(jax.random.randint(key_list[4], (SEEDS, F1), 0, SLOTS_DEV), jax.random.fold_in(key_list[4], 1), 0, SLOTS_DEV - 1).astype(jnp.int32),
        "hop2_slot": set_ends(jax.random.randint(key_list[5], (SEEDS, F1, F2), 0, SLOTS_DEV), jax.random.fold_in(key_list[5], 1), 0, SLOTS_DEV - 1).astype(jnp.int32),
        "hop1_rel": set_ends(jax.random.randint(key_list[6], (SEEDS, F1), 0, REL), jax.random.fold_in(key_list[6], 1), 0, REL - 1).astype(jnp.int32),
        "hop2_rel": set_ends(jax.random.randint(key_list[7], (SEEDS, F1, F2), 0, REL), jax.random.fold_in(key_list[7], 1), 0, REL - 1).astype(jnp.int32),
        "cotangent": noise_with(key_list[8], (SEEDS, HID), 1.0, 24.0, ((0, 128),), (0, 1, 128, 5.5)),
        "w_first": draw_w_first(jax.random.fold_in(key_list[11], 71), 0),
        "w_second": bell_draw(key_list[10], (1 + REL, HID, HID), ((1 + REL) * HID) ** -0.5, 0.109375),
    }


LEARNING_RATE = 0.1

def relation_means(features, relation, relations):
    onehot = (relation[..., None] == jnp.arange(relations, dtype=jnp.int32)).astype(jnp.float32)
    counts = lax.optimization_barrier(jnp.sum(onehot, axis=-2))
    inverse = 1.0 / jnp.maximum(counts, 1.0)
    totals = jnp.einsum('...kr,...kc->...rc', onehot, features.astype(jnp.float32))
    return ((totals * inverse[..., None]).astype(jnp.bfloat16), onehot * inverse[..., None, :])

def to_bf16_value(array):
    rounded = lax.optimization_barrier(array.astype(jnp.bfloat16))
    return rounded.astype(jnp.float32)

def silu_slope(values):
    sigma = jax.nn.sigmoid(values)
    return sigma * (1.0 + values * (1.0 - sigma))

def reference(table, accum, serve_rows, seed_slot, hop1_slot, hop2_slot, hop1_rel, hop2_rel, cotangent, w_first, w_second):
    owners = N_DP * N_TABLE
    per_owner = SLOTS_DEV // owners
    relations = REL
    served = serve_rows.reshape(owners, owners, per_owner)
    offsets = (jnp.arange(owners, dtype=jnp.int32) * ROWS_DEV)[:, None, None]
    global_rows = jnp.transpose(served + offsets, (1, 0, 2)).reshape(owners, SLOTS_DEV)
    first = w_first.astype(jnp.float32)
    second = w_second.astype(jnp.float32)

    def one_device(carry, device):
        grad_one, grad_two, row_grad = carry
        row_ids = global_rows[device]
        fetched = to_bf16_value(table[row_ids])
        seed_start = (device * SEEDS_DEV).astype(jnp.int32)

        def take_block(array):
            return lax.dynamic_slice_in_dim(array, seed_start, SEEDS_DEV, 0)
        slot_seed = take_block(seed_slot)
        slot_one = take_block(hop1_slot)
        slot_two = take_block(hop2_slot)
        rel_one = take_block(hop1_rel)
        rel_two = take_block(hop2_rel)
        x_seed = fetched[slot_seed]
        x_one = fetched[slot_one]
        x_two = fetched[slot_two]
        mean_one, spread_one = relation_means(x_one, rel_one, relations)
        mean_two, spread_two = relation_means(x_two, rel_two, relations)
        self_in = jnp.concatenate([x_seed, x_one.reshape(-1, D)], 0)
        mean_in = jnp.concatenate([mean_one, mean_two.reshape(-1, relations, D)], 0).astype(jnp.float32)
        layer_in = jnp.concatenate([self_in[:, None], mean_in], 1)
        pre_act = jnp.einsum('nkc,kch->nh', layer_in, first)
        hidden = jax.nn.silu(pre_act).astype(jnp.bfloat16)
        h_seed = hidden[:SEEDS_DEV]
        h_hop = hidden[SEEDS_DEV:].reshape(SEEDS_DEV, F1, HID)
        mean_hidden, unused = relation_means(h_hop, rel_one, relations)
        second_in = jnp.concatenate([h_seed[:, None], mean_hidden], 1).astype(jnp.float32)
        cot_block = take_block(cotangent).astype(jnp.float32)
        grad_two = grad_two + jnp.einsum('skh,so->kho', second_in, cot_block)
        back_second = jnp.einsum('so,kho->skh', cot_block, second)
        back_hop = jnp.einsum('sar,srh->sah', spread_one, back_second[:, 1:])
        back_hidden = jnp.concatenate([back_second[:, 0], back_hop.reshape(-1, HID)], 0)
        back_pre = to_bf16_value(back_hidden * silu_slope(pre_act))
        grad_one = grad_one + jnp.einsum('nkc,nh->kch', layer_in, back_pre)
        back_in = jnp.einsum('nh,kch->nkc', back_pre, first)
        back_seed = back_in[:SEEDS_DEV, 0]
        back_self = back_in[SEEDS_DEV:, 0].reshape(SEEDS_DEV, F1, D)
        back_mean_one = back_in[:SEEDS_DEV, 1:]
        back_mean_two = back_in[SEEDS_DEV:, 1:].reshape(SEEDS_DEV, F1, relations, D)
        hop_one_grad = back_self + jnp.einsum('sar,src->sac', spread_one, back_mean_one)
        hop_two_grad = jnp.einsum('sabr,sarc->sabc', spread_two, back_mean_two)
        slot_grad = jnp.zeros((SLOTS_DEV, D), jnp.float32)
        slot_grad = slot_grad.at[slot_seed].add(back_seed)
        slot_grad = slot_grad.at[slot_one.reshape(-1)].add(hop_one_grad.reshape(-1, D))
        slot_grad = slot_grad.at[slot_two.reshape(-1)].add(hop_two_grad.reshape(-1, D))
        row_grad = row_grad.at[row_ids].add(slot_grad)
        return ((grad_one, grad_two, row_grad), None)
    start = (jnp.zeros((1 + REL, D, HID), jnp.float32), jnp.zeros((1 + REL, HID, HID), jnp.float32), jnp.zeros((TABLE_ROWS, D), jnp.float32))
    carry, unused = lax.scan(one_device, start, jnp.arange(owners, dtype=jnp.int32))
    grad_one, grad_two, row_grad = carry
    new_accum = accum + lax.optimization_barrier(jnp.sum(row_grad * row_grad, axis=1)) / D
    new_table = table - LEARNING_RATE * row_grad * lax.rsqrt(new_accum)[:, None]
    return (new_table, new_accum, grad_one, grad_two)
```

```python
import functools
import jax
import jax.numpy as jnp
from jax import lax
from jax.experimental import pallas as pl
from jax.experimental.pallas import tpu as pltpu
from jax.sharding import Mesh
from jax.sharding import PartitionSpec as P

LEARNING_RATE = 0.1
BF16 = jnp.bfloat16
F32 = jnp.float32
LANES = 128
SEED_ROWS = 32
COT_ROWS = 16


def matmul(a, b, contract=(1, 0)):
    dims = (((contract[0],), (contract[1],)), ((), ()))
    return lax.dot_general(a, b, dims, preferred_element_type=F32)


def row_to_column(row):
    return jnp.transpose(jnp.broadcast_to(row, (LANES, LANES)))[:, 0:1]


def column_to_row(column):
    return jnp.transpose(jnp.broadcast_to(column, (LANES, LANES)))[0:1, :]


def call(kernel, outs, operands, flops, smem=0, scratch=()):
    moved = sum(o.size * o.dtype.itemsize for o in list(operands) + list(outs))
    specs = [pl.BlockSpec(memory_space=pltpu.SMEM)] * smem
    specs += [pl.BlockSpec(memory_space=pltpu.VMEM)] * (len(operands) - smem)
    return pl.pallas_call(
        kernel,
        out_shape=tuple(outs),
        in_specs=specs,
        out_specs=tuple(pl.BlockSpec(memory_space=pltpu.VMEM) for _ in outs),
        scratch_shapes=list(scratch),
        compiler_params=pltpu.CompilerParams(vmem_limit_bytes=40 * 1024 * 1024),
        cost_estimate=pl.CostEstimate(flops=flops, bytes_accessed=moved, transcendentals=0),
    )(*operands)


def shaped(shape, dtype):
    return jax.ShapeDtypeStruct(shape, dtype)


def serve_kernel(serve_ref, table_ref, out_ref):
    rows = table_ref[...].astype(BF16)
    lanes = lax.broadcasted_iota(jnp.int32, (LANES, rows.shape[0]), 1)
    for block in range(out_ref.shape[0] // LANES):
        span = slice(block * LANES, (block + 1) * LANES)
        wanted = row_to_column(serve_ref[:, span])
        onehot = jnp.where(wanted == lanes, 1.0, 0.0).astype(BF16)
        out_ref[span, :] = matmul(onehot, rows).astype(BF16)


def index_kernel(idx_ref, cot_ref, w2_ref, ct_ref, c_ref, inv_ref, et_ref, e_ref, back_ref, spread):
    nodes = idx_ref.shape[0]
    slots = ct_ref.shape[1]
    seeds = cot_ref.shape[0]
    neighbours = idx_ref.shape[1] - 2
    lanes = lax.broadcasted_iota(jnp.int32, (nodes, 2 * slots), 1)
    idx = idx_ref[...]
    counts = jnp.zeros((nodes, 2 * slots), F32)
    for j in range(1, 1 + neighbours):
        counts = counts + jnp.where(idx[:, j : j + 1] == lanes, 1.0, 0.0)
    own = jnp.where(idx[:, 0:1] == lanes[:, :slots], 1.0, 0.0)
    parts = (own, counts[:, :slots], counts[:, slots:])
    spread[...] = jnp.zeros(spread.shape, F32)
    for k, part in enumerate(parts):
        span = slice(k * nodes, (k + 1) * nodes)
        ct_ref[span, :] = part.astype(BF16)
        c_ref[:, span] = jnp.transpose(part).astype(BF16)
        if k == 0:
            inverse = jnp.ones((nodes, 1), F32)
        else:
            inverse = 1.0 / jnp.maximum(jnp.sum(part, axis=1, keepdims=True), 1.0)
        inv_ref[span, :] = jnp.broadcast_to(inverse, (nodes, LANES))
        back = matmul(cot_ref[...], w2_ref[k], (1, 1))
        spread[k * seeds : (k + 1) * seeds, :] = back * inverse[:seeds]
    groups = lax.broadcasted_iota(jnp.int32, (nodes, LANES), 1)
    member = jnp.where(idx[:, neighbours + 1 : neighbours + 2] == groups, 1.0, 0.0)
    et_ref[...] = member.astype(BF16)
    e_ref[...] = jnp.transpose(member)[:SEED_ROWS].astype(BF16)
    whole = spread[...]
    high = whole.astype(BF16)
    low = (whole - high.astype(F32)).astype(BF16)
    back_ref[...] = matmul(member.astype(BF16), high) + matmul(member.astype(BF16), low)


def first_kernel(fetched_ref, ct_ref, inv_ref, w1_ref, layer_ref, partial_ref):
    layers = w1_ref.shape[0]
    nodes = partial_ref.shape[0]
    total = None
    for k in range(layers):
        span = slice(k * nodes, (k + 1) * nodes)
        summed = matmul(ct_ref[span, :], fetched_ref[...])
        layer = (summed * inv_ref[span, 0:1]).astype(BF16)
        layer_ref[span, :] = layer
        term = matmul(layer, w1_ref[k])
        total = term if total is None else total + term
    partial_ref[...] = total


def hidden_kernel(place_ref, mine_ref, other_ref, back_ref, e_ref, inv_ref, c_ref, w1_ref, cot_ref,
                  pack_ref, slot_ref):
    layers = w1_ref.shape[0]
    nodes = mine_ref.shape[0]
    width = pack_ref.shape[2]
    seeds = cot_ref.shape[0]
    values = mine_ref[...] + other_ref[...]
    sigma = jax.nn.sigmoid(values)
    hidden = (values * sigma).astype(BF16)
    slope = sigma * (1.0 + values * (1.0 - sigma))
    back = (back_ref[...] * slope).astype(BF16)
    scale = jnp.concatenate(
        [inv_ref[k * nodes : k * nodes + seeds, 0:1] for k in range(layers)]
        + [jnp.zeros((SEED_ROWS - layers * seeds, 1), F32)],
        0,
    )
    second = matmul(e_ref[...], hidden) * scale
    half = second.shape[1] // 2
    second = jnp.where(place_ref[0] == 0, second[:, :half], second[:, half:])
    cot = cot_ref[...].astype(F32)
    cot = jnp.concatenate([cot, jnp.zeros((COT_ROWS - seeds, cot.shape[1]), F32)], 0)
    for j in range(pack_ref.shape[0]):
        span = slice(j * width, (j + 1) * width)
        pack_ref[j, :nodes, :] = back[:, span]
        for part in range(half // width):
            first = nodes + part * SEED_ROWS
            pack_ref[j, first : first + SEED_ROWS, :] = second[
                :, part * width : (part + 1) * width
            ].astype(BF16)
        first = nodes + half // width * SEED_ROWS
        pack_ref[j, first : first + COT_ROWS, :] = cot[:, span].astype(BF16)
    total = None
    for k in range(layers):
        span = slice(k * nodes, (k + 1) * nodes)
        back_in = matmul(back, w1_ref[k], (1, 1)) * inv_ref[span, 0:1]
        term = matmul(c_ref[:, span], back_in.astype(BF16))
        total = term if total is None else total + term
    slot_ref[...] = total.astype(BF16)


def weight_kernel(place_ref, *refs):
    count = place_ref.shape[0] - 2
    layers_in = refs[:count]
    pack_ref = refs[count]
    outs = refs[count + 1 : -1]
    total = refs[-1]
    width = pack_ref.shape[2]
    columns = layers_in[0].shape[1]
    nodes = LANES
    relations = layers_in[0].shape[0] // nodes
    half = (total.shape[1] // relations) - columns
    seeds = SEED_ROWS // (relations + 1)
    packs = [pack_ref.at[place_ref[2 + d]] for d in range(count)]
    left = jnp.concatenate([p[:nodes, :] for p in packs], 0)
    pieces = half // width
    first = nodes + pieces * SEED_ROWS
    cots = jnp.concatenate([p[first : first + COT_ROWS, :].astype(F32)[:seeds] for p in packs], 0)
    seconds = [
        jnp.concatenate(
            [p[nodes + part * SEED_ROWS : nodes + (part + 1) * SEED_ROWS, :].astype(F32) for part in range(pieces)],
            1,
        )
        for p in packs
    ]
    for k in range(relations):
        right = jnp.concatenate([r[k * nodes : (k + 1) * nodes, :] for r in layers_in], 0)
        total[:, k * columns : (k + 1) * columns] = matmul(left, right, (0, 0))
        right = jnp.concatenate([s[k * seeds : (k + 1) * seeds] for s in seconds], 0).astype(BF16)
        start = relations * columns + k * half
        total[:, start : start + half] = matmul(cots.astype(BF16), right, (0, 0))
    rows = outs[0].shape[0]
    for d, out in enumerate(outs):
        target = lax.rem(place_ref[1] + d, len(outs))
        block = total[pl.ds(pl.multiple_of(target * rows, rows), rows), :]
        out[...] = block.astype(out.dtype)


def row_kernel(serve_ref, arrived_ref, grad_ref, square_ref):
    rows = lax.broadcasted_iota(jnp.int32, (LANES, serve_ref.shape[1]), 0)
    arrived = arrived_ref[...]
    for block in range(grad_ref.shape[0] // LANES):
        span = slice(block * LANES, (block + 1) * LANES)
        onehot = jnp.where(serve_ref[...] == rows + block * LANES, 1.0, 0.0).astype(BF16)
        grad = matmul(onehot, arrived)
        grad_ref[span, :] = grad
        square_ref[block : block + 1, :] = column_to_row(jnp.sum(grad * grad, axis=1, keepdims=True))


def update_kernel(columns, table_ref, grad_ref, accum_ref, mine_ref, other_ref, table_out, accum_out):
    accum = accum_ref[...] + (mine_ref[...] + other_ref[...]) / columns
    accum_out[...] = accum
    inverse = lax.rsqrt(accum)
    for block in range(accum.shape[0]):
        span = slice(block * LANES, (block + 1) * LANES)
        scale = row_to_column(inverse[block : block + 1, :])
        table_out[span, :] = table_ref[span, :] - LEARNING_RATE * grad_ref[span, :] * scale


def shift(array, axis, by):
    size = lax.axis_size(axis)
    return lax.ppermute(array, axis, [(i, (i + by) % size) for i in range(size)])


def body(
    table,
    accum,
    serve_rows,
    seed_slot,
    hop1_slot,
    hop2_slot,
    hop1_rel,
    hop2_rel,
    cotangent,
    w_first,
    w_second,
):
    everyone = ("dp", "y", "z")
    owners = lax.axis_size(everyone)
    table_rows, columns = table.shape
    slots = serve_rows.shape[1]
    seeds, fanout = hop1_slot.shape
    fanout_two = hop2_slot.shape[2]
    nodes = seeds + seeds * fanout
    layers, hidden_units = w_second.shape[:2]
    half = hidden_units // 2
    n_x, n_y, n_z = (lax.axis_size(a) for a in everyone)
    x, y = lax.axis_index("dp"), lax.axis_index("y")
    width = hidden_units // n_x

    outgoing = call(
        serve_kernel, [shaped((slots, columns), BF16)], (serve_rows, table), 2 * slots * table_rows * columns
    )[0]
    fetched = lax.all_to_all(
        outgoing.reshape(owners, slots // owners, columns), everyone, split_axis=0, concat_axis=0, tiled=True
    ).reshape(slots, columns)

    key_one = hop1_slot + slots * hop1_rel
    key_two = (hop2_slot + slots * hop2_rel).reshape(seeds * fanout, fanout_two)
    seed_ids = jnp.arange(seeds, dtype=jnp.int32)[:, None]
    group = (seeds * (1 + hop1_rel) + seed_ids).reshape(-1, 1)
    spare = jnp.full((seeds * fanout, fanout - fanout_two), -1, jnp.int32)
    idx = jnp.concatenate(
        [
            jnp.concatenate([seed_slot[:, None], key_one, seed_ids], 1),
            jnp.concatenate([hop1_slot.reshape(-1, 1), key_two, spare, group], 1),
        ],
        0,
    )
    ct, c, inverse, member_t, member, back_hidden = call(
        index_kernel,
        [
            shaped((layers * nodes, slots), BF16),
            shaped((slots, layers * nodes), BF16),
            shaped((layers * nodes, LANES), F32),
            shaped((nodes, LANES), BF16),
            shaped((SEED_ROWS, nodes), BF16),
            shaped((nodes, hidden_units), F32),
        ],
        (idx, cotangent, w_second),
        2 * layers * seeds * hidden_units * hidden_units,
        scratch=[pltpu.VMEM((LANES, hidden_units), F32)],
    )

    layer_in, partial_pre = call(
        first_kernel,
        [shaped((layers * nodes, columns), BF16), shaped((nodes, hidden_units), F32)],
        (fetched, ct, inverse, w_first),
        2 * layers * nodes * columns * (slots + hidden_units),
    )
    other_pre = shift(partial_pre, "col", 1)
    layer_parts = [layer_in] + [shift(layer_in, "dp", d) for d in range(1, n_x)]

    pack_rows = nodes + half // width * SEED_ROWS + COT_ROWS
    pack, slot_grad = call(
        hidden_kernel,
        [shaped((n_x, pack_rows, width), BF16), shaped((slots, columns), BF16)],
        (
            lax.axis_index("col").reshape(1),
            partial_pre,
            other_pre,
            back_hidden,
            member,
            inverse,
            c,
            w_first,
            cotangent,
        ),
        2 * layers * nodes * columns * (slots + hidden_units),
        smem=1,
    )
    pack = lax.all_to_all(pack, "dp", split_axis=0, concat_axis=0, tiled=True)
    arrived = lax.all_to_all(
        slot_grad.reshape(owners, slots // owners, columns), everyone, split_axis=0, concat_axis=0, tiled=True
    ).reshape(slots, columns)

    grad_columns = layers * (columns + half)
    place = jnp.stack([jnp.int32(0), y] + [lax.rem(x + n_x - d, n_x) for d in range(n_x)]).astype(jnp.int32)
    block_rows = width // n_y
    blocks = call(
        weight_kernel,
        [shaped((block_rows, grad_columns), F32 if d == 0 else BF16) for d in range(n_y)],
        (place, *layer_parts, pack),
        2 * n_x * nodes * width * grad_columns,
        smem=1,
        scratch=[pltpu.VMEM((width, grad_columns), F32)],
    )
    grads = blocks[0]
    for d in range(1, n_y):
        grads = grads + shift(blocks[d], "y", d).astype(F32)
    grads = grads.astype(BF16).reshape(n_z, block_rows // n_z, grad_columns)
    grads = lax.all_to_all(grads, "z", split_axis=0, concat_axis=0, tiled=True)
    grads = jnp.sum(grads.astype(F32), axis=0)
    grad_one = grads[:, : layers * columns].reshape(-1, layers, columns).transpose(1, 2, 0)
    grad_two = grads[:, layers * columns :].reshape(-1, layers, half).transpose(1, 2, 0)

    row_grad, squares = call(
        row_kernel,
        [shaped((table_rows, columns), F32), shaped((table_rows // LANES, LANES), F32)],
        (serve_rows, arrived),
        2 * slots * table_rows * columns,
    )
    other_squares = shift(squares, "col", 1)
    new_table, new_accum = call(
        functools.partial(update_kernel, 2 * columns),
        [shaped((table_rows, columns), F32), shaped((table_rows // LANES, LANES), F32)],
        (table, row_grad, accum.reshape(-1, LANES), squares, other_squares),
        3 * table_rows * columns,
    )
    return (new_table, new_accum.reshape(-1), grad_one, grad_two)


def solution(mesh):
    n_dp, n_table, n_col = (mesh.shape[a] for a in ("dp", "table", "col"))
    n_y = 4 if n_table % 4 == 0 and n_table > 4 else 2
    fine = Mesh(mesh.devices.reshape(n_dp, n_y, n_table // n_y, n_col), ("dp", "y", "z", "col"))
    rows = ("dp", "y", "z")
    placed = (
        P(rows, "col"),
        P(rows),
        P(rows, None),
        P(rows),
        P(rows, None),
        P(rows, None, None),
        P(rows, None),
        P(rows, None, None),
        P(rows, None),
        P(None, "col", None),
        P(),
    )
    return jax.shard_map(
        body,
        mesh=fine,
        in_specs=placed,
        out_specs=(P(rows, "col"), P(rows), P(None, "col", rows), P(None, "col", rows)),
        check_vma=False,
    )
```

```python
import functools
import jax
import jax.numpy as jnp
from jax import lax
from jax.experimental import pallas as pl
from jax.experimental.pallas import tpu as pltpu
from jax.sharding import Mesh
from jax.sharding import PartitionSpec as P

LEARNING_RATE = 0.1
BF16 = jnp.bfloat16
F32 = jnp.float32
LANES = 128
SEED_ROWS = 32
COT_ROWS = 16


def matmul(a, b, contract=(1, 0)):
    dims = (((contract[0],), (contract[1],)), ((), ()))
    return lax.dot_general(a, b, dims, preferred_element_type=F32)


def row_to_column(row):
    return jnp.transpose(jnp.broadcast_to(row, (LANES, LANES)))[:, 0:1]


def column_to_row(column):
    return jnp.transpose(jnp.broadcast_to(column, (LANES, LANES)))[0:1, :]


class Incoming:
    def __init__(self, source, buffer, semaphore):
        self.buffer, self.waiting = buffer, True
        self.shape = buffer.shape
        self.copy = pltpu.make_async_copy(source, buffer, semaphore)
        self.copy.start()

    def get(self):
        if self.waiting:
            self.copy.wait()
        self.waiting = False
        return self.buffer


class Outgoing:
    def __init__(self, target, buffer, semaphore):
        self.buffer = buffer
        self.copy = pltpu.make_async_copy(buffer, target, semaphore)

    def send(self):
        self.copy.start()


def call(kernel, outs, operands, flops, smem=0, scratch=(), hbm_in=(), hbm_out=(), hbm_raw=()):
    limit = LIMITS.get(getattr(kernel, "func", kernel), 12)
    moved = sum(o.size * o.dtype.itemsize for o in list(operands) + list(outs))
    specs = [
        pl.BlockSpec(memory_space=pltpu.SMEM if i < smem else pltpu.HBM if i in hbm_in else pltpu.VMEM)
        for i in range(len(operands))
    ]
    made = [
        pl.BlockSpec(memory_space=pltpu.HBM if i in hbm_out or i in hbm_raw else pltpu.VMEM)
        for i in range(len(outs))
    ]
    buffers = [pltpu.VMEM(operands[i].shape, operands[i].dtype) for i in hbm_in]
    buffers += [pltpu.VMEM(outs[i].shape, outs[i].dtype) for i in hbm_out]
    semaphores = [pltpu.SemaphoreType.DMA((len(buffers),))] if buffers else []

    def wrapped(*refs):
        refs = list(refs)
        if not buffers:
            kernel(*refs)
            return
        first = len(operands) + len(outs)
        held, sems = refs[first : first + len(buffers)], refs[first + len(buffers)]
        rest = refs[first + len(buffers) + 1 :]
        for j, i in enumerate(hbm_in):
            refs[i] = Incoming(refs[i], held[j], sems.at[j])
        leaving = []
        for j, i in enumerate(hbm_out, len(hbm_in)):
            place = len(operands) + i
            refs[place] = Outgoing(refs[place], held[j], sems.at[j])
            leaving.append(refs[place])
        kernel(*refs[:first], *rest)
        for out in leaving:
            out.copy.wait()

    return pl.pallas_call(
        wrapped,
        out_shape=tuple(outs),
        in_specs=specs,
        out_specs=tuple(made),
        scratch_shapes=buffers + semaphores + list(scratch),
        compiler_params=pltpu.CompilerParams(vmem_limit_bytes=limit * 1024 * 1024),
        cost_estimate=pl.CostEstimate(flops=flops, bytes_accessed=moved, transcendentals=0),
    )(*operands)


def shaped(shape, dtype):
    return jax.ShapeDtypeStruct(shape, dtype)


def serve_kernel(serve_ref, table_ref, out_ref):
    serve_ref = serve_ref.get()
    rows = table_ref.get()[...].astype(BF16)
    lanes = lax.broadcasted_iota(jnp.int32, (LANES, rows.shape[0]), 1)
    owners = LANES // out_ref.shape[1]
    for block in range(serve_ref.shape[1] // LANES):
        wanted = row_to_column(serve_ref[:, block * LANES : (block + 1) * LANES])
        onehot = jnp.where(wanted == lanes, 1.0, 0.0).astype(BF16)
        picked = matmul(onehot, rows).astype(BF16)
        out_ref[block * owners : (block + 1) * owners] = picked.reshape(owners, *out_ref.shape[1:])


def index_kernel(idx_ref, cot_ref, w2_ref, *refs):
    outs, spread = refs[:-1], refs[-1]
    ct_ref, c_ref, inv_ref, e_ref, back_ref = (o.buffer for o in outs)
    nodes = idx_ref.shape[0]
    slots = ct_ref.shape[1]
    seeds = cot_ref.shape[0]
    neighbours = idx_ref.shape[1] - 2
    lanes = lax.broadcasted_iota(jnp.int32, (nodes, 2 * slots), 1)
    idx = idx_ref[...]
    counts = jnp.zeros((nodes, 2 * slots), F32)
    for j in range(1, 1 + neighbours):
        counts = counts + jnp.where(idx[:, j : j + 1] == lanes, 1.0, 0.0)
    own = jnp.where(idx[:, 0:1] == lanes[:, :slots], 1.0, 0.0)
    parts = (own, counts[:, :slots], counts[:, slots:])
    spread[...] = jnp.zeros(spread.shape, F32)
    for k, part in enumerate(parts):
        span = slice(k * nodes, (k + 1) * nodes)
        ct_ref[span, :] = part.astype(BF16)
        c_ref[:, span] = jnp.transpose(part).astype(BF16)
        if k == 0:
            inverse = jnp.ones((nodes, 1), F32)
        else:
            inverse = 1.0 / jnp.maximum(jnp.sum(part, axis=1, keepdims=True), 1.0)
        inv_ref[span, :] = jnp.broadcast_to(inverse, (nodes, LANES))
        back = matmul(cot_ref[...], w2_ref[k], (1, 1))
        spread[k * seeds : (k + 1) * seeds, :] = back * inverse[:seeds]
    groups = lax.broadcasted_iota(jnp.int32, (nodes, LANES), 1)
    member = jnp.where(idx[:, neighbours + 1 : neighbours + 2] == groups, 1.0, 0.0)
    e_ref[...] = jnp.transpose(member)[:SEED_ROWS].astype(BF16)
    whole = spread[...]
    high = whole.astype(BF16)
    low = (whole - high.astype(F32)).astype(BF16)
    for out in outs[:-1]:
        out.send()
    back_ref[...] = matmul(member.astype(BF16), high) + matmul(member.astype(BF16), low)
    outs[-1].send()


def first_kernel(fetched_ref, ct_ref, w1_ref, layer_ref, partial_ref):
    layers = w1_ref.shape[0]
    layer_out, partial_out = layer_ref, partial_ref
    layer_ref, partial_ref = layer_ref.buffer, partial_ref.buffer
    nodes = partial_ref.shape[0]
    fetched = fetched_ref[...].reshape(ct_ref.shape[1], layer_ref.shape[1])
    total = None
    ct_ref = ct_ref.get()
    ones = jnp.ones((ct_ref.shape[1], LANES), BF16)
    for k in range(layers):
        span = slice(k * nodes, (k + 1) * nodes)
        summed = matmul(ct_ref[span, :], fetched)
        inverse = 1.0 / jnp.maximum(matmul(ct_ref[span, :], ones)[:, 0:1], 1.0)
        layer_ref[span, :] = (summed * inverse).astype(BF16)
    layer_out.send()
    for k in range(layers):
        term = matmul(layer_ref[k * nodes : (k + 1) * nodes, :], w1_ref[k])
        total = term if total is None else total + term
    partial_ref[...] = total
    partial_out.send()


def hidden_kernel(place_ref, mine_ref, other_ref, back_ref, e_ref, inv_ref, cot_ref, c_ref, w1_ref, slot_ref, *refs):
    packs, stage, sems = refs[:-2], refs[-2], refs[-1]
    nodes = mine_ref.shape[0]
    width = stage.shape[2]
    seeds = cot_ref.shape[0]
    layers = inv_ref.shape[0] // nodes
    values = mine_ref.get()[...] + other_ref.get()[...]
    back_ref, e_ref, inv_ref = back_ref.get(), e_ref.get(), inv_ref.get()
    sigma = jax.nn.sigmoid(values)
    hidden = (values * sigma).astype(BF16)
    slope = sigma * (1.0 + values * (1.0 - sigma))
    back = (back_ref[...] * slope).astype(BF16)
    scale = jnp.concatenate(
        [inv_ref[k * nodes : k * nodes + seeds, 0:1] for k in range(layers)]
        + [jnp.zeros((SEED_ROWS - layers * seeds, 1), F32)],
        0,
    )
    second = matmul(e_ref[...], hidden) * scale
    half = second.shape[1] // 2
    second = jnp.where(place_ref[0] == 0, second[:, :half], second[:, half:]).astype(BF16)
    cot = cot_ref[...].astype(F32)
    cot = jnp.concatenate([cot, jnp.zeros((COT_ROWS - seeds, cot.shape[1]), F32)], 0).astype(BF16)
    for j in range(len(packs)):
        span = slice(j * width, (j + 1) * width)
        stage[j, :nodes, :] = back[:, span]
        for part in range(half // width):
            first = nodes + part * SEED_ROWS
            stage[j, first : first + SEED_ROWS, :] = second[:, part * width : (part + 1) * width]
        first = nodes + half // width * SEED_ROWS
        stage[j, first : first + COT_ROWS, :] = cot[:, span]
    copies = [
        pltpu.make_async_copy(stage.at[lax.rem(place_ref[1] + d, len(packs))], pack, sems.at[d])
        for d, pack in enumerate(packs)
    ]
    for copy in copies:
        copy.start()
    total = None
    for k in range(layers):
        span = slice(k * nodes, (k + 1) * nodes)
        back_in = matmul(back, w1_ref[k], (1, 1)) * inv_ref[span, 0:1]
        term = matmul(c_ref.get()[:, span], back_in.astype(BF16))
        total = term if total is None else total + term
    slot_ref[...] = total.astype(BF16).reshape(slot_ref.shape)
    for copy in copies:
        copy.wait()


def weight_kernel(place_ref, *refs):
    count = refs[0].shape[0]
    layer_refs = [refs[0].get().at[lax.rem(place_ref[1] + count - d, count)] for d in range(count)]
    pack_refs = (refs[1].get(), *refs[2 : 1 + count])
    own_ref, outs = refs[1 + count], refs[2 + count : -1]
    total = refs[-1]
    width = pack_refs[0].shape[1]
    columns = layer_refs[0].shape[1]
    nodes = LANES
    relations = layer_refs[0].shape[0] // nodes
    rows = own_ref.shape[0]
    left = jnp.concatenate([p[:nodes, :] for p in pack_refs], 0)
    for k in range(relations):
        right = jnp.concatenate([r[k * nodes : (k + 1) * nodes, :] for r in layer_refs], 0)
        total[k] = matmul(left, right, (0, 0))
    pieces = (pack_refs[0].shape[0] - nodes - COT_ROWS) // SEED_ROWS
    half = pieces * width
    seeds = SEED_ROWS // (relations + 1)
    first = nodes + pieces * SEED_ROWS
    cots = jnp.concatenate([p[first : first + COT_ROWS, :].astype(F32)[:seeds] for p in pack_refs], 0)
    seconds = [
        jnp.concatenate(
            [p[nodes + part * SEED_ROWS : nodes + (part + 1) * SEED_ROWS, :].astype(F32) for part in range(pieces)],
            1,
        )
        for p in pack_refs
    ]
    second = jnp.concatenate(
        [jnp.concatenate([s[k * seeds : (k + 1) * seeds] for s in seconds], 0) for k in range(relations)], 1
    ).astype(BF16)
    group = count * seeds
    tail = relations * rows
    for d, out in enumerate(outs):
        target = lax.rem(place_ref[0] + d, len(outs))
        start = pl.multiple_of(target * rows, rows)
        for k in range(relations):
            block = total[k, pl.ds(start, rows), :]
            if d == 0:
                own_ref[:, k * columns : (k + 1) * columns] = block
            else:
                out[k * rows : (k + 1) * rows, :] = block.astype(BF16)
        for piece in range(relations * half // columns):
            out[tail + piece * group : tail + (piece + 1) * group, :] = second[
                :, piece * columns : (piece + 1) * columns
            ]
        chosen = cots[:, :rows]
        for j in range(1, len(outs)):
            chosen = jnp.where(target == j, cots[:, j * rows : (j + 1) * rows], chosen)
        chosen = jnp.concatenate([chosen, jnp.zeros((group, columns - rows), F32)], 1)
        out[out.shape[0] - group :, :] = chosen.astype(BF16)


def group_kernel(relations, own_ref, *refs):
    packs, out_ref = refs[:-1], refs[-1]
    rows = own_ref.shape[0]
    columns = packs[0].shape[1]
    tail = relations * rows
    wide = out_ref.shape[1] - relations * columns
    pieces = wide // columns
    group = (packs[0].shape[0] - tail) // (pieces + 1)
    for k in range(relations):
        span = slice(k * columns, (k + 1) * columns)
        block = own_ref[:, span]
        for pack in packs[1:]:
            block = block + pack[k * rows : (k + 1) * rows, :].astype(F32)
        out_ref[:, span] = block.astype(BF16)
    cots = jnp.concatenate([p[tail + pieces * group :, :] for p in packs], 0)
    for piece in range(pieces):
        first = tail + piece * group
        second = jnp.concatenate([p[first : first + group, :] for p in packs], 0)
        start = (relations + piece) * columns
        out_ref[:, start : start + columns] = matmul(cots, second, (0, 0))[:rows].astype(BF16)


def sum_kernel(parts_ref, one_ref, two_ref):
    total = jnp.sum(parts_ref[...].astype(F32), axis=0)
    start = 0
    for ref in (one_ref, two_ref):
        wide = ref.shape[2]
        for k in range(ref.shape[0]):
            ref[k] = total[:, start : start + wide]
            start += wide


def row_kernel(serve_ref, arrived_ref, grad_ref, square_ref):
    rows = lax.broadcasted_iota(jnp.int32, (LANES, serve_ref.shape[1]), 0)
    arrived = arrived_ref[...].reshape(serve_ref.shape[1], grad_ref.shape[1])
    for block in range(grad_ref.shape[0] // LANES):
        span = slice(block * LANES, (block + 1) * LANES)
        onehot = jnp.where(serve_ref[...] == rows + block * LANES, 1.0, 0.0).astype(BF16)
        grad = matmul(onehot, arrived)
        grad_ref[span, :] = grad
        square_ref[block : block + 1, :] = column_to_row(jnp.sum(grad * grad, axis=1, keepdims=True))


def update_kernel(columns, table_ref, grad_ref, accum_ref, mine_ref, other_ref, table_out, accum_out):
    accum = accum_ref[...] + (mine_ref[...] + other_ref[...]) / columns
    accum_out[...] = accum
    inverse = lax.rsqrt(accum)
    for block in range(accum.shape[0]):
        span = slice(block * LANES, (block + 1) * LANES)
        scale = row_to_column(inverse[block : block + 1, :])
        table_out[span, :] = table_ref[span, :] - LEARNING_RATE * grad_ref[span, :] * scale


def shift(array, axis, by):
    size = lax.axis_size(axis)
    return lax.ppermute(array, axis, [(i, (i + by) % size) for i in range(size)])


LIMITS = {serve_kernel: 60, index_kernel: 60, first_kernel: 50, hidden_kernel: 50}


def body(
    table,
    accum,
    serve_rows,
    seed_slot,
    hop1_slot,
    hop2_slot,
    hop1_rel,
    hop2_rel,
    cotangent,
    w_first,
    w_second,
):
    everyone = ("dp", "y", "z")
    owners = lax.axis_size(everyone)
    table_rows, columns = table.shape
    slots = serve_rows.shape[1]
    seeds, fanout = hop1_slot.shape
    fanout_two = hop2_slot.shape[2]
    nodes = seeds + seeds * fanout
    layers, hidden_units = w_second.shape[:2]
    half = hidden_units // 2
    n_x, n_y, n_z = (lax.axis_size(a) for a in everyone)
    x, y = lax.axis_index("dp"), lax.axis_index("y")
    width = hidden_units // n_x

    blocks_shape = (owners, slots // owners, columns)
    outgoing = call(
        serve_kernel, [shaped(blocks_shape, BF16)], (serve_rows, table), 2 * slots * table_rows * columns, hbm_in=(0, 1)
    )[0]
    fetched = lax.all_to_all(outgoing, everyone, split_axis=0, concat_axis=0, tiled=True)

    key_one = hop1_slot + slots * hop1_rel
    key_two = (hop2_slot + slots * hop2_rel).reshape(seeds * fanout, fanout_two)
    seed_ids = jnp.arange(seeds, dtype=jnp.int32)[:, None]
    group = (seeds * (1 + hop1_rel) + seed_ids).reshape(-1, 1)
    spare = jnp.full((seeds * fanout, fanout - fanout_two), -1, jnp.int32)
    idx = jnp.concatenate(
        [
            jnp.concatenate([seed_slot[:, None], key_one, seed_ids], 1),
            jnp.concatenate([hop1_slot.reshape(-1, 1), key_two, spare, group], 1),
        ],
        0,
    )
    ct, c, inverse, member, back_hidden = call(
        index_kernel,
        [
            shaped((layers * nodes, slots), BF16),
            shaped((slots, layers * nodes), BF16),
            shaped((layers * nodes, LANES), F32),
            shaped((SEED_ROWS, nodes), BF16),
            shaped((nodes, hidden_units), F32),
        ],
        (idx, cotangent, w_second),
        2 * layers * seeds * hidden_units * hidden_units,
        scratch=[pltpu.VMEM((LANES, hidden_units), F32)],
        hbm_out=range(5),
    )

    layer_in, partial_pre = call(
        first_kernel,
        [shaped((layers * nodes, columns), BF16), shaped((nodes, hidden_units), F32)],
        (fetched, ct, w_first),
        2 * layers * nodes * columns * (slots + hidden_units),
        hbm_in=(1,),
        hbm_out=(0, 1),
    )
    other_pre = shift(partial_pre, "col", 1)
    layer_parts = lax.all_gather(layer_in, "dp")

    pack_rows = nodes + half // width * SEED_ROWS + COT_ROWS
    pack_shape = (pack_rows, width)
    slot_grad, *packs = call(
        hidden_kernel,
        [shaped(blocks_shape, BF16)] + [shaped(pack_shape, BF16)] * n_x,
        (
            jnp.stack([lax.axis_index("col"), x]),
            partial_pre,
            other_pre,
            back_hidden,
            member,
            inverse,
            cotangent,
            c,
            w_first,
        ),
        2 * layers * nodes * columns * (slots + hidden_units),
        smem=1,
        scratch=[pltpu.VMEM((n_x, *pack_shape), BF16), pltpu.SemaphoreType.DMA((n_x,))],
        hbm_in=(1, 2, 3, 4, 5, 7),
        hbm_raw=range(1, 1 + n_x),
    )
    packs = [packs[0]] + [shift(packs[d], "dp", d) for d in range(1, n_x)]
    arrived = lax.all_to_all(slot_grad, everyone, split_axis=0, concat_axis=0, tiled=True)

    block_rows = width // n_y
    group_rows = layers * block_rows + (layers * half // columns + 1) * n_x * seeds
    own, *blocks = call(
        weight_kernel,
        [shaped((block_rows, layers * columns), F32)] + [shaped((group_rows, columns), BF16)] * n_y,
        (jnp.stack([y, x]), layer_parts, *packs),
        2 * n_x * nodes * width * layers * columns,
        smem=1,
        scratch=[pltpu.VMEM((layers, width, columns), F32)],
        hbm_in=(1, 2),
    )
    blocks = [blocks[0]] + [shift(blocks[d], "y", d) for d in range(1, n_y)]
    grad_columns = layers * (columns + half)
    grads = call(
        functools.partial(group_kernel, layers),
        [shaped((block_rows, grad_columns), BF16)],
        (own, *blocks),
        2 * n_x * n_y * seeds * block_rows * layers * half,
    )[0]
    grads = grads.reshape(n_z, block_rows // n_z, grad_columns)
    grads = lax.all_to_all(grads, "z", split_axis=0, concat_axis=0, tiled=True)
    grad_one, grad_two = call(
        sum_kernel,
        [shaped((layers, block_rows // n_z, wide), F32) for wide in (columns, half)],
        (grads,),
        block_rows * grad_columns,
    )
    grad_one, grad_two = grad_one.transpose(0, 2, 1), grad_two.transpose(0, 2, 1)

    row_grad, squares = call(
        row_kernel,
        [shaped((table_rows, columns), F32), shaped((table_rows // LANES, LANES), F32)],
        (serve_rows, arrived),
        2 * slots * table_rows * columns,
    )
    other_squares = shift(squares, "col", 1)
    new_table, new_accum = call(
        functools.partial(update_kernel, 2 * columns),
        [shaped((table_rows, columns), F32), shaped((table_rows // LANES, LANES), F32)],
        (table, row_grad, accum.reshape(-1, LANES), squares, other_squares),
        3 * table_rows * columns,
    )
    return (new_table, new_accum.reshape(-1), grad_one, grad_two)


def solution(mesh):
    n_dp, n_table, n_col = (mesh.shape[a] for a in ("dp", "table", "col"))
    n_y = 4 if n_table % 4 == 0 and n_table > 4 else 2
    fine = Mesh(mesh.devices.reshape(n_dp, n_y, n_table // n_y, n_col), ("dp", "y", "z", "col"))
    rows = ("dp", "y", "z")
    placed = (
        P(rows, "col"),
        P(rows),
        P(rows, None),
        P(rows),
        P(rows, None),
        P(rows, None, None),
        P(rows, None),
        P(rows, None, None),
        P(rows, None),
        P(None, "col", None),
        P(),
    )
    return jax.shard_map(
        body,
        mesh=fine,
        in_specs=placed,
        out_specs=(P(rows, "col"), P(rows), P(None, "col", rows), P(None, "col", rows)),
        check_vma=False,
    )
```

```python
import functools
import jax
import jax.numpy as jnp
from jax import lax
from jax.experimental import pallas as pl
from jax.experimental.pallas import tpu as pltpu
from jax.sharding import Mesh
from jax.sharding import PartitionSpec as P

LEARNING_RATE = 0.1
BF16 = jnp.bfloat16
F32 = jnp.float32
LANES = 128
SEED_ROWS = 32
COT_ROWS = 16


def matmul(a, b, contract=(1, 0)):
    dims = (((contract[0],), (contract[1],)), ((), ()))
    return lax.dot_general(a, b, dims, preferred_element_type=F32)


def row_to_column(row):
    return jnp.transpose(jnp.broadcast_to(row, (LANES, LANES)))[:, 0:1]


def column_to_row(column):
    return jnp.transpose(jnp.broadcast_to(column, (LANES, LANES)))[0:1, :]


class Incoming:
    def __init__(self, source, buffer, semaphore):
        self.buffer, self.waiting = buffer, True
        self.shape = buffer.shape
        self.copy = pltpu.make_async_copy(source, buffer, semaphore)
        self.copy.start()

    def get(self):
        if self.waiting:
            self.copy.wait()
        self.waiting = False
        return self.buffer


class Outgoing:
    def __init__(self, target, buffer, semaphore):
        self.buffer = buffer
        self.copy = pltpu.make_async_copy(buffer, target, semaphore)

    def send(self):
        self.copy.start()


def call(kernel, outs, operands, flops, smem=0, scratch=(), hbm_in=(), hbm_out=(), hbm_raw=()):
    name = getattr(kernel, "func", kernel)
    limit, flops = LIMITS.get(name, 12), FLOPS.get(name, 10**12)
    moved = sum(o.size * o.dtype.itemsize for o in list(operands) + list(outs))
    specs = [
        pl.BlockSpec(memory_space=pltpu.SMEM if i < smem else pltpu.HBM if i in hbm_in else pltpu.VMEM)
        for i in range(len(operands))
    ]
    made = [
        pl.BlockSpec(memory_space=pltpu.HBM if i in hbm_out or i in hbm_raw else pltpu.VMEM)
        for i in range(len(outs))
    ]
    buffers = [pltpu.VMEM(operands[i].shape, operands[i].dtype) for i in hbm_in]
    buffers += [pltpu.VMEM(outs[i].shape, outs[i].dtype) for i in hbm_out]
    semaphores = [pltpu.SemaphoreType.DMA((len(buffers),))] if buffers else []

    def wrapped(*refs):
        refs = list(refs)
        if not buffers:
            kernel(*refs)
            return
        first = len(operands) + len(outs)
        held, sems = refs[first : first + len(buffers)], refs[first + len(buffers)]
        rest = refs[first + len(buffers) + 1 :]
        for j, i in enumerate(hbm_in):
            refs[i] = Incoming(refs[i], held[j], sems.at[j])
        leaving = []
        for j, i in enumerate(hbm_out, len(hbm_in)):
            place = len(operands) + i
            refs[place] = Outgoing(refs[place], held[j], sems.at[j])
            leaving.append(refs[place])
        kernel(*refs[:first], *rest)
        for out in leaving:
            out.copy.wait()

    return pl.pallas_call(
        wrapped,
        out_shape=tuple(outs),
        in_specs=specs,
        out_specs=tuple(made),
        scratch_shapes=buffers + semaphores + list(scratch),
        compiler_params=pltpu.CompilerParams(vmem_limit_bytes=limit * 1024 * 1024),
        cost_estimate=pl.CostEstimate(flops=flops, bytes_accessed=moved, transcendentals=0),
    )(*operands)


def shaped(shape, dtype):
    return jax.ShapeDtypeStruct(shape, dtype)


def serve_kernel(serve_ref, table_ref, out_ref):
    serve_ref = serve_ref.get()
    rows = table_ref.get()[...].astype(BF16)
    lanes = lax.broadcasted_iota(jnp.int32, (LANES, rows.shape[0]), 1)
    owners = LANES // out_ref.shape[1]
    for block in range(serve_ref.shape[1] // LANES):
        wanted = row_to_column(serve_ref[:, block * LANES : (block + 1) * LANES])
        onehot = jnp.where(wanted == lanes, 1.0, 0.0).astype(BF16)
        picked = matmul(onehot, rows).astype(BF16)
        out_ref[block * owners : (block + 1) * owners] = picked.reshape(owners, *out_ref.shape[1:])


def index_kernel(idx_ref, cot_ref, w2_ref, *refs):
    outs, spread = refs[:-1], refs[-1]
    ct_ref, c_ref, inv_ref, e_ref, back_ref = (o.buffer for o in outs)
    nodes = idx_ref.shape[0]
    slots = ct_ref.shape[1]
    seeds = cot_ref.shape[0]
    neighbours = idx_ref.shape[1] - 2
    lanes = lax.broadcasted_iota(jnp.int32, (nodes, 2 * slots), 1)
    idx = idx_ref[...]
    counts = jnp.zeros((nodes, 2 * slots), F32)
    for j in range(1, 1 + neighbours):
        counts = counts + jnp.where(idx[:, j : j + 1] == lanes, 1.0, 0.0)
    own = jnp.where(idx[:, 0:1] == lanes[:, :slots], 1.0, 0.0)
    parts = (own, counts[:, :slots], counts[:, slots:])
    spread[...] = jnp.zeros(spread.shape, F32)
    for k, part in enumerate(parts):
        span = slice(k * nodes, (k + 1) * nodes)
        ct_ref[span, :] = part.astype(BF16)
        c_ref[:, span] = jnp.transpose(part).astype(BF16)
        if k == 0:
            inverse = jnp.ones((nodes, 1), F32)
        else:
            inverse = 1.0 / jnp.maximum(jnp.sum(part, axis=1, keepdims=True), 1.0)
        inv_ref[span, :] = jnp.broadcast_to(inverse, (nodes, LANES))
        back = matmul(cot_ref[...], w2_ref[k], (1, 1))
        spread[k * seeds : (k + 1) * seeds, :] = back * inverse[:seeds]
    groups = lax.broadcasted_iota(jnp.int32, (nodes, LANES), 1)
    member = jnp.where(idx[:, neighbours + 1 : neighbours + 2] == groups, 1.0, 0.0)
    e_ref[...] = jnp.transpose(member)[:SEED_ROWS].astype(BF16)
    whole = spread[...]
    high = whole.astype(BF16)
    low = (whole - high.astype(F32)).astype(BF16)
    for out in outs[:-1]:
        out.send()
    back_ref[...] = matmul(member.astype(BF16), high) + matmul(member.astype(BF16), low)
    outs[-1].send()


def first_kernel(fetched_ref, ct_ref, w1_ref, layer_ref, partial_ref):
    layers = w1_ref.shape[0]
    layer_out, partial_out = layer_ref, partial_ref
    layer_ref, partial_ref = layer_ref.buffer, partial_ref.buffer
    nodes = partial_ref.shape[0]
    fetched = fetched_ref[...].reshape(ct_ref.shape[1], layer_ref.shape[1])
    total = None
    ct_ref = ct_ref.get()
    ones = jnp.ones((ct_ref.shape[1], LANES), BF16)
    for k in range(layers):
        span = slice(k * nodes, (k + 1) * nodes)
        summed = matmul(ct_ref[span, :], fetched)
        inverse = 1.0 / jnp.maximum(matmul(ct_ref[span, :], ones)[:, 0:1], 1.0)
        layer_ref[span, :] = (summed * inverse).astype(BF16)
    layer_out.send()
    for k in range(layers):
        term = matmul(layer_ref[k * nodes : (k + 1) * nodes, :], w1_ref[k])
        total = term if total is None else total + term
    partial_ref[...] = total
    partial_out.send()


def hidden_kernel(place_ref, mine_ref, other_ref, back_ref, e_ref, inv_ref, cot_ref, c_ref, w1_ref, slot_ref, *refs):
    packs, stage, sems = refs[:-2], refs[-2], refs[-1]
    nodes = mine_ref.shape[0]
    width = stage.shape[2]
    seeds = cot_ref.shape[0]
    layers = inv_ref.shape[0] // nodes
    values = mine_ref.get()[...] + other_ref.get()[...]
    back_ref, e_ref, inv_ref = back_ref.get(), e_ref.get(), inv_ref.get()
    sigma = jax.nn.sigmoid(values)
    hidden = (values * sigma).astype(BF16)
    slope = sigma * (1.0 + values * (1.0 - sigma))
    back = (back_ref[...] * slope).astype(BF16)
    scale = jnp.concatenate(
        [inv_ref[k * nodes : k * nodes + seeds, 0:1] for k in range(layers)]
        + [jnp.zeros((SEED_ROWS - layers * seeds, 1), F32)],
        0,
    )
    second = matmul(e_ref[...], hidden) * scale
    half = second.shape[1] // 2
    second = jnp.where(place_ref[0] == 0, second[:, :half], second[:, half:]).astype(BF16)
    cot = cot_ref[...].astype(F32)
    cot = jnp.concatenate([cot, jnp.zeros((COT_ROWS - seeds, cot.shape[1]), F32)], 0).astype(BF16)
    for j in range(len(packs)):
        span = slice(j * width, (j + 1) * width)
        stage[j, :nodes, :] = back[:, span]
        for part in range(half // width):
            first = nodes + part * SEED_ROWS
            stage[j, first : first + SEED_ROWS, :] = second[:, part * width : (part + 1) * width]
        first = nodes + half // width * SEED_ROWS
        stage[j, first : first + COT_ROWS, :] = cot[:, span]
    copies = [
        pltpu.make_async_copy(stage.at[lax.rem(place_ref[1] + d, len(packs))], pack, sems.at[d])
        for d, pack in enumerate(packs)
    ]
    for copy in copies:
        copy.start()
    total = None
    for k in range(layers):
        span = slice(k * nodes, (k + 1) * nodes)
        back_in = matmul(back, w1_ref[k], (1, 1)) * inv_ref[span, 0:1]
        term = matmul(c_ref.get()[:, span], back_in.astype(BF16))
        total = term if total is None else total + term
    slot_ref[...] = total.astype(BF16).reshape(slot_ref.shape)
    for copy in copies:
        copy.wait()


def weight_kernel(count, place_ref, *refs):
    layer_refs, pack_refs = refs[:count], refs[count : 2 * count]
    own_ref, outs = refs[2 * count], refs[2 * count + 1 : -1]
    total = refs[-1]
    width = pack_refs[0].shape[1]
    columns = layer_refs[0].shape[1]
    nodes = LANES
    relations = layer_refs[0].shape[0] // nodes
    rows = own_ref.shape[0]
    left = jnp.concatenate([p[:nodes, :] for p in pack_refs], 0)
    for k in range(relations):
        right = jnp.concatenate([r[k * nodes : (k + 1) * nodes, :] for r in layer_refs], 0)
        total[k] = matmul(left, right, (0, 0))
    pieces = (pack_refs[0].shape[0] - nodes - COT_ROWS) // SEED_ROWS
    half = pieces * width
    seeds = SEED_ROWS // (relations + 1)
    first = nodes + pieces * SEED_ROWS
    cots = jnp.concatenate([p[first : first + COT_ROWS, :].astype(F32)[:seeds] for p in pack_refs], 0)
    seconds = [
        jnp.concatenate(
            [p[nodes + part * SEED_ROWS : nodes + (part + 1) * SEED_ROWS, :].astype(F32) for part in range(pieces)],
            1,
        )
        for p in pack_refs
    ]
    second = jnp.concatenate(
        [jnp.concatenate([s[k * seeds : (k + 1) * seeds] for s in seconds], 0) for k in range(relations)], 1
    ).astype(BF16)
    group = count * seeds
    tail = relations * rows
    for d, out in enumerate(outs):
        target = lax.rem(place_ref[0] + d, len(outs))
        start = pl.multiple_of(target * rows, rows)
        for k in range(relations):
            block = total[k, pl.ds(start, rows), :]
            if d == 0:
                own_ref[:, k * columns : (k + 1) * columns] = block
            else:
                out[k * rows : (k + 1) * rows, :] = block.astype(BF16)
        for piece in range(relations * half // columns):
            out[tail + piece * group : tail + (piece + 1) * group, :] = second[
                :, piece * columns : (piece + 1) * columns
            ]
        chosen = cots[:, :rows]
        for j in range(1, len(outs)):
            chosen = jnp.where(target == j, cots[:, j * rows : (j + 1) * rows], chosen)
        chosen = jnp.concatenate([chosen, jnp.zeros((group, columns - rows), F32)], 1)
        out[out.shape[0] - group :, :] = chosen.astype(BF16)


def group_kernel(relations, own_ref, *refs):
    packs, out_ref = refs[:-1], refs[-1]
    rows = own_ref.shape[0]
    columns = packs[0].shape[1]
    tail = relations * rows
    wide = out_ref.shape[1] - relations * columns
    pieces = wide // columns
    group = (packs[0].shape[0] - tail) // (pieces + 1)
    for k in range(relations):
        span = slice(k * columns, (k + 1) * columns)
        block = own_ref[:, span]
        for pack in packs[1:]:
            block = block + pack[k * rows : (k + 1) * rows, :].astype(F32)
        out_ref[:, span] = block.astype(BF16)
    cots = jnp.concatenate([p[tail + pieces * group :, :] for p in packs], 0)
    for piece in range(pieces):
        first = tail + piece * group
        second = jnp.concatenate([p[first : first + group, :] for p in packs], 0)
        start = (relations + piece) * columns
        out_ref[:, start : start + columns] = matmul(cots, second, (0, 0))[:rows].astype(BF16)


def sum_kernel(parts_ref, one_ref, two_ref):
    total = jnp.sum(parts_ref[...].astype(F32), axis=0)
    start = 0
    for ref in (one_ref, two_ref):
        wide = ref.shape[2]
        for k in range(ref.shape[0]):
            ref[k] = total[:, start : start + wide]
            start += wide


def row_kernel(serve_ref, arrived_ref, grad_ref, square_ref):
    rows = lax.broadcasted_iota(jnp.int32, (LANES, serve_ref.shape[1]), 0)
    arrived = arrived_ref[...].reshape(serve_ref.shape[1], grad_ref.shape[1])
    for block in range(grad_ref.shape[0] // LANES):
        span = slice(block * LANES, (block + 1) * LANES)
        onehot = jnp.where(serve_ref[...] == rows + block * LANES, 1.0, 0.0).astype(BF16)
        grad = matmul(onehot, arrived)
        grad_ref[span, :] = grad
        square_ref[block : block + 1, :] = column_to_row(jnp.sum(grad * grad, axis=1, keepdims=True))


def update_kernel(columns, table_ref, grad_ref, accum_ref, mine_ref, other_ref, table_out, accum_out):
    accum = accum_ref[...] + (mine_ref[...] + other_ref[...]) / columns
    accum_out[...] = accum
    inverse = lax.rsqrt(accum)
    for block in range(accum.shape[0]):
        span = slice(block * LANES, (block + 1) * LANES)
        scale = row_to_column(inverse[block : block + 1, :])
        table_out[span, :] = table_ref[span, :] - LEARNING_RATE * grad_ref[span, :] * scale


def shift(array, axis, by):
    size = lax.axis_size(axis)
    return lax.ppermute(array, axis, [(i, (i + by) % size) for i in range(size)])


LIMITS = {serve_kernel: 60, index_kernel: 60, first_kernel: 60, hidden_kernel: 50}
FLOPS = {}


def body(
    table,
    accum,
    serve_rows,
    seed_slot,
    hop1_slot,
    hop2_slot,
    hop1_rel,
    hop2_rel,
    cotangent,
    w_first,
    w_second,
):
    everyone = ("dp", "y", "z")
    owners = lax.axis_size(everyone)
    table_rows, columns = table.shape
    slots = serve_rows.shape[1]
    seeds, fanout = hop1_slot.shape
    fanout_two = hop2_slot.shape[2]
    nodes = seeds + seeds * fanout
    layers, hidden_units = w_second.shape[:2]
    half = hidden_units // 2
    n_x, n_y, n_z = (lax.axis_size(a) for a in everyone)
    x, y = lax.axis_index("dp"), lax.axis_index("y")
    width = hidden_units // n_x

    blocks_shape = (owners, slots // owners, columns)
    outgoing = call(
        serve_kernel, [shaped(blocks_shape, BF16)], (serve_rows, table), 2 * slots * table_rows * columns, hbm_in=(0, 1)
    )[0]
    fetched = lax.all_to_all(outgoing, everyone, split_axis=0, concat_axis=0, tiled=True)

    key_one = hop1_slot + slots * hop1_rel
    key_two = (hop2_slot + slots * hop2_rel).reshape(seeds * fanout, fanout_two)
    seed_ids = jnp.arange(seeds, dtype=jnp.int32)[:, None]
    group = (seeds * (1 + hop1_rel) + seed_ids).reshape(-1, 1)
    spare = jnp.full((seeds * fanout, fanout - fanout_two), -1, jnp.int32)
    idx = jnp.concatenate(
        [
            jnp.concatenate([seed_slot[:, None], key_one, seed_ids], 1),
            jnp.concatenate([hop1_slot.reshape(-1, 1), key_two, spare, group], 1),
        ],
        0,
    )
    ct, c, inverse, member, back_hidden = call(
        index_kernel,
        [
            shaped((layers * nodes, slots), BF16),
            shaped((slots, layers * nodes), BF16),
            shaped((layers * nodes, LANES), F32),
            shaped((SEED_ROWS, nodes), BF16),
            shaped((nodes, hidden_units), F32),
        ],
        (idx, cotangent, w_second),
        2 * layers * seeds * hidden_units * hidden_units,
        scratch=[pltpu.VMEM((LANES, hidden_units), F32)],
        hbm_out=range(5),
    )

    layer_in, partial_pre = call(
        first_kernel,
        [shaped((layers * nodes, columns), BF16), shaped((nodes, hidden_units), F32)],
        (fetched, ct, w_first),
        2 * layers * nodes * columns * (slots + hidden_units),
        hbm_in=(1,),
        hbm_out=(0, 1),
    )
    other_pre = shift(partial_pre, "col", 1)
    layer_parts = [layer_in] + [shift(layer_in, "dp", d) for d in range(1, n_x)]

    pack_rows = nodes + half // width * SEED_ROWS + COT_ROWS
    pack_shape = (pack_rows, width)
    slot_grad, *packs = call(
        hidden_kernel,
        [shaped(blocks_shape, BF16)] + [shaped(pack_shape, BF16)] * n_x,
        (
            jnp.stack([lax.axis_index("col"), x]),
            partial_pre,
            other_pre,
            back_hidden,
            member,
            inverse,
            cotangent,
            c,
            w_first,
        ),
        2 * layers * nodes * columns * (slots + hidden_units),
        smem=1,
        scratch=[pltpu.VMEM((n_x, *pack_shape), BF16), pltpu.SemaphoreType.DMA((n_x,))],
        hbm_in=(1, 2, 3, 4, 5, 7),
        hbm_raw=range(1, 1 + n_x),
    )
    packs = [packs[0]] + [shift(packs[d], "dp", d) for d in range(1, n_x)]
    arrived = lax.all_to_all(slot_grad, everyone, split_axis=0, concat_axis=0, tiled=True)

    block_rows = width // n_y
    group_rows = layers * block_rows + (layers * half // columns + 1) * n_x * seeds
    own, *blocks = call(
        functools.partial(weight_kernel, n_x),
        [shaped((block_rows, layers * columns), F32)] + [shaped((group_rows, columns), BF16)] * n_y,
        (y.reshape(1), *layer_parts, *packs),
        2 * n_x * nodes * width * layers * columns,
        smem=1,
        scratch=[pltpu.VMEM((layers, width, columns), F32)],
    )
    blocks = [blocks[0]] + [shift(blocks[d], "y", d) for d in range(1, n_y)]
    grad_columns = layers * (columns + half)
    grads = call(
        functools.partial(group_kernel, layers),
        [shaped((block_rows, grad_columns), BF16)],
        (own, *blocks),
        2 * n_x * n_y * seeds * block_rows * layers * half,
    )[0]
    grads = grads.reshape(n_z, block_rows // n_z, grad_columns)
    grads = lax.all_to_all(grads, "z", split_axis=0, concat_axis=0, tiled=True)
    grad_one, grad_two = call(
        sum_kernel,
        [shaped((layers, block_rows // n_z, wide), F32) for wide in (columns, half)],
        (grads,),
        block_rows * grad_columns,
    )
    grad_one, grad_two = grad_one.transpose(0, 2, 1), grad_two.transpose(0, 2, 1)

    row_grad, squares = call(
        row_kernel,
        [shaped((table_rows, columns), F32), shaped((table_rows // LANES, LANES), F32)],
        (serve_rows, arrived),
        2 * slots * table_rows * columns,
    )
    other_squares = shift(squares, "col", 1)
    new_table, new_accum = call(
        functools.partial(update_kernel, 2 * columns),
        [shaped((table_rows, columns), F32), shaped((table_rows // LANES, LANES), F32)],
        (table, row_grad, accum.reshape(-1, LANES), squares, other_squares),
        3 * table_rows * columns,
    )
    return (new_table, new_accum.reshape(-1), grad_one, grad_two)


def solution(mesh):
    n_dp, n_table, n_col = (mesh.shape[a] for a in ("dp", "table", "col"))
    n_y = 4 if n_table % 4 == 0 and n_table > 4 else 2
    fine = Mesh(mesh.devices.reshape(n_dp, n_y, n_table // n_y, n_col), ("dp", "y", "z", "col"))
    rows = ("dp", "y", "z")
    placed = (
        P(rows, "col"),
        P(rows),
        P(rows, None),
        P(rows),
        P(rows, None),
        P(rows, None, None),
        P(rows, None),
        P(rows, None, None),
        P(rows, None),
        P(None, "col", None),
        P(),
    )
    return jax.shard_map(
        body,
        mesh=fine,
        in_specs=placed,
        out_specs=(P(rows, "col"), P(rows), P(None, "col", rows), P(None, "col", rows)),
        check_vma=False,
    )
```

```python
import functools
import jax
import jax.numpy as jnp
from jax import lax
from jax.experimental import pallas as pl
from jax.experimental.pallas import tpu as pltpu
from jax.sharding import Mesh
from jax.sharding import PartitionSpec as P

LEARNING_RATE = 0.1
BF16 = jnp.bfloat16
F32 = jnp.float32
LANES = 128
SEED_ROWS = 32
COT_ROWS = 16


def matmul(a, b, contract=(1, 0)):
    dims = (((contract[0],), (contract[1],)), ((), ()))
    return lax.dot_general(a, b, dims, preferred_element_type=F32)


def row_to_column(row):
    return jnp.transpose(jnp.broadcast_to(row, (LANES, LANES)))[:, 0:1]


def column_to_row(column):
    return jnp.transpose(jnp.broadcast_to(column, (LANES, LANES)))[0:1, :]


class Incoming:
    def __init__(self, source, buffer, semaphore):
        self.buffer, self.waiting = buffer, True
        self.shape = buffer.shape
        self.copy = pltpu.make_async_copy(source, buffer, semaphore)
        self.copy.start()

    def get(self):
        if self.waiting:
            self.copy.wait()
        self.waiting = False
        return self.buffer


class Outgoing:
    def __init__(self, target, buffer, semaphore):
        self.buffer = buffer
        self.copy = pltpu.make_async_copy(buffer, target, semaphore)

    def send(self):
        self.copy.start()


def call(kernel, outs, operands, smem=0, scratch=(), hbm_in=(), hbm_out=(), raw_in=(), hbm_raw=()):
    name = getattr(kernel, "func", kernel)
    limit, flops = LIMITS.get(name, 12), COSTS.get(name, 10**12)
    moved = sum(o.size * o.dtype.itemsize for o in list(operands) + list(outs))
    specs = [
        pl.BlockSpec(memory_space=pltpu.SMEM if i < smem else pltpu.HBM if i in hbm_in or i in raw_in else pltpu.VMEM)
        for i in range(len(operands))
    ]
    made = [
        pl.BlockSpec(memory_space=pltpu.HBM if i in hbm_out or i in hbm_raw else pltpu.VMEM)
        for i in range(len(outs))
    ]
    buffers = [pltpu.VMEM(operands[i].shape, operands[i].dtype) for i in hbm_in]
    buffers += [pltpu.VMEM(outs[i].shape, outs[i].dtype) for i in hbm_out]
    semaphores = [pltpu.SemaphoreType.DMA((len(buffers),))] if buffers else []

    def wrapped(*refs):
        refs = list(refs)
        if not buffers:
            kernel(*refs)
            return
        first = len(operands) + len(outs)
        held, sems = refs[first : first + len(buffers)], refs[first + len(buffers)]
        rest = refs[first + len(buffers) + 1 :]
        for j, i in enumerate(hbm_in):
            refs[i] = Incoming(refs[i], held[j], sems.at[j])
        leaving = []
        for j, i in enumerate(hbm_out, len(hbm_in)):
            place = len(operands) + i
            refs[place] = Outgoing(refs[place], held[j], sems.at[j])
            leaving.append(refs[place])
        kernel(*refs[:first], *rest)
        for out in leaving:
            out.copy.wait()

    return pl.pallas_call(
        wrapped,
        out_shape=tuple(outs),
        in_specs=specs,
        out_specs=tuple(made),
        scratch_shapes=buffers + semaphores + list(scratch),
        compiler_params=pltpu.CompilerParams(vmem_limit_bytes=limit * 1024 * 1024),
        cost_estimate=pl.CostEstimate(flops=flops, bytes_accessed=moved, transcendentals=0),
    )(*operands)


def shaped(shape, dtype):
    return jax.ShapeDtypeStruct(shape, dtype)


def serve_kernel(serve_ref, table_ref, out_ref, onehot):
    serve = serve_ref.get()[...]
    lanes = lax.broadcasted_iota(jnp.int32, (LANES, onehot.shape[1]), 1)
    for block in range(serve.shape[1] // LANES):
        span = slice(block * LANES, (block + 1) * LANES)
        onehot[span, :] = jnp.where(row_to_column(serve[:, span]) == lanes, 1.0, 0.0).astype(BF16)
    rows = table_ref.get()[...].astype(BF16)
    out_ref[...] = matmul(onehot[...], rows).astype(BF16).reshape(out_ref.shape)


def index_kernel(idx_ref, cot_ref, w2_ref, *refs):
    outs, spread = refs[:-1], refs[-1]
    ct_ref, c_ref, inv_ref, e_ref, back_ref = (o.buffer for o in outs)
    nodes = idx_ref.shape[0]
    slots = ct_ref.shape[1]
    seeds = cot_ref.shape[0]
    neighbours = idx_ref.shape[1] - 2
    lanes = lax.broadcasted_iota(jnp.int32, (nodes, 2 * slots), 1)
    idx = idx_ref[...]
    counts = jnp.zeros((nodes, 2 * slots), F32)
    for j in range(1, 1 + neighbours):
        counts = counts + jnp.where(idx[:, j : j + 1] == lanes, 1.0, 0.0)
    own = jnp.where(idx[:, 0:1] == lanes[:, :slots], 1.0, 0.0)
    parts = (own, counts[:, :slots], counts[:, slots:])
    spread[...] = jnp.zeros(spread.shape, F32)
    for k, part in enumerate(parts):
        span = slice(k * nodes, (k + 1) * nodes)
        ct_ref[span, :] = part.astype(BF16)
        c_ref[:, span] = jnp.transpose(part).astype(BF16)
        if k == 0:
            inverse = jnp.ones((nodes, 1), F32)
        else:
            inverse = 1.0 / jnp.maximum(jnp.sum(part, axis=1, keepdims=True), 1.0)
        inv_ref[span, :] = jnp.broadcast_to(inverse, (nodes, LANES))
        back = matmul(cot_ref[...], w2_ref[k], (1, 1))
        spread[k * seeds : (k + 1) * seeds, :] = back * inverse[:seeds]
    groups = lax.broadcasted_iota(jnp.int32, (nodes, LANES), 1)
    member = jnp.where(idx[:, neighbours + 1 : neighbours + 2] == groups, 1.0, 0.0)
    e_ref[...] = jnp.transpose(member)[:SEED_ROWS].astype(BF16)
    whole = spread[...]
    high = whole.astype(BF16)
    low = (whole - high.astype(F32)).astype(BF16)
    for out in outs[:-1]:
        out.send()
    back_ref[...] = matmul(member.astype(BF16), high) + matmul(member.astype(BF16), low)
    outs[-1].send()


def first_kernel(fetched_ref, ct_ref, w1_ref, layer_ref, partial_ref):
    layers = w1_ref.shape[0]
    layer_out, partial_out = layer_ref, partial_ref
    layer_ref, partial_ref = layer_ref.buffer, partial_ref.buffer
    nodes = partial_ref.shape[0]
    fetched = fetched_ref.get()[...].reshape(ct_ref.shape[1], layer_ref.shape[1])
    total = None
    ct_ref = ct_ref.get()
    ones = jnp.ones((ct_ref.shape[1], LANES), BF16)
    for k in range(layers):
        span = slice(k * nodes, (k + 1) * nodes)
        summed = matmul(ct_ref[span, :], fetched)
        inverse = 1.0 / jnp.maximum(matmul(ct_ref[span, :], ones)[:, 0:1], 1.0)
        layer_ref[span, :] = (summed * inverse).astype(BF16)
    layer_out.send()
    for k in range(layers):
        term = matmul(layer_ref[k * nodes : (k + 1) * nodes, :], w1_ref.get()[k])
        total = term if total is None else total + term
    partial_ref[...] = total
    partial_out.send()


def hidden_kernel(place_ref, mine_ref, other_ref, back_ref, e_ref, inv_ref, cot_ref, layer_ref, out_ref, *refs):
    packs, stage, sems = refs[:-2], refs[-2], refs[-1]
    nodes = mine_ref.shape[0]
    width = stage.shape[2]
    seeds = cot_ref.shape[0]
    layers = inv_ref.shape[0] // nodes
    values = mine_ref.get()[...] + other_ref.get()[...]
    back_ref, e_ref, inv_ref = back_ref.get(), e_ref.get(), inv_ref.get()
    sigma = jax.nn.sigmoid(values)
    hidden = (values * sigma).astype(BF16)
    slope = sigma * (1.0 + values * (1.0 - sigma))
    back = (back_ref[...] * slope).astype(BF16)
    out_ref[...] = back
    scale = jnp.concatenate(
        [inv_ref[k * nodes : k * nodes + seeds, 0:1] for k in range(layers)]
        + [jnp.zeros((SEED_ROWS - layers * seeds, 1), F32)],
        0,
    )
    second = matmul(e_ref[...], hidden) * scale
    half = second.shape[1] // 2
    second = jnp.where(place_ref[0] == 0, second[:, :half], second[:, half:]).astype(BF16)
    cot = cot_ref[...].astype(F32)
    cot = jnp.concatenate([cot, jnp.zeros((COT_ROWS - seeds, cot.shape[1]), F32)], 0).astype(BF16)
    for j in range(len(packs)):
        span = slice(j * width, (j + 1) * width)
        stage[j, :nodes, :] = back[:, span]
        for part in range(half // width):
            first = nodes + part * SEED_ROWS
            stage[j, first : first + SEED_ROWS, :] = second[:, part * width : (part + 1) * width]
        first = nodes + half // width * SEED_ROWS
        stage[j, first : first + COT_ROWS, :] = cot[:, span]
    moves = []
    for d, pack in enumerate(packs):
        chosen = stage.at[lax.rem(place_ref[1] + d, len(packs))]
        if d != len(packs) // 2:
            moves.append((chosen, pack))
            continue
        start = 0
        for source in (chosen, layer_ref):
            rows, wide = source.shape
            for lane in range(0, wide, LANES):
                moves.append((source.at[:, lane : lane + LANES], pack.at[start : start + rows, :]))
                start += rows
    copies = [pltpu.make_async_copy(source, target, sems.at[i]) for i, (source, target) in enumerate(moves)]
    for copy in copies:
        copy.start()
    for copy in copies:
        copy.wait()


def slot_kernel(back_ref, inv_ref, c_ref, w1_ref, slot_ref):
    nodes = back_ref.shape[0]
    total = None
    for k in range(w1_ref.shape[0]):
        span = slice(k * nodes, (k + 1) * nodes)
        back_in = matmul(back_ref[...], w1_ref.get()[k], (1, 1)) * inv_ref.get()[span, 0:1]
        term = matmul(c_ref.get()[:, span], back_in.astype(BF16))
        total = term if total is None else total + term
    slot_ref[...] = total.astype(BF16).reshape(slot_ref.shape)


def weight_kernel(count, place_ref, *refs):
    layer_refs, pack_refs = list(refs[: count - 1]), list(refs[count - 1 : 2 * count - 1])
    own_ref, outs, total = refs[2 * count - 1], refs[2 * count : -1], refs[-1]
    pack_rows, width = pack_refs[0].shape
    layer_rows, columns = layer_refs[0].shape
    layer_parts = [r.get()[...] for r in layer_refs]
    far = pack_refs[count // 2][...]
    parts, start = [], 0
    for rows, wide in ((pack_rows, width), (layer_rows, columns)):
        lanes = [far[start + i * rows : start + (i + 1) * rows] for i in range(wide // LANES)]
        parts.append(jnp.concatenate(lanes, 1))
        start += rows * len(lanes)
    layer_parts.insert(count // 2, parts[1])
    packs = [parts[0] if d == count // 2 else ref[...] for d, ref in enumerate(pack_refs)]
    nodes = LANES
    relations = layer_rows // nodes
    rows = own_ref.shape[0]
    left = jnp.concatenate([p[:nodes, :] for p in packs], 0)
    for k in range(relations):
        right = jnp.concatenate([r[k * nodes : (k + 1) * nodes, :] for r in layer_parts], 0)
        total[k] = matmul(left, right, (0, 0))
    pieces = (pack_rows - nodes - COT_ROWS) // SEED_ROWS
    half = pieces * width
    seeds = SEED_ROWS // (relations + 1)
    first = nodes + pieces * SEED_ROWS
    cots = jnp.concatenate([p[first : first + COT_ROWS, :].astype(F32)[:seeds] for p in packs], 0)
    seconds = [
        jnp.concatenate(
            [p[nodes + part * SEED_ROWS : nodes + (part + 1) * SEED_ROWS, :].astype(F32) for part in range(pieces)],
            1,
        )
        for p in packs
    ]
    second = jnp.concatenate(
        [jnp.concatenate([s[k * seeds : (k + 1) * seeds] for s in seconds], 0) for k in range(relations)], 1
    ).astype(BF16)
    group = count * seeds
    tail = relations * rows
    for d, out in enumerate(outs):
        target = lax.rem(place_ref[0] + d, len(outs))
        start = pl.multiple_of(target * rows, rows)
        for k in range(relations):
            block = total[k, pl.ds(start, rows), :]
            if d == 0:
                own_ref[:, k * columns : (k + 1) * columns] = block
            else:
                out[k * rows : (k + 1) * rows, :] = block.astype(BF16)
        for piece in range(relations * half // columns):
            out[tail + piece * group : tail + (piece + 1) * group, :] = second[
                :, piece * columns : (piece + 1) * columns
            ]
        chosen = cots[:, :rows]
        for j in range(1, len(outs)):
            chosen = jnp.where(target == j, cots[:, j * rows : (j + 1) * rows], chosen)
        chosen = jnp.concatenate([chosen, jnp.zeros((group, columns - rows), F32)], 1)
        out[out.shape[0] - group :, :] = chosen.astype(BF16)


def group_kernel(relations, own_ref, *refs):
    packs, out_ref = refs[:-1], refs[-1]
    rows = own_ref.shape[0]
    columns = packs[0].shape[1]
    tail = relations * rows
    wide = out_ref.shape[1] - relations * columns
    pieces = wide // columns
    group = (packs[0].shape[0] - tail) // (pieces + 1)
    for k in range(relations):
        span = slice(k * columns, (k + 1) * columns)
        block = own_ref[:, span]
        for pack in packs[1:]:
            block = block + pack[k * rows : (k + 1) * rows, :].astype(F32)
        out_ref[:, span] = block.astype(BF16)
    cots = jnp.concatenate([p[tail + pieces * group :, :] for p in packs], 0)
    for piece in range(pieces):
        first = tail + piece * group
        second = jnp.concatenate([p[first : first + group, :] for p in packs], 0)
        start = (relations + piece) * columns
        out_ref[:, start : start + columns] = matmul(cots, second, (0, 0))[:rows].astype(BF16)


def sum_kernel(parts_ref, one_ref, two_ref):
    total = jnp.sum(parts_ref[...].astype(F32), axis=0)
    start = 0
    for ref in (one_ref, two_ref):
        wide = ref.shape[2]
        for k in range(ref.shape[0]):
            ref[k] = total[:, start : start + wide]
            start += wide


def row_kernel(serve_ref, arrived_ref, grad_ref, square_ref):
    rows = lax.broadcasted_iota(jnp.int32, (LANES, serve_ref.shape[1]), 0)
    arrived = arrived_ref[...].reshape(serve_ref.shape[1], grad_ref.shape[1])
    for block in range(grad_ref.shape[0] // LANES):
        span = slice(block * LANES, (block + 1) * LANES)
        onehot = jnp.where(serve_ref[...] == rows + block * LANES, 1.0, 0.0).astype(BF16)
        grad = matmul(onehot, arrived)
        grad_ref[span, :] = grad
        square_ref[block : block + 1, :] = column_to_row(jnp.sum(grad * grad, axis=1, keepdims=True))


def update_kernel(columns, table_ref, grad_ref, accum_ref, mine_ref, other_ref, table_out, accum_out):
    accum = accum_ref[...] + (mine_ref[...] + other_ref[...]) / columns
    accum_out[...] = accum
    inverse = lax.rsqrt(accum)
    for block in range(accum.shape[0]):
        span = slice(block * LANES, (block + 1) * LANES)
        scale = row_to_column(inverse[block : block + 1, :])
        table_out[span, :] = table_ref[span, :] - LEARNING_RATE * grad_ref[span, :] * scale


def shift(array, axis, by):
    size = lax.axis_size(axis)
    return lax.ppermute(array, axis, [(i, (i + by) % size) for i in range(size)])


LIMITS = {serve_kernel: 60, index_kernel: 60, first_kernel: 60, hidden_kernel: 60, slot_kernel: 50}
COSTS = {update_kernel: 0, group_kernel: 0, row_kernel: 0}


def body(
    table,
    accum,
    serve_rows,
    seed_slot,
    hop1_slot,
    hop2_slot,
    hop1_rel,
    hop2_rel,
    cotangent,
    w_first,
    w_second,
):
    everyone = ("dp", "y", "z")
    owners = lax.axis_size(everyone)
    table_rows, columns = table.shape
    slots = serve_rows.shape[1]
    seeds, fanout = hop1_slot.shape
    fanout_two = hop2_slot.shape[2]
    nodes = seeds + seeds * fanout
    layers, hidden_units = w_second.shape[:2]
    half = hidden_units // 2
    n_x, n_y, n_z = (lax.axis_size(a) for a in everyone)
    x, y = lax.axis_index("dp"), lax.axis_index("y")
    width = hidden_units // n_x

    blocks_shape = (owners, slots // owners, columns)
    outgoing = call(
        serve_kernel, [shaped(blocks_shape, BF16)], (serve_rows, table), scratch=[pltpu.VMEM((slots, table_rows), BF16)], hbm_in=(0, 1)
    )[0]
    fetched = lax.all_to_all(outgoing, everyone, split_axis=0, concat_axis=0, tiled=True)

    key_one = hop1_slot + slots * hop1_rel
    key_two = (hop2_slot + slots * hop2_rel).reshape(seeds * fanout, fanout_two)
    seed_ids = jnp.arange(seeds, dtype=jnp.int32)[:, None]
    group = (seeds * (1 + hop1_rel) + seed_ids).reshape(-1, 1)
    spare = jnp.full((seeds * fanout, fanout - fanout_two), -1, jnp.int32)
    idx = jnp.concatenate(
        [
            jnp.concatenate([seed_slot[:, None], key_one, seed_ids], 1),
            jnp.concatenate([hop1_slot.reshape(-1, 1), key_two, spare, group], 1),
        ],
        0,
    )
    ct, c, inverse, member, back_hidden = call(
        index_kernel,
        [
            shaped((layers * nodes, slots), BF16),
            shaped((slots, layers * nodes), BF16),
            shaped((layers * nodes, LANES), F32),
            shaped((SEED_ROWS, nodes), BF16),
            shaped((nodes, hidden_units), F32),
        ],
        (idx, cotangent, w_second),
        scratch=[pltpu.VMEM((LANES, hidden_units), F32)],
        hbm_out=range(5),
    )

    layer_in, partial_pre = call(
        first_kernel,
        [shaped((layers * nodes, columns), BF16), shaped((nodes, hidden_units), F32)],
        (fetched, ct, w_first),
        hbm_in=(0, 1, 2),
        hbm_out=(0, 1),
    )
    other_pre = shift(partial_pre, "col", 1)
    layer_parts = [layer_in] + [shift(layer_in, "dp", d) for d in range(1, n_x) if d != n_x // 2]

    pack_rows = nodes + half // width * SEED_ROWS + COT_ROWS
    pack_shape = (pack_rows, width)
    far = n_x // 2
    far_shape = ((pack_rows * width + layers * nodes * columns) // LANES, LANES)
    back, *packs = call(
        hidden_kernel,
        [shaped((nodes, hidden_units), BF16)] + [shaped(far_shape if d == far else pack_shape, BF16) for d in range(n_x)],
        (
            jnp.stack([lax.axis_index("col"), x]),
            partial_pre,
            other_pre,
            back_hidden,
            member,
            inverse,
            cotangent,
            layer_in,
        ),
        smem=1,
        scratch=[pltpu.VMEM((n_x, *pack_shape), BF16), pltpu.SemaphoreType.DMA((n_x - 1 + (width + columns) // LANES,))],
        hbm_in=(1, 2, 3, 4, 5),
        raw_in=(7,),
        hbm_raw=range(1, 1 + n_x),
    )
    packs = [packs[0]] + [shift(packs[d], "dp", d) for d in range(1, n_x)]
    back, *layer_parts[1:] = lax.optimization_barrier((back, *layer_parts[1:]))
    slot_grad = call(slot_kernel, [shaped(blocks_shape, BF16)], (back, inverse, c, w_first), hbm_in=(1, 2, 3))[0]
    arrived = lax.all_to_all(slot_grad, everyone, split_axis=0, concat_axis=0, tiled=True)

    block_rows = width // n_y
    group_rows = layers * block_rows + (layers * half // columns + 1) * n_x * seeds
    own, *blocks = call(
        functools.partial(weight_kernel, n_x),
        [shaped((block_rows, layers * columns), F32)] + [shaped((group_rows, columns), BF16)] * n_y,
        (y.reshape(1), *layer_parts, *packs),
        smem=1,
        hbm_in=range(1, n_x),
        scratch=[pltpu.VMEM((layers, width, columns), F32)],
    )
    blocks = [blocks[0]] + [shift(blocks[d], "y", d) for d in range(1, n_y)]
    grad_columns = layers * (columns + half)
    grads = call(
        functools.partial(group_kernel, layers),
        [shaped((block_rows, grad_columns), BF16)],
        (own, *blocks),
    )[0]
    grads = grads.reshape(n_z, block_rows // n_z, grad_columns)
    grads = lax.all_to_all(grads, "z", split_axis=0, concat_axis=0, tiled=True)
    grad_one, grad_two = call(
        sum_kernel,
        [shaped((layers, block_rows // n_z, wide), F32) for wide in (columns, half)],
        (grads,),
    )
    grad_one, grad_two = grad_one.transpose(0, 2, 1), grad_two.transpose(0, 2, 1)

    row_grad, squares = call(
        row_kernel,
        [shaped((table_rows, columns), F32), shaped((table_rows // LANES, LANES), F32)],
        (serve_rows, arrived),
    )
    other_squares = shift(squares, "col", 1)
    new_table, new_accum = call(
        functools.partial(update_kernel, 2 * columns),
        [shaped((table_rows, columns), F32), shaped((table_rows // LANES, LANES), F32)],
        (table, row_grad, accum.reshape(-1, LANES), squares, other_squares),
    )
    return (new_table, new_accum.reshape(-1), grad_one, grad_two)


def solution(mesh):
    n_dp, n_table, n_col = (mesh.shape[a] for a in ("dp", "table", "col"))
    n_y = 4 if n_table % 4 == 0 and n_table > 4 else 2
    fine = Mesh(mesh.devices.reshape(n_dp, n_y, n_table // n_y, n_col), ("dp", "y", "z", "col"))
    rows = ("dp", "y", "z")
    placed = (
        P(rows, "col"),
        P(rows),
        P(rows, None),
        P(rows),
        P(rows, None),
        P(rows, None, None),
        P(rows, None),
        P(rows, None, None),
        P(rows, None),
        P(None, "col", None),
        P(),
    )
    return jax.shard_map(
        body,
        mesh=fine,
        in_specs=placed,
        out_specs=(P(rows, "col"), P(rows), P(None, "col", rows), P(None, "col", rows)),
        check_vma=False,
    )
```

```python
import functools
import jax
import jax.numpy as jnp
from jax import lax
from jax.experimental import pallas as pl
from jax.experimental.pallas import tpu as pltpu
from jax.sharding import Mesh
from jax.sharding import PartitionSpec as P

LEARNING_RATE = 0.1
BF16 = jnp.bfloat16
F32 = jnp.float32
LANES = 128
SEED_ROWS = 32
COT_ROWS = 16


def matmul(a, b, contract=(1, 0)):
    dims = (((contract[0],), (contract[1],)), ((), ()))
    return lax.dot_general(a, b, dims, preferred_element_type=F32)


def row_to_column(row):
    return jnp.transpose(jnp.broadcast_to(row, (LANES, LANES)))[:, 0:1]


def column_to_row(column):
    return jnp.transpose(jnp.broadcast_to(column, (LANES, LANES)))[0:1, :]


class Incoming:
    def __init__(self, source, buffer, semaphore):
        self.buffer, self.waiting = buffer, True
        self.shape = buffer.shape
        self.copy = pltpu.make_async_copy(source, buffer, semaphore)
        self.copy.start()

    def get(self):
        if self.waiting:
            self.copy.wait()
        self.waiting = False
        return self.buffer


class Outgoing:
    def __init__(self, target, buffer, semaphore):
        self.buffer = buffer
        self.copy = pltpu.make_async_copy(buffer, target, semaphore)

    def send(self):
        self.copy.start()


def call(kernel, outs, operands, smem=0, scratch=(), hbm_in=(), hbm_out=(), hbm_raw=()):
    name = getattr(kernel, "func", kernel)
    limit, flops = LIMITS.get(name, 12), COSTS.get(name, 10**12)
    moved = sum(o.size * o.dtype.itemsize for o in list(operands) + list(outs))
    specs = [
        pl.BlockSpec(memory_space=pltpu.SMEM if i < smem else pltpu.HBM if i in hbm_in else pltpu.VMEM)
        for i in range(len(operands))
    ]
    made = [
        pl.BlockSpec(memory_space=pltpu.HBM if i in hbm_out or i in hbm_raw else pltpu.VMEM)
        for i in range(len(outs))
    ]
    buffers = [pltpu.VMEM(operands[i].shape, operands[i].dtype) for i in hbm_in]
    buffers += [pltpu.VMEM(outs[i].shape, outs[i].dtype) for i in hbm_out]
    semaphores = [pltpu.SemaphoreType.DMA((len(buffers),))] if buffers else []

    def wrapped(*refs):
        refs = list(refs)
        if not buffers:
            kernel(*refs)
            return
        first = len(operands) + len(outs)
        held, sems = refs[first : first + len(buffers)], refs[first + len(buffers)]
        rest = refs[first + len(buffers) + 1 :]
        for j, i in enumerate(hbm_in):
            refs[i] = Incoming(refs[i], held[j], sems.at[j])
        leaving = []
        for j, i in enumerate(hbm_out, len(hbm_in)):
            place = len(operands) + i
            refs[place] = Outgoing(refs[place], held[j], sems.at[j])
            leaving.append(refs[place])
        kernel(*refs[:first], *rest)
        for out in leaving:
            out.copy.wait()

    return pl.pallas_call(
        wrapped,
        out_shape=tuple(outs),
        in_specs=specs,
        out_specs=tuple(made),
        scratch_shapes=buffers + semaphores + list(scratch),
        compiler_params=pltpu.CompilerParams(vmem_limit_bytes=limit * 1024 * 1024),
        cost_estimate=pl.CostEstimate(flops=flops, bytes_accessed=moved, transcendentals=0),
    )(*operands)


def shaped(shape, dtype):
    return jax.ShapeDtypeStruct(shape, dtype)


def serve_kernel(serve_ref, table_ref, out_ref, onehot):
    serve = serve_ref.get()[...]
    lanes = lax.broadcasted_iota(jnp.int32, (LANES, onehot.shape[1]), 1)
    for block in range(serve.shape[1] // LANES):
        span = slice(block * LANES, (block + 1) * LANES)
        onehot[span, :] = jnp.where(row_to_column(serve[:, span]) == lanes, 1.0, 0.0).astype(BF16)
    rows = table_ref.get()[...].astype(BF16)
    out_ref[...] = matmul(onehot[...], rows).astype(BF16).reshape(out_ref.shape)


def index_kernel(idx_ref, cot_ref, w2_ref, *refs):
    outs, spread = refs[:-1], refs[-1]
    ct_ref, c_ref, inv_ref, e_ref, back_ref = (o.buffer for o in outs)
    nodes = idx_ref.shape[0]
    slots = ct_ref.shape[1]
    seeds = cot_ref.shape[0]
    neighbours = idx_ref.shape[1] - 2
    lanes = lax.broadcasted_iota(jnp.int32, (nodes, 2 * slots), 1)
    idx = idx_ref[...]
    counts = jnp.zeros((nodes, 2 * slots), F32)
    for j in range(1, 1 + neighbours):
        counts = counts + jnp.where(idx[:, j : j + 1] == lanes, 1.0, 0.0)
    own = jnp.where(idx[:, 0:1] == lanes[:, :slots], 1.0, 0.0)
    parts = (own, counts[:, :slots], counts[:, slots:])
    spread[...] = jnp.zeros(spread.shape, F32)
    for k, part in enumerate(parts):
        span = slice(k * nodes, (k + 1) * nodes)
        ct_ref[span, :] = part.astype(BF16)
        c_ref[:, span] = jnp.transpose(part).astype(BF16)
        if k == 0:
            inverse = jnp.ones((nodes, 1), F32)
        else:
            inverse = 1.0 / jnp.maximum(jnp.sum(part, axis=1, keepdims=True), 1.0)
        inv_ref[span, :] = jnp.broadcast_to(inverse, (nodes, LANES))
        back = matmul(cot_ref[...], w2_ref[k], (1, 1))
        spread[k * seeds : (k + 1) * seeds, :] = back * inverse[:seeds]
    groups = lax.broadcasted_iota(jnp.int32, (nodes, LANES), 1)
    member = jnp.where(idx[:, neighbours + 1 : neighbours + 2] == groups, 1.0, 0.0)
    e_ref[...] = jnp.transpose(member)[:SEED_ROWS].astype(BF16)
    whole = spread[...]
    high = whole.astype(BF16)
    low = (whole - high.astype(F32)).astype(BF16)
    for out in outs[:-1]:
        out.send()
    back_ref[...] = matmul(member.astype(BF16), high) + matmul(member.astype(BF16), low)
    outs[-1].send()


def first_kernel(fetched_ref, ct_ref, w1_ref, layer_ref, partial_ref):
    layers = w1_ref.shape[0]
    layer_out, partial_out = layer_ref, partial_ref
    layer_ref, partial_ref = layer_ref.buffer, partial_ref.buffer
    nodes = partial_ref.shape[0]
    fetched = fetched_ref.get()[...].reshape(ct_ref.shape[1], layer_ref.shape[1])
    total = None
    ct_ref = ct_ref.get()
    ones = jnp.ones((ct_ref.shape[1], LANES), BF16)
    for k in range(layers):
        span = slice(k * nodes, (k + 1) * nodes)
        summed = matmul(ct_ref[span, :], fetched)
        inverse = 1.0 / jnp.maximum(matmul(ct_ref[span, :], ones)[:, 0:1], 1.0)
        layer_ref[span, :] = (summed * inverse).astype(BF16)
    layer_out.send()
    for k in range(layers):
        term = matmul(layer_ref[k * nodes : (k + 1) * nodes, :], w1_ref.get()[k])
        total = term if total is None else total + term
    partial_ref[...] = total
    partial_out.send()


def hidden_kernel(place_ref, mine_ref, other_ref, back_ref, e_ref, inv_ref, cot_ref, layer_ref, out_ref, *refs):
    packs, stage, sems = refs[:-2], refs[-2], refs[-1]
    nodes = mine_ref.shape[0]
    width = stage.shape[2]
    seeds = cot_ref.shape[0]
    layers = inv_ref.shape[0] // nodes
    values = mine_ref.get()[...] + other_ref.get()[...]
    back_ref, e_ref, inv_ref = back_ref.get(), e_ref.get(), inv_ref.get()
    sigma = jax.nn.sigmoid(values)
    hidden = (values * sigma).astype(BF16)
    slope = sigma * (1.0 + values * (1.0 - sigma))
    back = (back_ref[...] * slope).astype(BF16)
    out_ref[...] = back
    scale = jnp.concatenate(
        [inv_ref[k * nodes : k * nodes + seeds, 0:1] for k in range(layers)]
        + [jnp.zeros((SEED_ROWS - layers * seeds, 1), F32)],
        0,
    )
    second = matmul(e_ref[...], hidden) * scale
    half = second.shape[1] // 2
    second = jnp.where(place_ref[0] == 0, second[:, :half], second[:, half:]).astype(BF16)
    cot = cot_ref[...].astype(F32)
    cot = jnp.concatenate([cot, jnp.zeros((COT_ROWS - seeds, cot.shape[1]), F32)], 0).astype(BF16)
    for j in range(len(packs)):
        span = slice(j * width, (j + 1) * width)
        stage[j, :nodes, :] = back[:, span]
        for part in range(half // width):
            first = nodes + part * SEED_ROWS
            stage[j, first : first + SEED_ROWS, :] = second[:, part * width : (part + 1) * width]
        first = nodes + half // width * SEED_ROWS
        stage[j, first : first + COT_ROWS, :] = cot[:, span]
    moves = []
    for d, pack in enumerate(packs):
        chosen = stage.at[lax.rem(place_ref[1] + d, len(packs))]
        if d != len(packs) // 2:
            moves.append((chosen, pack))
            continue
        start = 0
        for source in (chosen, layer_ref.get()):
            rows, wide = source.shape
            for lane in range(0, wide, LANES):
                moves.append((source.at[:, lane : lane + LANES], pack.at[start : start + rows, :]))
                start += rows
    copies = [pltpu.make_async_copy(source, target, sems.at[i]) for i, (source, target) in enumerate(moves)]
    for copy in copies:
        copy.start()
    for copy in copies:
        copy.wait()


def slot_kernel(back_ref, inv_ref, c_ref, w1_ref, slot_ref):
    nodes = back_ref.shape[0]
    total = None
    for k in range(w1_ref.shape[0]):
        span = slice(k * nodes, (k + 1) * nodes)
        back_in = matmul(back_ref[...], w1_ref.get()[k], (1, 1)) * inv_ref.get()[span, 0:1]
        term = matmul(c_ref.get()[:, span], back_in.astype(BF16))
        total = term if total is None else total + term
    slot_ref[...] = total.astype(BF16).reshape(slot_ref.shape)


def weight_kernel(count, place_ref, *refs):
    layer_refs, pack_refs = list(refs[: count - 1]), list(refs[count - 1 : 2 * count - 1])
    own_ref, outs, total = refs[2 * count - 1], refs[2 * count : -1], refs[-1]
    pack_rows, width = pack_refs[0].shape
    layer_rows, columns = layer_refs[0].shape
    layer_parts = [r.get()[...] for r in layer_refs]
    far = pack_refs[count // 2][...]
    parts, start = [], 0
    for rows, wide in ((pack_rows, width), (layer_rows, columns)):
        lanes = [far[start + i * rows : start + (i + 1) * rows] for i in range(wide // LANES)]
        parts.append(jnp.concatenate(lanes, 1))
        start += rows * len(lanes)
    layer_parts.insert(count // 2, parts[1])
    packs = [parts[0] if d == count // 2 else ref[...] for d, ref in enumerate(pack_refs)]
    nodes = LANES
    relations = layer_rows // nodes
    rows = own_ref.shape[0]
    left = jnp.concatenate([p[:nodes, :] for p in packs], 0)
    for k in range(relations):
        right = jnp.concatenate([r[k * nodes : (k + 1) * nodes, :] for r in layer_parts], 0)
        total[k] = matmul(left, right, (0, 0))
    pieces = (pack_rows - nodes - COT_ROWS) // SEED_ROWS
    half = pieces * width
    seeds = SEED_ROWS // (relations + 1)
    first = nodes + pieces * SEED_ROWS
    cots = jnp.concatenate([p[first : first + COT_ROWS, :].astype(F32)[:seeds] for p in packs], 0)
    seconds = [
        jnp.concatenate(
            [p[nodes + part * SEED_ROWS : nodes + (part + 1) * SEED_ROWS, :].astype(F32) for part in range(pieces)],
            1,
        )
        for p in packs
    ]
    second = jnp.concatenate(
        [jnp.concatenate([s[k * seeds : (k + 1) * seeds] for s in seconds], 0) for k in range(relations)], 1
    ).astype(BF16)
    group = count * seeds
    tail = relations * rows
    for d, out in enumerate(outs):
        target = lax.rem(place_ref[0] + d, len(outs))
        start = pl.multiple_of(target * rows, rows)
        for k in range(relations):
            block = total[k, pl.ds(start, rows), :]
            if d == 0:
                own_ref[:, k * columns : (k + 1) * columns] = block
            else:
                out[k * rows : (k + 1) * rows, :] = block.astype(BF16)
        for piece in range(relations * half // columns):
            out[tail + piece * group : tail + (piece + 1) * group, :] = second[
                :, piece * columns : (piece + 1) * columns
            ]
        chosen = cots[:, :rows]
        for j in range(1, len(outs)):
            chosen = jnp.where(target == j, cots[:, j * rows : (j + 1) * rows], chosen)
        chosen = jnp.concatenate([chosen, jnp.zeros((group, columns - rows), F32)], 1)
        out[out.shape[0] - group :, :] = chosen.astype(BF16)


def group_kernel(relations, own_ref, *refs):
    packs, out_ref = refs[:-1], refs[-1]
    rows = own_ref.shape[0]
    columns = packs[0].shape[1]
    tail = relations * rows
    wide = out_ref.shape[1] - relations * columns
    pieces = wide // columns
    group = (packs[0].shape[0] - tail) // (pieces + 1)
    for k in range(relations):
        span = slice(k * columns, (k + 1) * columns)
        block = own_ref[:, span]
        for pack in packs[1:]:
            block = block + pack[k * rows : (k + 1) * rows, :].astype(F32)
        out_ref[:, span] = block.astype(BF16)
    cots = jnp.concatenate([p[tail + pieces * group :, :] for p in packs], 0)
    for piece in range(pieces):
        first = tail + piece * group
        second = jnp.concatenate([p[first : first + group, :] for p in packs], 0)
        start = (relations + piece) * columns
        out_ref[:, start : start + columns] = matmul(cots, second, (0, 0))[:rows].astype(BF16)


def sum_kernel(parts_ref, one_ref, two_ref):
    total = jnp.sum(parts_ref[...].astype(F32), axis=0)
    start = 0
    for ref in (one_ref, two_ref):
        wide = ref.shape[2]
        for k in range(ref.shape[0]):
            ref[k] = total[:, start : start + wide]
            start += wide


def row_kernel(serve_ref, arrived_ref, grad_ref, square_ref):
    rows = lax.broadcasted_iota(jnp.int32, (LANES, serve_ref.shape[1]), 0)
    arrived = arrived_ref[...].reshape(serve_ref.shape[1], grad_ref.shape[1])
    for block in range(grad_ref.shape[0] // LANES):
        span = slice(block * LANES, (block + 1) * LANES)
        onehot = jnp.where(serve_ref[...] == rows + block * LANES, 1.0, 0.0).astype(BF16)
        grad = matmul(onehot, arrived)
        grad_ref[span, :] = grad
        square_ref[block : block + 1, :] = column_to_row(jnp.sum(grad * grad, axis=1, keepdims=True))


def update_kernel(columns, table_ref, grad_ref, accum_ref, mine_ref, other_ref, table_out, accum_out):
    accum = accum_ref[...] + (mine_ref[...] + other_ref[...]) / columns
    accum_out[...] = accum
    inverse = lax.rsqrt(accum)
    for block in range(accum.shape[0]):
        span = slice(block * LANES, (block + 1) * LANES)
        scale = row_to_column(inverse[block : block + 1, :])
        table_out[span, :] = table_ref[span, :] - LEARNING_RATE * grad_ref[span, :] * scale


def shift(array, axis, by):
    size = lax.axis_size(axis)
    return lax.ppermute(array, axis, [(i, (i + by) % size) for i in range(size)])


LIMITS = {serve_kernel: 60, index_kernel: 60, first_kernel: 60, hidden_kernel: 60, slot_kernel: 50}
COSTS = {update_kernel: 0, group_kernel: 0, row_kernel: 0}


def body(
    table,
    accum,
    serve_rows,
    seed_slot,
    hop1_slot,
    hop2_slot,
    hop1_rel,
    hop2_rel,
    cotangent,
    w_first,
    w_second,
):
    everyone = ("dp", "y", "z")
    owners = lax.axis_size(everyone)
    table_rows, columns = table.shape
    slots = serve_rows.shape[1]
    seeds, fanout = hop1_slot.shape
    fanout_two = hop2_slot.shape[2]
    nodes = seeds + seeds * fanout
    layers, hidden_units = w_second.shape[:2]
    half = hidden_units // 2
    n_x, n_y, n_z = (lax.axis_size(a) for a in everyone)
    x, y = lax.axis_index("dp"), lax.axis_index("y")
    width = hidden_units // n_x

    blocks_shape = (owners, slots // owners, columns)
    outgoing = call(
        serve_kernel, [shaped(blocks_shape, BF16)], (serve_rows, table), scratch=[pltpu.VMEM((slots, table_rows), BF16)], hbm_in=(0, 1)
    )[0]
    fetched = lax.all_to_all(outgoing, everyone, split_axis=0, concat_axis=0, tiled=True)

    key_one = hop1_slot + slots * hop1_rel
    key_two = (hop2_slot + slots * hop2_rel).reshape(seeds * fanout, fanout_two)
    seed_ids = jnp.arange(seeds, dtype=jnp.int32)[:, None]
    group = (seeds * (1 + hop1_rel) + seed_ids).reshape(-1, 1)
    spare = jnp.full((seeds * fanout, fanout - fanout_two), -1, jnp.int32)
    idx = jnp.concatenate(
        [
            jnp.concatenate([seed_slot[:, None], key_one, seed_ids], 1),
            jnp.concatenate([hop1_slot.reshape(-1, 1), key_two, spare, group], 1),
        ],
        0,
    )
    ct, c, inverse, member, back_hidden = call(
        index_kernel,
        [
            shaped((layers * nodes, slots), BF16),
            shaped((slots, layers * nodes), BF16),
            shaped((layers * nodes, LANES), F32),
            shaped((SEED_ROWS, nodes), BF16),
            shaped((nodes, hidden_units), F32),
        ],
        (idx, cotangent, w_second),
        scratch=[pltpu.VMEM((LANES, hidden_units), F32)],
        hbm_out=range(5),
    )

    layer_in, partial_pre = call(
        first_kernel,
        [shaped((layers * nodes, columns), BF16), shaped((nodes, hidden_units), F32)],
        (fetched, ct, w_first),
        hbm_in=(0, 1, 2),
        hbm_out=(0, 1),
    )
    other_pre = shift(partial_pre, "col", 1)
    layer_parts = [layer_in] + [shift(layer_in, "dp", d) for d in range(1, n_x) if d != n_x // 2]

    pack_rows = nodes + half // width * SEED_ROWS + COT_ROWS
    pack_shape = (pack_rows, width)
    far = n_x // 2
    far_shape = ((pack_rows * width + layers * nodes * columns) // LANES, LANES)
    back, *packs = call(
        hidden_kernel,
        [shaped((nodes, hidden_units), BF16)] + [shaped(far_shape if d == far else pack_shape, BF16) for d in range(n_x)],
        (
            jnp.stack([lax.axis_index("col"), x]),
            partial_pre,
            other_pre,
            back_hidden,
            member,
            inverse,
            cotangent,
            layer_in,
        ),
        smem=1,
        scratch=[pltpu.VMEM((n_x, *pack_shape), BF16), pltpu.SemaphoreType.DMA((n_x - 1 + (width + columns) // LANES,))],
        hbm_in=(1, 2, 3, 4, 5, 7),
        hbm_raw=range(1, 1 + n_x),
    )
    packs = [packs[0]] + [shift(packs[d], "dp", d) for d in range(1, n_x)]
    back, *layer_parts[1:] = lax.optimization_barrier((back, *layer_parts[1:]))
    slot_grad = call(slot_kernel, [shaped(blocks_shape, BF16)], (back, inverse, c, w_first), hbm_in=(1, 2, 3))[0]
    arrived = lax.all_to_all(slot_grad, everyone, split_axis=0, concat_axis=0, tiled=True)

    block_rows = width // n_y
    group_rows = layers * block_rows + (layers * half // columns + 1) * n_x * seeds
    own, *blocks = call(
        functools.partial(weight_kernel, n_x),
        [shaped((block_rows, layers * columns), F32)] + [shaped((group_rows, columns), BF16)] * n_y,
        (y.reshape(1), *layer_parts, *packs),
        smem=1,
        hbm_in=range(1, n_x),
        scratch=[pltpu.VMEM((layers, width, columns), F32)],
    )
    blocks = [blocks[0]] + [shift(blocks[d], "y", d) for d in range(1, n_y)]
    grad_columns = layers * (columns + half)
    grads = call(
        functools.partial(group_kernel, layers),
        [shaped((block_rows, grad_columns), BF16)],
        (own, *blocks),
    )[0]
    grads = grads.reshape(n_z, block_rows // n_z, grad_columns)
    grads = lax.all_to_all(grads, "z", split_axis=0, concat_axis=0, tiled=True)
    grad_one, grad_two = call(
        sum_kernel,
        [shaped((layers, block_rows // n_z, wide), F32) for wide in (columns, half)],
        (grads,),
    )
    grad_one, grad_two = grad_one.transpose(0, 2, 1), grad_two.transpose(0, 2, 1)

    row_grad, squares = call(
        row_kernel,
        [shaped((table_rows, columns), F32), shaped((table_rows // LANES, LANES), F32)],
        (serve_rows, arrived),
    )
    other_squares = shift(squares, "col", 1)
    new_table, new_accum = call(
        functools.partial(update_kernel, 2 * columns),
        [shaped((table_rows, columns), F32), shaped((table_rows // LANES, LANES), F32)],
        (table, row_grad, accum.reshape(-1, LANES), squares, other_squares),
    )
    return (new_table, new_accum.reshape(-1), grad_one, grad_two)


def solution(mesh):
    n_dp, n_table, n_col = (mesh.shape[a] for a in ("dp", "table", "col"))
    n_y = 4 if n_table % 4 == 0 and n_table > 4 else 2
    fine = Mesh(mesh.devices.reshape(n_dp, n_y, n_table // n_y, n_col), ("dp", "y", "z", "col"))
    rows = ("dp", "y", "z")
    placed = (
        P(rows, "col"),
        P(rows),
        P(rows, None),
        P(rows),
        P(rows, None),
        P(rows, None, None),
        P(rows, None),
        P(rows, None, None),
        P(rows, None),
        P(None, "col", None),
        P(),
    )
    return jax.shard_map(
        body,
        mesh=fine,
        in_specs=placed,
        out_specs=(P(rows, "col"), P(rows), P(None, "col", rows), P(None, "col", rows)),
        check_vma=False,
    )
```

```python
import functools
import jax
import jax.numpy as jnp
from jax import lax
from jax.experimental import pallas as pl
from jax.experimental.pallas import tpu as pltpu
from jax.sharding import Mesh
from jax.sharding import PartitionSpec as P

LEARNING_RATE = 0.1
BF16 = jnp.bfloat16
F32 = jnp.float32
LANES = 128
SEED_ROWS = 32
COT_ROWS = 16


def matmul(a, b, contract=(1, 0)):
    dims = (((contract[0],), (contract[1],)), ((), ()))
    return lax.dot_general(a, b, dims, preferred_element_type=F32)


def row_to_column(row):
    return jnp.transpose(jnp.broadcast_to(row, (LANES, LANES)))[:, 0:1]


def column_to_row(column):
    return jnp.transpose(jnp.broadcast_to(column, (LANES, LANES)))[0:1, :]


class Incoming:
    def __init__(self, source, buffer, semaphore):
        self.buffer, self.waiting = buffer, True
        self.shape = buffer.shape
        self.copy = pltpu.make_async_copy(source, buffer, semaphore)
        self.copy.start()

    def get(self):
        if self.waiting:
            self.copy.wait()
        self.waiting = False
        return self.buffer


class Outgoing:
    def __init__(self, target, buffer, semaphore):
        self.buffer = buffer
        self.copy = pltpu.make_async_copy(buffer, target, semaphore)

    def send(self):
        self.copy.start()


def call(kernel, outs, operands, smem=0, scratch=(), hbm_in=(), hbm_out=(), hbm_raw=()):
    name = getattr(kernel, "func", kernel)
    limit, flops = LIMITS.get(name, 12), COSTS.get(name, 10**12)
    moved = sum(o.size * o.dtype.itemsize for o in list(operands) + list(outs))
    specs = [
        pl.BlockSpec(memory_space=pltpu.SMEM if i < smem else pltpu.HBM if i in hbm_in else pltpu.VMEM)
        for i in range(len(operands))
    ]
    made = [
        pl.BlockSpec(memory_space=pltpu.HBM if i in hbm_out or i in hbm_raw else pltpu.VMEM)
        for i in range(len(outs))
    ]
    buffers = [pltpu.VMEM(operands[i].shape, operands[i].dtype) for i in hbm_in]
    buffers += [pltpu.VMEM(outs[i].shape, outs[i].dtype) for i in hbm_out]
    semaphores = [pltpu.SemaphoreType.DMA((len(buffers),))] if buffers else []

    def wrapped(*refs):
        refs = list(refs)
        if not buffers:
            kernel(*refs)
            return
        first = len(operands) + len(outs)
        held, sems = refs[first : first + len(buffers)], refs[first + len(buffers)]
        rest = refs[first + len(buffers) + 1 :]
        for j, i in enumerate(hbm_in):
            refs[i] = Incoming(refs[i], held[j], sems.at[j])
        leaving = []
        for j, i in enumerate(hbm_out, len(hbm_in)):
            place = len(operands) + i
            refs[place] = Outgoing(refs[place], held[j], sems.at[j])
            leaving.append(refs[place])
        kernel(*refs[:first], *rest)
        for out in leaving:
            out.copy.wait()

    return pl.pallas_call(
        wrapped,
        out_shape=tuple(outs),
        in_specs=specs,
        out_specs=tuple(made),
        scratch_shapes=buffers + semaphores + list(scratch),
        compiler_params=pltpu.CompilerParams(vmem_limit_bytes=limit * 1024 * 1024),
        cost_estimate=pl.CostEstimate(flops=flops, bytes_accessed=moved, transcendentals=0),
    )(*operands)


def shaped(shape, dtype):
    return jax.ShapeDtypeStruct(shape, dtype)


def serve_kernel(serve_ref, table_ref, out_ref, onehot):
    serve = serve_ref.get()[...]
    lanes = lax.broadcasted_iota(jnp.int32, (LANES, onehot.shape[1]), 1)
    for block in range(serve.shape[1] // LANES):
        span = slice(block * LANES, (block + 1) * LANES)
        onehot[span, :] = jnp.where(row_to_column(serve[:, span]) == lanes, 1.0, 0.0).astype(BF16)
    rows = table_ref.get()[...].astype(BF16)
    out_ref[...] = matmul(onehot[...], rows).astype(BF16).reshape(out_ref.shape)


def index_kernel(idx_ref, cot_ref, w2_ref, *refs):
    outs, spread = refs[:-1], refs[-1]
    ct_ref, c_ref, inv_ref, e_ref, back_ref = (o.buffer for o in outs)
    nodes = idx_ref.shape[0]
    slots = ct_ref.shape[1]
    seeds = cot_ref.shape[0]
    neighbours = idx_ref.shape[1] - 2
    lanes = lax.broadcasted_iota(jnp.int32, (nodes, 2 * slots), 1)
    idx = idx_ref[...]
    counts = jnp.zeros((nodes, 2 * slots), F32)
    for j in range(1, 1 + neighbours):
        counts = counts + jnp.where(idx[:, j : j + 1] == lanes, 1.0, 0.0)
    own = jnp.where(idx[:, 0:1] == lanes[:, :slots], 1.0, 0.0)
    parts = (own, counts[:, :slots], counts[:, slots:])
    spread[...] = jnp.zeros(spread.shape, F32)
    for k, part in enumerate(parts):
        span = slice(k * nodes, (k + 1) * nodes)
        ct_ref[span, :] = part.astype(BF16)
        c_ref[:, span] = jnp.transpose(part).astype(BF16)
        if k == 0:
            inverse = jnp.ones((nodes, 1), F32)
        else:
            inverse = 1.0 / jnp.maximum(jnp.sum(part, axis=1, keepdims=True), 1.0)
        inv_ref[span, :] = jnp.broadcast_to(inverse, (nodes, LANES))
        back = matmul(cot_ref[...], w2_ref[k], (1, 1))
        spread[k * seeds : (k + 1) * seeds, :] = back * inverse[:seeds]
    groups = lax.broadcasted_iota(jnp.int32, (nodes, LANES), 1)
    member = jnp.where(idx[:, neighbours + 1 : neighbours + 2] == groups, 1.0, 0.0)
    e_ref[...] = jnp.transpose(member)[:SEED_ROWS].astype(BF16)
    whole = spread[...]
    high = whole.astype(BF16)
    low = (whole - high.astype(F32)).astype(BF16)
    for out in outs[:-1]:
        out.send()
    back_ref[...] = matmul(member.astype(BF16), high) + matmul(member.astype(BF16), low)
    outs[-1].send()


def first_kernel(fetched_ref, ct_ref, w1_ref, layer_ref, partial_ref):
    layers = w1_ref.shape[0]
    layer_out, partial_out = layer_ref, partial_ref
    layer_ref, partial_ref = layer_ref.buffer, partial_ref.buffer
    nodes = partial_ref.shape[0]
    fetched = fetched_ref.get()[...].reshape(ct_ref.shape[1], layer_ref.shape[1])
    total = None
    ct_ref = ct_ref.get()
    ones = jnp.ones((ct_ref.shape[1], LANES), BF16)
    for k in range(layers):
        span = slice(k * nodes, (k + 1) * nodes)
        summed = matmul(ct_ref[span, :], fetched)
        inverse = 1.0 / jnp.maximum(matmul(ct_ref[span, :], ones)[:, 0:1], 1.0)
        layer_ref[span, :] = (summed * inverse).astype(BF16)
    layer_out.send()
    for k in range(layers):
        term = matmul(layer_ref[k * nodes : (k + 1) * nodes, :], w1_ref.get()[k])
        total = term if total is None else total + term
    partial_ref[...] = total
    partial_out.send()


def hidden_kernel(place_ref, mine_ref, other_ref, back_ref, e_ref, inv_ref, cot_ref, layer_ref, out_ref, *refs):
    packs, stage, sems = refs[:-2], refs[-2], refs[-1]
    nodes = mine_ref.shape[0]
    width = stage.shape[2]
    seeds = cot_ref.shape[0]
    layers = inv_ref.shape[0] // nodes
    values = mine_ref.get()[...] + other_ref.get()[...]
    back_ref, e_ref, inv_ref = back_ref.get(), e_ref.get(), inv_ref.get()
    sigma = jax.nn.sigmoid(values)
    hidden = (values * sigma).astype(BF16)
    slope = sigma * (1.0 + values * (1.0 - sigma))
    back = (back_ref[...] * slope).astype(BF16)
    out_ref[...] = back
    scale = jnp.concatenate(
        [inv_ref[k * nodes : k * nodes + seeds, 0:1] for k in range(layers)]
        + [jnp.zeros((SEED_ROWS - layers * seeds, 1), F32)],
        0,
    )
    second = matmul(e_ref[...], hidden) * scale
    half = second.shape[1] // 2
    second = jnp.where(place_ref[0] == 0, second[:, :half], second[:, half:]).astype(BF16)
    cot = cot_ref[...].astype(F32)
    cot = jnp.concatenate([cot, jnp.zeros((COT_ROWS - seeds, cot.shape[1]), F32)], 0).astype(BF16)
    for j in range(len(packs)):
        span = slice(j * width, (j + 1) * width)
        stage[j, :nodes, :] = back[:, span]
        for part in range(half // width):
            first = nodes + part * SEED_ROWS
            stage[j, first : first + SEED_ROWS, :] = second[:, part * width : (part + 1) * width]
        first = nodes + half // width * SEED_ROWS
        stage[j, first : first + COT_ROWS, :] = cot[:, span]
    moves = []
    for d, pack in enumerate(packs):
        chosen = stage.at[lax.rem(place_ref[1] + d, len(packs))]
        if d != len(packs) // 2:
            moves.append((chosen, pack))
            continue
        start = 0
        for source in (chosen, layer_ref.get()):
            rows, wide = source.shape
            for lane in range(0, wide, LANES):
                moves.append((source.at[:, lane : lane + LANES], pack.at[start : start + rows, :]))
                start += rows
    copies = [pltpu.make_async_copy(source, target, sems.at[i]) for i, (source, target) in enumerate(moves)]
    for copy in copies:
        copy.start()
    for copy in copies:
        copy.wait()


def slot_kernel(back_ref, inv_ref, c_ref, w1_ref, slot_ref):
    nodes = back_ref.shape[0]
    total = None
    for k in range(w1_ref.shape[0]):
        span = slice(k * nodes, (k + 1) * nodes)
        back_in = matmul(back_ref[...], w1_ref.get()[k], (1, 1)) * inv_ref.get()[span, 0:1]
        term = matmul(c_ref.get()[:, span], back_in.astype(BF16))
        total = term if total is None else total + term
    slot_ref[...] = total.astype(BF16).reshape(slot_ref.shape)


def weight_kernel(count, place_ref, *refs):
    layer_refs, pack_refs = list(refs[: count - 1]), list(refs[count - 1 : 2 * count - 1])
    own_ref, outs, total = refs[2 * count - 1], refs[2 * count : -1], refs[-1]
    pack_rows, width = pack_refs[0].shape
    layer_rows, columns = layer_refs[0].shape
    layer_parts = [r.get()[...] for r in layer_refs]
    far = pack_refs[count // 2][...]
    parts, start = [], 0
    for rows, wide in ((pack_rows, width), (layer_rows, columns)):
        lanes = [far[start + i * rows : start + (i + 1) * rows] for i in range(wide // LANES)]
        parts.append(jnp.concatenate(lanes, 1))
        start += rows * len(lanes)
    layer_parts.insert(count // 2, parts[1])
    packs = [parts[0] if d == count // 2 else ref[...] for d, ref in enumerate(pack_refs)]
    nodes = LANES
    relations = layer_rows // nodes
    rows = own_ref.shape[0]
    left = jnp.concatenate([p[:nodes, :] for p in packs], 0)
    for k in range(relations):
        right = jnp.concatenate([r[k * nodes : (k + 1) * nodes, :] for r in layer_parts], 0)
        total[k] = matmul(left, right, (0, 0))
    pieces = (pack_rows - nodes - COT_ROWS) // SEED_ROWS
    half = pieces * width
    seeds = SEED_ROWS // (relations + 1)
    first = nodes + pieces * SEED_ROWS
    cots = jnp.concatenate([p[first : first + COT_ROWS, :].astype(F32)[:seeds] for p in packs], 0)
    seconds = [
        jnp.concatenate(
            [p[nodes + part * SEED_ROWS : nodes + (part + 1) * SEED_ROWS, :].astype(F32) for part in range(pieces)],
            1,
        )
        for p in packs
    ]
    second = jnp.concatenate(
        [jnp.concatenate([s[k * seeds : (k + 1) * seeds] for s in seconds], 0) for k in range(relations)], 1
    ).astype(BF16)
    group = count * seeds
    tail = relations * rows
    for d, out in enumerate(outs):
        target = lax.rem(place_ref[0] + d, len(outs))
        start = pl.multiple_of(target * rows, rows)
        for k in range(relations):
            block = total[k, pl.ds(start, rows), :]
            if d == 0:
                own_ref[:, k * columns : (k + 1) * columns] = block
            else:
                out[k * rows : (k + 1) * rows, :] = block.astype(BF16)
        for piece in range(relations * half // columns):
            out[tail + piece * group : tail + (piece + 1) * group, :] = second[
                :, piece * columns : (piece + 1) * columns
            ]
        chosen = cots[:, :rows]
        for j in range(1, len(outs)):
            chosen = jnp.where(target == j, cots[:, j * rows : (j + 1) * rows], chosen)
        chosen = jnp.concatenate([chosen, jnp.zeros((group, columns - rows), F32)], 1)
        out[out.shape[0] - group :, :] = chosen.astype(BF16)


def group_kernel(relations, count, place_ref, own_ref, *refs):
    packs, outs, out_ref = refs[:count], refs[count:-1], refs[-1]
    rows = own_ref.shape[0]
    columns = packs[0].shape[1]
    tail = relations * rows
    wide = out_ref.shape[1] - relations * columns
    pieces = wide // columns
    group = (packs[0].shape[0] - tail) // (pieces + 1)
    for k in range(relations):
        span = slice(k * columns, (k + 1) * columns)
        block = own_ref[:, span]
        for pack in packs[1:]:
            block = block + pack[k * rows : (k + 1) * rows, :].astype(F32)
        out_ref[:, span] = block
    cots = jnp.concatenate([p[tail + pieces * group :, :] for p in packs], 0)
    for piece in range(pieces):
        first = tail + piece * group
        second = jnp.concatenate([p[first : first + group, :] for p in packs], 0)
        start = (relations + piece) * columns
        out_ref[:, start : start + columns] = matmul(cots, second, (0, 0))[:rows]
    part = outs[0].shape[0]
    for d, out in enumerate(outs):
        start = pl.multiple_of(lax.rem(place_ref[0] + d, len(outs)) * part, part)
        out[...] = out_ref[pl.ds(start, part), :].astype(out.dtype)


def sum_kernel(*refs):
    parts, (one_ref, two_ref) = refs[:-2], refs[-2:]
    total = parts[0][...]
    for part in parts[1:]:
        total = total + part[...].astype(F32)
    start = 0
    for ref in (one_ref, two_ref):
        wide = ref.shape[2]
        for k in range(ref.shape[0]):
            ref[k] = total[:, start : start + wide]
            start += wide


def row_kernel(serve_ref, arrived_ref, grad_ref, square_ref):
    rows = lax.broadcasted_iota(jnp.int32, (LANES, serve_ref.shape[1]), 0)
    arrived = arrived_ref[...].reshape(serve_ref.shape[1], grad_ref.shape[1])
    for block in range(grad_ref.shape[0] // LANES):
        span = slice(block * LANES, (block + 1) * LANES)
        onehot = jnp.where(serve_ref[...] == rows + block * LANES, 1.0, 0.0).astype(BF16)
        grad = matmul(onehot, arrived)
        grad_ref[span, :] = grad
        square_ref[block : block + 1, :] = column_to_row(jnp.sum(grad * grad, axis=1, keepdims=True))


def update_kernel(columns, table_ref, grad_ref, accum_ref, mine_ref, other_ref, table_out, accum_out):
    accum = accum_ref[...] + (mine_ref[...] + other_ref[...]) / columns
    accum_out[...] = accum
    inverse = lax.rsqrt(accum)
    for block in range(accum.shape[0]):
        span = slice(block * LANES, (block + 1) * LANES)
        scale = row_to_column(inverse[block : block + 1, :])
        table_out[span, :] = table_ref[span, :] - LEARNING_RATE * grad_ref[span, :] * scale


def shift(array, axis, by):
    size = lax.axis_size(axis)
    return lax.ppermute(array, axis, [(i, (i + by) % size) for i in range(size)])


LIMITS = {serve_kernel: 60, index_kernel: 60, first_kernel: 60, hidden_kernel: 60, slot_kernel: 60}
COSTS = {update_kernel: 0, row_kernel: 0}


def body(
    table,
    accum,
    serve_rows,
    seed_slot,
    hop1_slot,
    hop2_slot,
    hop1_rel,
    hop2_rel,
    cotangent,
    w_first,
    w_second,
):
    everyone = ("dp", "y", "z")
    owners = lax.axis_size(everyone)
    table_rows, columns = table.shape
    slots = serve_rows.shape[1]
    seeds, fanout = hop1_slot.shape
    fanout_two = hop2_slot.shape[2]
    nodes = seeds + seeds * fanout
    layers, hidden_units = w_second.shape[:2]
    half = hidden_units // 2
    n_x, n_y, n_z = (lax.axis_size(a) for a in everyone)
    x, y, z = (lax.axis_index(a) for a in everyone)
    width = hidden_units // n_x

    blocks_shape = (owners, slots // owners, columns)
    outgoing = call(
        serve_kernel, [shaped(blocks_shape, BF16)], (serve_rows, table), scratch=[pltpu.VMEM((slots, table_rows), BF16)], hbm_in=(0, 1)
    )[0]
    fetched = lax.all_to_all(outgoing, everyone, split_axis=0, concat_axis=0, tiled=True)

    key_one = hop1_slot + slots * hop1_rel
    key_two = (hop2_slot + slots * hop2_rel).reshape(seeds * fanout, fanout_two)
    seed_ids = jnp.arange(seeds, dtype=jnp.int32)[:, None]
    group = (seeds * (1 + hop1_rel) + seed_ids).reshape(-1, 1)
    spare = jnp.full((seeds * fanout, fanout - fanout_two), -1, jnp.int32)
    idx = jnp.concatenate(
        [
            jnp.concatenate([seed_slot[:, None], key_one, seed_ids], 1),
            jnp.concatenate([hop1_slot.reshape(-1, 1), key_two, spare, group], 1),
        ],
        0,
    )
    idx, place, y, z = lax.optimization_barrier((idx, jnp.stack([lax.axis_index("col"), x]), y, z))
    ct, c, inverse, member, back_hidden = call(
        index_kernel,
        [
            shaped((layers * nodes, slots), BF16),
            shaped((slots, layers * nodes), BF16),
            shaped((layers * nodes, LANES), F32),
            shaped((SEED_ROWS, nodes), BF16),
            shaped((nodes, hidden_units), F32),
        ],
        (idx, cotangent, w_second),
        scratch=[pltpu.VMEM((LANES, hidden_units), F32)],
        hbm_out=range(5),
    )

    layer_in, partial_pre = call(
        first_kernel,
        [shaped((layers * nodes, columns), BF16), shaped((nodes, hidden_units), F32)],
        (fetched, ct, w_first),
        hbm_in=(0, 1, 2),
        hbm_out=(0, 1),
    )
    other_pre = shift(partial_pre, "col", 1)
    layer_parts = [layer_in] + [shift(layer_in, "dp", d) for d in range(1, n_x) if d != n_x // 2]

    pack_rows = nodes + half // width * SEED_ROWS + COT_ROWS
    pack_shape = (pack_rows, width)
    far = n_x // 2
    far_shape = ((pack_rows * width + layers * nodes * columns) // LANES, LANES)
    back, *packs = call(
        hidden_kernel,
        [shaped((nodes, hidden_units), BF16)] + [shaped(far_shape if d == far else pack_shape, BF16) for d in range(n_x)],
        (
            place,
            partial_pre,
            other_pre,
            back_hidden,
            member,
            inverse,
            cotangent,
            layer_in,
        ),
        smem=1,
        scratch=[pltpu.VMEM((n_x, *pack_shape), BF16), pltpu.SemaphoreType.DMA((n_x - 1 + (width + columns) // LANES,))],
        hbm_in=(1, 2, 3, 4, 5, 7),
        hbm_raw=range(1, 1 + n_x),
    )
    packs, layer_parts = lax.optimization_barrier((packs, layer_parts))
    packs = [packs[0]] + [shift(packs[d], "dp", d) for d in range(1, n_x)]
    block_rows = width // n_y
    group_rows = layers * block_rows + (layers * half // columns + 1) * n_x * seeds
    own, *blocks = call(
        functools.partial(weight_kernel, n_x),
        [shaped((block_rows, layers * columns), F32)] + [shaped((group_rows, columns), BF16)] * n_y,
        (y.reshape(1), *layer_parts, *packs),
        smem=1,
        hbm_in=range(1, n_x),
        scratch=[pltpu.VMEM((layers, width, columns), F32)],
    )
    back, own = lax.optimization_barrier((back, own))
    slot_grad = call(slot_kernel, [shaped(blocks_shape, BF16)], (back, inverse, c, w_first), hbm_in=(1, 2, 3))[0]
    arrived = lax.all_to_all(slot_grad, everyone, split_axis=0, concat_axis=0, tiled=True)

    blocks = [blocks[0]] + [shift(blocks[d], "y", d) for d in range(1, n_y)]
    grad_columns = layers * (columns + half)
    rows = block_rows // n_z
    own, *parts = call(
        functools.partial(group_kernel, layers, n_y),
        [shaped((rows, grad_columns), F32 if d == 0 else BF16) for d in range(n_z)],
        (z.reshape(1), own, *blocks),
        smem=1,
        scratch=[pltpu.VMEM((block_rows, grad_columns), F32)],
    )
    parts = [shift(part, "z", d) for d, part in enumerate(parts, 1)]
    grad_one, grad_two = call(
        sum_kernel, [shaped((layers, rows, wide), F32) for wide in (columns, half)], (own, *parts)
    )
    grad_one, grad_two = grad_one.transpose(0, 2, 1), grad_two.transpose(0, 2, 1)

    row_grad, squares = call(
        row_kernel,
        [shaped((table_rows, columns), F32), shaped((table_rows // LANES, LANES), F32)],
        (serve_rows, arrived),
    )
    other_squares = shift(squares, "col", 1)
    new_table, new_accum = call(
        functools.partial(update_kernel, 2 * columns),
        [shaped((table_rows, columns), F32), shaped((table_rows // LANES, LANES), F32)],
        (table, row_grad, accum.reshape(-1, LANES), squares, other_squares),
    )
    return (new_table, new_accum.reshape(-1), grad_one, grad_two)


def solution(mesh):
    n_dp, n_table, n_col = (mesh.shape[a] for a in ("dp", "table", "col"))
    n_y = 4 if n_table % 4 == 0 and n_table > 4 else 2
    fine = Mesh(mesh.devices.reshape(n_dp, n_y, n_table // n_y, n_col), ("dp", "y", "z", "col"))
    rows = ("dp", "y", "z")
    placed = (
        P(rows, "col"),
        P(rows),
        P(rows, None),
        P(rows),
        P(rows, None),
        P(rows, None, None),
        P(rows, None),
        P(rows, None, None),
        P(rows, None),
        P(None, "col", None),
        P(),
    )
    return jax.shard_map(
        body,
        mesh=fine,
        in_specs=placed,
        out_specs=(P(rows, "col"), P(rows), P(None, "col", rows), P(None, "col", rows)),
        check_vma=False,
    )
```

```python
import functools
import jax
import jax.numpy as jnp
from jax import lax
from jax.experimental import pallas as pl
from jax.experimental.pallas import tpu as pltpu
from jax.sharding import Mesh
from jax.sharding import PartitionSpec as P

LEARNING_RATE = 0.1
BF16 = jnp.bfloat16
F32 = jnp.float32
LANES = 128
SEED_ROWS = 32
COT_ROWS = 16


def matmul(a, b, contract=(1, 0)):
    dims = (((contract[0],), (contract[1],)), ((), ()))
    return lax.dot_general(a, b, dims, preferred_element_type=F32)


def row_to_column(row):
    return jnp.transpose(jnp.broadcast_to(row, (LANES, LANES)))[:, 0:1]


def column_to_row(column):
    return jnp.transpose(jnp.broadcast_to(column, (LANES, LANES)))[0:1, :]


class Incoming:
    def __init__(self, source, buffer, semaphore):
        self.buffer, self.waiting = buffer, True
        self.shape = buffer.shape
        self.copy = pltpu.make_async_copy(source, buffer, semaphore)
        self.copy.start()

    def get(self):
        if self.waiting:
            self.copy.wait()
        self.waiting = False
        return self.buffer


class Outgoing:
    def __init__(self, target, buffer, semaphore):
        self.buffer = buffer
        self.copy = pltpu.make_async_copy(buffer, target, semaphore)

    def send(self):
        self.copy.start()


def call(kernel, outs, operands, smem=0, scratch=(), hbm_in=(), hbm_out=(), hbm_raw=()):
    name = getattr(kernel, "func", kernel)
    limit, flops = LIMITS.get(name, 12), COSTS.get(name, 10**12)
    moved = sum(o.size * o.dtype.itemsize for o in list(operands) + list(outs))
    specs = [
        pl.BlockSpec(memory_space=pltpu.SMEM if i < smem else pltpu.HBM if i in hbm_in else pltpu.VMEM)
        for i in range(len(operands))
    ]
    made = [
        pl.BlockSpec(memory_space=pltpu.HBM if i in hbm_out or i in hbm_raw else pltpu.VMEM)
        for i in range(len(outs))
    ]
    buffers = [pltpu.VMEM(operands[i].shape, operands[i].dtype) for i in hbm_in]
    buffers += [pltpu.VMEM(outs[i].shape, outs[i].dtype) for i in hbm_out]
    semaphores = [pltpu.SemaphoreType.DMA((len(buffers),))] if buffers else []

    def wrapped(*refs):
        refs = list(refs)
        if not buffers:
            kernel(*refs)
            return
        first = len(operands) + len(outs)
        held, sems = refs[first : first + len(buffers)], refs[first + len(buffers)]
        rest = refs[first + len(buffers) + 1 :]
        for j, i in enumerate(hbm_in):
            refs[i] = Incoming(refs[i], held[j], sems.at[j])
        leaving = []
        for j, i in enumerate(hbm_out, len(hbm_in)):
            place = len(operands) + i
            refs[place] = Outgoing(refs[place], held[j], sems.at[j])
            leaving.append(refs[place])
        kernel(*refs[:first], *rest)
        for out in leaving:
            out.copy.wait()

    return pl.pallas_call(
        wrapped,
        out_shape=tuple(outs),
        in_specs=specs,
        out_specs=tuple(made),
        scratch_shapes=buffers + semaphores + list(scratch),
        compiler_params=pltpu.CompilerParams(vmem_limit_bytes=limit * 1024 * 1024),
        cost_estimate=pl.CostEstimate(flops=flops, bytes_accessed=moved, transcendentals=0),
    )(*operands)


def is_near(distance, count):
    return distance not in (0, count // 2)


def shaped(shape, dtype):
    return jax.ShapeDtypeStruct(shape, dtype)


def serve_kernel(serve_ref, table_ref, out_ref, onehot):
    serve = serve_ref.get()[...]
    lanes = lax.broadcasted_iota(jnp.int32, (LANES, onehot.shape[1]), 1)
    for block in range(serve.shape[1] // LANES):
        span = slice(block * LANES, (block + 1) * LANES)
        onehot[span, :] = jnp.where(row_to_column(serve[:, span]) == lanes, 1.0, 0.0).astype(BF16)
    rows = table_ref.get()[...].astype(BF16)
    out_ref[...] = matmul(onehot[...], rows).astype(BF16).reshape(out_ref.shape)


def index_kernel(idx_ref, cot_ref, w2_ref, *refs):
    outs, spread = refs[:-1], refs[-1]
    ct_ref, c_ref, inv_ref, e_ref, back_ref = (o.buffer for o in outs)
    nodes = idx_ref.shape[0]
    slots = ct_ref.shape[1]
    seeds = cot_ref.shape[0]
    neighbours = idx_ref.shape[1] - 2
    lanes = lax.broadcasted_iota(jnp.int32, (nodes, 2 * slots), 1)
    idx = idx_ref[...]
    counts = jnp.zeros((nodes, 2 * slots), F32)
    for j in range(1, 1 + neighbours):
        counts = counts + jnp.where(idx[:, j : j + 1] == lanes, 1.0, 0.0)
    own = jnp.where(idx[:, 0:1] == lanes[:, :slots], 1.0, 0.0)
    parts = (own, counts[:, :slots], counts[:, slots:])
    spread[...] = jnp.zeros(spread.shape, F32)
    for k, part in enumerate(parts):
        span = slice(k * nodes, (k + 1) * nodes)
        ct_ref[span, :] = part.astype(BF16)
        c_ref[:, span] = jnp.transpose(part).astype(BF16)
        if k == 0:
            inverse = jnp.ones((nodes, 1), F32)
        else:
            inverse = 1.0 / jnp.maximum(jnp.sum(part, axis=1, keepdims=True), 1.0)
        inv_ref[span, :] = jnp.broadcast_to(inverse, (nodes, LANES))
        back = matmul(cot_ref[...], w2_ref[k], (1, 1))
        spread[k * seeds : (k + 1) * seeds, :] = back * inverse[:seeds]
    groups = lax.broadcasted_iota(jnp.int32, (nodes, LANES), 1)
    member = jnp.where(idx[:, neighbours + 1 : neighbours + 2] == groups, 1.0, 0.0)
    e_ref[...] = jnp.transpose(member)[:SEED_ROWS].astype(BF16)
    whole = spread[...]
    high = whole.astype(BF16)
    low = (whole - high.astype(F32)).astype(BF16)
    for out in outs[:-1]:
        out.send()
    back_ref[...] = matmul(member.astype(BF16), high) + matmul(member.astype(BF16), low)
    outs[-1].send()


def first_kernel(fetched_ref, ct_ref, w1_ref, layer_ref, partial_ref):
    layers = w1_ref.shape[0]
    layer_out, partial_out = layer_ref, partial_ref
    layer_ref, partial_ref = layer_ref.buffer, partial_ref.buffer
    nodes = partial_ref.shape[0]
    fetched = fetched_ref.get()[...].reshape(ct_ref.shape[1], layer_ref.shape[1])
    total = None
    ct_ref = ct_ref.get()
    ones = jnp.ones((ct_ref.shape[1], LANES), BF16)
    for k in range(layers):
        span = slice(k * nodes, (k + 1) * nodes)
        summed = matmul(ct_ref[span, :], fetched)
        inverse = 1.0 / jnp.maximum(matmul(ct_ref[span, :], ones)[:, 0:1], 1.0)
        layer_ref[span, :] = (summed * inverse).astype(BF16)
    layer_out.send()
    for k in range(layers):
        term = matmul(layer_ref[k * nodes : (k + 1) * nodes, :], w1_ref.get()[k])
        total = term if total is None else total + term
    partial_ref[...] = total
    partial_out.send()


def hidden_kernel(place_ref, mine_ref, other_ref, back_ref, e_ref, inv_ref, cot_ref, c_ref, w1_ref, layer_ref, slot_ref, *refs):
    packs, stage, sems = refs[:-2], refs[-2], refs[-1]
    nodes = mine_ref.shape[0]
    width = stage.shape[2]
    seeds = cot_ref.shape[0]
    layers = inv_ref.shape[0] // nodes
    values = mine_ref.get()[...] + other_ref.get()[...]
    back_ref, e_ref, inv_ref = back_ref.get(), e_ref.get(), inv_ref.get()
    sigma = jax.nn.sigmoid(values)
    hidden = (values * sigma).astype(BF16)
    slope = sigma * (1.0 + values * (1.0 - sigma))
    back = (back_ref[...] * slope).astype(BF16)
    scale = jnp.concatenate(
        [inv_ref[k * nodes : k * nodes + seeds, 0:1] for k in range(layers)]
        + [jnp.zeros((SEED_ROWS - layers * seeds, 1), F32)],
        0,
    )
    second = matmul(e_ref[...], hidden) * scale
    half = second.shape[1] // 2
    second = jnp.where(place_ref[0] == 0, second[:, :half], second[:, half:]).astype(BF16)
    cot = cot_ref[...].astype(F32)
    cot = jnp.concatenate([cot, jnp.zeros((COT_ROWS - seeds, cot.shape[1]), F32)], 0).astype(BF16)
    for j in range(len(packs)):
        span = slice(j * width, (j + 1) * width)
        stage[j, :nodes, :] = back[:, span]
        for part in range(half // width):
            first = nodes + part * SEED_ROWS
            stage[j, first : first + SEED_ROWS, :] = second[:, part * width : (part + 1) * width]
        first = nodes + half // width * SEED_ROWS
        stage[j, first : first + COT_ROWS, :] = cot[:, span]
    moves = []
    for d, pack in enumerate(packs):
        chosen = stage.at[lax.rem(place_ref[1] + d, len(packs))]
        if not is_near(d, len(packs)):
            moves.append((chosen, pack))
            continue
        start = 0
        for source in (chosen, layer_ref.get()):
            rows, wide = source.shape
            for lane in range(0, wide, LANES):
                moves.append((source.at[:, lane : lane + LANES], pack.at[start : start + rows, :]))
                start += rows
    layer_ref.get()
    copies = [pltpu.make_async_copy(source, target, sems.at[i]) for i, (source, target) in enumerate(moves)]
    for copy in copies:
        copy.start()
    total = None
    for k in range(layers):
        span = slice(k * nodes, (k + 1) * nodes)
        back_in = matmul(back, w1_ref.get()[k], (1, 1)) * inv_ref[span, 0:1]
        term = matmul(c_ref.get()[:, span], back_in.astype(BF16))
        total = term if total is None else total + term
    slot_ref[...] = total.astype(BF16).reshape(slot_ref.shape)
    for copy in copies:
        copy.wait()


def weight_kernel(count, place_ref, *refs):
    layer_refs, pack_refs = refs[:2], refs[2 : 2 + count]
    own_ref, outs, total = refs[2 + count], refs[3 + count : -1], refs[-1]
    pack_rows, width = pack_refs[0].shape
    layer_rows, columns = layer_refs[0].shape
    layer_parts, packs = [], []
    for d, ref in enumerate(pack_refs):
        if not is_near(d, count):
            packs.append(ref.get()[...])
            layer_parts.append(layer_refs[min(d, 1)].get()[...])
            continue
        near, start = ref.get()[...], 0
        for rows, wide, made in ((pack_rows, width, packs), (layer_rows, columns, layer_parts)):
            lanes = [near[start + i * rows : start + (i + 1) * rows] for i in range(wide // LANES)]
            made.append(jnp.concatenate(lanes, 1))
            start += rows * len(lanes)
    nodes = LANES
    relations = layer_rows // nodes
    rows = own_ref.shape[0]
    left = jnp.concatenate([p[:nodes, :] for p in packs], 0)
    for k in range(relations):
        right = jnp.concatenate([r[k * nodes : (k + 1) * nodes, :] for r in layer_parts], 0)
        total[k] = matmul(left, right, (0, 0))
    pieces = (pack_rows - nodes - COT_ROWS) // SEED_ROWS
    half = pieces * width
    seeds = SEED_ROWS // (relations + 1)
    first = nodes + pieces * SEED_ROWS
    cots = jnp.concatenate([p[first : first + COT_ROWS, :].astype(F32)[:seeds] for p in packs], 0)
    seconds = [
        jnp.concatenate(
            [p[nodes + part * SEED_ROWS : nodes + (part + 1) * SEED_ROWS, :].astype(F32) for part in range(pieces)],
            1,
        )
        for p in packs
    ]
    second = jnp.concatenate(
        [jnp.concatenate([s[k * seeds : (k + 1) * seeds] for s in seconds], 0) for k in range(relations)], 1
    ).astype(BF16)
    group = count * seeds
    per = columns // (group // COT_ROWS)
    tail = relations * rows
    for d, out in enumerate(outs):
        target = lax.rem(place_ref[0] + d, len(outs))
        start = pl.multiple_of(target * rows, rows)
        for k in range(relations):
            block = total[k, pl.ds(start, rows), :]
            if d == 0:
                own_ref[:, k * columns : (k + 1) * columns] = block
            else:
                out[k * rows : (k + 1) * rows, :] = block.astype(BF16)
        for piece in range(relations * half // columns):
            out[tail + piece * group : tail + (piece + 1) * group, :] = second[
                :, piece * columns : (piece + 1) * columns
            ]
        chosen = cots[:, :rows]
        for j in range(1, len(outs)):
            chosen = jnp.where(target == j, cots[:, j * rows : (j + 1) * rows], chosen)
        for piece in range(group // COT_ROWS):
            lanes = slice(piece * per, piece * per + rows)
            out[out.shape[0] - COT_ROWS :, lanes] = chosen[piece * COT_ROWS : (piece + 1) * COT_ROWS].astype(BF16)


def group_kernel(relations, own_ref, *refs):
    packs, out_ref = refs[:-1], refs[-1]
    rows = own_ref.shape[0]
    columns = packs[0].shape[1]
    tail = relations * rows
    wide = out_ref.shape[1] - relations * columns
    pieces = wide // columns
    group = (packs[0].shape[0] - tail - COT_ROWS) // pieces
    per = columns // (group // COT_ROWS)
    for k in range(relations):
        span = slice(k * columns, (k + 1) * columns)
        block = own_ref[:, span]
        for pack in packs[1:]:
            block = block + pack[k * rows : (k + 1) * rows, :].astype(F32)
        out_ref[:, span] = block.astype(BF16)
    cots = jnp.concatenate(
        [
            p[tail + pieces * group :, piece * per : piece * per + rows]
            for p in packs
            for piece in range(group // COT_ROWS)
        ],
        0,
    )
    for piece in range(pieces):
        first = tail + piece * group
        second = jnp.concatenate([p[first : first + group, :] for p in packs], 0)
        start = (relations + piece) * columns
        out_ref[:, start : start + columns] = matmul(cots, second, (0, 0)).astype(BF16)


def sum_kernel(parts_ref, one_ref, two_ref):
    total = jnp.sum(parts_ref[...].astype(F32), axis=0)
    start = 0
    for ref in (one_ref, two_ref):
        wide = ref.shape[2]
        for k in range(ref.shape[0]):
            ref[k] = total[:, start : start + wide]
            start += wide


def row_kernel(serve_ref, arrived_ref, grad_ref, square_ref):
    rows = lax.broadcasted_iota(jnp.int32, (LANES, serve_ref.shape[1]), 0)
    arrived = arrived_ref[...].reshape(serve_ref.shape[1], grad_ref.shape[1])
    for block in range(grad_ref.shape[0] // LANES):
        span = slice(block * LANES, (block + 1) * LANES)
        onehot = jnp.where(serve_ref[...] == rows + block * LANES, 1.0, 0.0).astype(BF16)
        grad = matmul(onehot, arrived)
        grad_ref[span, :] = grad
        square_ref[block : block + 1, :] = column_to_row(jnp.sum(grad * grad, axis=1, keepdims=True))


def update_kernel(columns, table_ref, grad_ref, accum_ref, mine_ref, other_ref, table_out, accum_out):
    accum = accum_ref[...] + (mine_ref[...] + other_ref[...]) / columns
    accum_out[...] = accum
    inverse = lax.rsqrt(accum)
    for block in range(accum.shape[0]):
        span = slice(block * LANES, (block + 1) * LANES)
        scale = row_to_column(inverse[block : block + 1, :])
        table_out[span, :] = table_ref[span, :] - LEARNING_RATE * grad_ref[span, :] * scale


def shift(array, axis, by):
    size = lax.axis_size(axis)
    return lax.ppermute(array, axis, [(i, (i + by) % size) for i in range(size)])


LIMITS = {serve_kernel: 60, index_kernel: 60, first_kernel: 60, hidden_kernel: 60}
COSTS = {update_kernel: 0, group_kernel: 0, row_kernel: 0}


def body(
    table,
    accum,
    serve_rows,
    seed_slot,
    hop1_slot,
    hop2_slot,
    hop1_rel,
    hop2_rel,
    cotangent,
    w_first,
    w_second,
):
    everyone = ("dp", "y", "z")
    owners = lax.axis_size(everyone)
    table_rows, columns = table.shape
    slots = serve_rows.shape[1]
    seeds, fanout = hop1_slot.shape
    fanout_two = hop2_slot.shape[2]
    nodes = seeds + seeds * fanout
    layers, hidden_units = w_second.shape[:2]
    half = hidden_units // 2
    n_x, n_y, n_z = (lax.axis_size(a) for a in everyone)
    x, y = lax.axis_index("dp"), lax.axis_index("y")
    width = hidden_units // n_x

    blocks_shape = (owners, slots // owners, columns)
    outgoing = call(
        serve_kernel, [shaped(blocks_shape, BF16)], (serve_rows, table), scratch=[pltpu.VMEM((slots, table_rows), BF16)], hbm_in=(0, 1)
    )[0]
    fetched = lax.all_to_all(outgoing, everyone, split_axis=0, concat_axis=0, tiled=True)

    key_one = hop1_slot + slots * hop1_rel
    key_two = (hop2_slot + slots * hop2_rel).reshape(seeds * fanout, fanout_two)
    seed_ids = jnp.arange(seeds, dtype=jnp.int32)[:, None]
    group = (seeds * (1 + hop1_rel) + seed_ids).reshape(-1, 1)
    spare = jnp.full((seeds * fanout, fanout - fanout_two), -1, jnp.int32)
    idx = jnp.concatenate(
        [
            jnp.concatenate([seed_slot[:, None], key_one, seed_ids], 1),
            jnp.concatenate([hop1_slot.reshape(-1, 1), key_two, spare, group], 1),
        ],
        0,
    )
    idx, place, y = lax.optimization_barrier((idx, jnp.stack([lax.axis_index("col"), x]), y))
    ct, c, inverse, member, back_hidden = call(
        index_kernel,
        [
            shaped((layers * nodes, slots), BF16),
            shaped((slots, layers * nodes), BF16),
            shaped((layers * nodes, LANES), F32),
            shaped((SEED_ROWS, nodes), BF16),
            shaped((nodes, hidden_units), F32),
        ],
        (idx, cotangent, w_second),
        scratch=[pltpu.VMEM((LANES, hidden_units), F32)],
        hbm_out=range(5),
    )

    layer_in, partial_pre = call(
        first_kernel,
        [shaped((layers * nodes, columns), BF16), shaped((nodes, hidden_units), F32)],
        (fetched, ct, w_first),
        hbm_in=(0, 1, 2),
        hbm_out=(0, 1),
    )
    other_pre = shift(partial_pre, "col", 1)
    layer_parts = [layer_in, shift(layer_in, "dp", n_x // 2)]

    pack_rows = nodes + half // width * SEED_ROWS + COT_ROWS
    pack_shape = (pack_rows, width)
    near_shape = ((pack_rows * width + layers * nodes * columns) // LANES, LANES)
    slot_grad, *packs = call(
        hidden_kernel,
        [shaped(blocks_shape, BF16)] + [shaped(near_shape if is_near(d, n_x) else pack_shape, BF16) for d in range(n_x)],
        (
            place,
            partial_pre,
            other_pre,
            back_hidden,
            member,
            inverse,
            cotangent,
            c,
            w_first,
            layer_in,
        ),
        smem=1,
        scratch=[pltpu.VMEM((n_x, *pack_shape), BF16), pltpu.SemaphoreType.DMA((n_x * (width + columns) // LANES,))],
        hbm_in=(1, 2, 3, 4, 5, 7, 8, 9),
        hbm_raw=range(1, 1 + n_x),
    )
    packs, layer_parts = lax.optimization_barrier((packs, layer_parts))
    packs = [packs[0]] + [shift(packs[d], "dp", d) for d in range(1, n_x)]
    arrived = lax.all_to_all(slot_grad, everyone, split_axis=0, concat_axis=0, tiled=True)

    block_rows = width // n_y
    group_rows = layers * block_rows + (layers * half // columns) * n_x * seeds + COT_ROWS
    own, *blocks = call(
        functools.partial(weight_kernel, n_x),
        [shaped((block_rows, layers * columns), F32)] + [shaped((group_rows, columns), BF16)] * n_y,
        (y.reshape(1), *layer_parts, *packs),
        smem=1,
        hbm_in=range(1, 3 + n_x),
        scratch=[pltpu.VMEM((layers, width, columns), F32)],
    )
    blocks = [blocks[0]] + [shift(blocks[d], "y", d) for d in range(1, n_y)]
    grad_columns = layers * (columns + half)
    grads = call(
        functools.partial(group_kernel, layers),
        [shaped((block_rows, grad_columns), BF16)],
        (own, *blocks),
    )[0]
    grads = grads.reshape(n_z, block_rows // n_z, grad_columns)
    grads = lax.all_to_all(grads, "z", split_axis=0, concat_axis=0, tiled=True)
    grad_one, grad_two = call(
        sum_kernel,
        [shaped((layers, block_rows // n_z, wide), F32) for wide in (columns, half)],
        (grads,),
    )
    grad_one, grad_two = grad_one.transpose(0, 2, 1), grad_two.transpose(0, 2, 1)

    row_grad, squares = call(
        row_kernel,
        [shaped((table_rows, columns), F32), shaped((table_rows // LANES, LANES), F32)],
        (serve_rows, arrived),
    )
    other_squares = shift(squares, "col", 1)
    new_table, new_accum = call(
        functools.partial(update_kernel, 2 * columns),
        [shaped((table_rows, columns), F32), shaped((table_rows // LANES, LANES), F32)],
        (table, row_grad, accum.reshape(-1, LANES), squares, other_squares),
    )
    return (new_table, new_accum.reshape(-1), grad_one, grad_two)


def solution(mesh):
    n_dp, n_table, n_col = (mesh.shape[a] for a in ("dp", "table", "col"))
    n_y = 4 if n_table % 4 == 0 and n_table > 4 else 2
    fine = Mesh(mesh.devices.reshape(n_dp, n_y, n_table // n_y, n_col), ("dp", "y", "z", "col"))
    rows = ("dp", "y", "z")
    placed = (
        P(rows, "col"),
        P(rows),
        P(rows, None),
        P(rows),
        P(rows, None),
        P(rows, None, None),
        P(rows, None),
        P(rows, None, None),
        P(rows, None),
        P(None, "col", None),
        P(),
    )
    return jax.shard_map(
        body,
        mesh=fine,
        in_specs=placed,
        out_specs=(P(rows, "col"), P(rows), P(None, "col", rows), P(None, "col", rows)),
        check_vma=False,
    )
```

```python
import functools
import jax
import jax.numpy as jnp
from jax import lax
from jax.experimental import pallas as pl
from jax.experimental.pallas import tpu as pltpu
from jax.sharding import Mesh
from jax.sharding import PartitionSpec as P

LEARNING_RATE = 0.1
BF16 = jnp.bfloat16
F32 = jnp.float32
LANES = 128
SEED_ROWS = 32
COT_ROWS = 16


def matmul(a, b, contract=(1, 0)):
    dims = (((contract[0],), (contract[1],)), ((), ()))
    return lax.dot_general(a, b, dims, preferred_element_type=F32)


def row_to_column(row):
    return jnp.transpose(jnp.broadcast_to(row, (LANES, LANES)))[:, 0:1]


def column_to_row(column):
    return jnp.transpose(jnp.broadcast_to(column, (LANES, LANES)))[0:1, :]


class Incoming:
    def __init__(self, source, buffer, semaphore):
        self.buffer, self.waiting = buffer, True
        self.shape = buffer.shape
        self.copy = pltpu.make_async_copy(source, buffer, semaphore)
        self.copy.start()

    def get(self):
        if self.waiting:
            self.copy.wait()
        self.waiting = False
        return self.buffer


class Outgoing:
    def __init__(self, target, buffer, semaphore):
        self.buffer = buffer
        self.copy = pltpu.make_async_copy(buffer, target, semaphore)

    def send(self):
        self.copy.start()


def call(kernel, outs, operands, smem=0, scratch=(), hbm_in=(), hbm_out=(), raw_in=(), hbm_raw=()):
    name = getattr(kernel, "func", kernel)
    limit, flops = LIMITS.get(name, 12), COSTS.get(name, 10**12)
    moved = sum(o.size * o.dtype.itemsize for o in list(operands) + list(outs))
    specs = [
        pl.BlockSpec(memory_space=pltpu.SMEM if i < smem else pltpu.HBM if i in hbm_in or i in raw_in else pltpu.VMEM)
        for i in range(len(operands))
    ]
    made = [
        pl.BlockSpec(memory_space=pltpu.HBM if i in hbm_out or i in hbm_raw else pltpu.VMEM)
        for i in range(len(outs))
    ]
    buffers = [pltpu.VMEM(operands[i].shape, operands[i].dtype) for i in hbm_in]
    buffers += [pltpu.VMEM(outs[i].shape, outs[i].dtype) for i in hbm_out]
    semaphores = [pltpu.SemaphoreType.DMA((len(buffers),))] if buffers else []

    def wrapped(*refs):
        refs = list(refs)
        if not buffers:
            kernel(*refs)
            return
        first = len(operands) + len(outs)
        held, sems = refs[first : first + len(buffers)], refs[first + len(buffers)]
        rest = refs[first + len(buffers) + 1 :]
        for j, i in enumerate(hbm_in):
            refs[i] = Incoming(refs[i], held[j], sems.at[j])
        leaving = []
        for j, i in enumerate(hbm_out, len(hbm_in)):
            place = len(operands) + i
            refs[place] = Outgoing(refs[place], held[j], sems.at[j])
            leaving.append(refs[place])
        kernel(*refs[:first], *rest)
        for out in leaving:
            out.copy.wait()

    return pl.pallas_call(
        wrapped,
        out_shape=tuple(outs),
        in_specs=specs,
        out_specs=tuple(made),
        scratch_shapes=buffers + semaphores + list(scratch),
        compiler_params=pltpu.CompilerParams(vmem_limit_bytes=limit * 1024 * 1024),
        cost_estimate=pl.CostEstimate(flops=flops, bytes_accessed=moved, transcendentals=0),
    )(*operands)


def is_near(distance, count):
    return distance not in (0, count // 2)


def shaped(shape, dtype):
    return jax.ShapeDtypeStruct(shape, dtype)


def serve_kernel(serve_ref, table_ref, out_ref, onehot, rows, picked, sems):
    chunks = range(table_ref.shape[1] // LANES)
    loads = [
        pltpu.make_async_copy(table_ref.at[:, i * LANES : (i + 1) * LANES], rows.at[i], sems.at[i]) for i in chunks
    ]
    for load in loads:
        load.start()
    serve = serve_ref.get()[...]
    lanes = lax.broadcasted_iota(jnp.int32, (LANES, onehot.shape[1]), 1)
    for block in range(serve.shape[1] // LANES):
        span = slice(block * LANES, (block + 1) * LANES)
        onehot[span, :] = jnp.where(row_to_column(serve[:, span]) == lanes, 1.0, 0.0).astype(BF16)
    stores = []
    for i in chunks:
        loads[i].wait()
        found = matmul(onehot[...], rows[i].astype(BF16)).astype(BF16)
        picked[i] = found.reshape(picked.shape[1:])
        target = out_ref.at[:, :, i * LANES : (i + 1) * LANES]
        stores.append(pltpu.make_async_copy(picked.at[i], target, sems.at[len(chunks) + i]))
        stores[i].start()
    for store in stores:
        store.wait()


def index_kernel(idx_ref, cot_ref, w2_ref, *refs):
    outs, spread = refs[:-1], refs[-1]
    ct_ref, c_ref, inv_ref, e_ref, back_ref = (o.buffer for o in outs)
    nodes = idx_ref.shape[0]
    slots = ct_ref.shape[1]
    seeds = cot_ref.shape[0]
    neighbours = idx_ref.shape[1] - 2
    lanes = lax.broadcasted_iota(jnp.int32, (nodes, 2 * slots), 1)
    idx = idx_ref[...]
    counts = jnp.zeros((nodes, 2 * slots), F32)
    for j in range(1, 1 + neighbours):
        counts = counts + jnp.where(idx[:, j : j + 1] == lanes, 1.0, 0.0)
    own = jnp.where(idx[:, 0:1] == lanes[:, :slots], 1.0, 0.0)
    parts = (own, counts[:, :slots], counts[:, slots:])
    spread[...] = jnp.zeros(spread.shape, F32)
    for k, part in enumerate(parts):
        span = slice(k * nodes, (k + 1) * nodes)
        ct_ref[span, :] = part.astype(BF16)
        c_ref[:, span] = jnp.transpose(part).astype(BF16)
        if k == 0:
            inverse = jnp.ones((nodes, 1), F32)
        else:
            inverse = 1.0 / jnp.maximum(jnp.sum(part, axis=1, keepdims=True), 1.0)
        inv_ref[span, :] = jnp.broadcast_to(inverse, (nodes, LANES))
        back = matmul(cot_ref[...], w2_ref[k], (1, 1))
        spread[k * seeds : (k + 1) * seeds, :] = back * inverse[:seeds]
    groups = lax.broadcasted_iota(jnp.int32, (nodes, LANES), 1)
    member = jnp.where(idx[:, neighbours + 1 : neighbours + 2] == groups, 1.0, 0.0)
    e_ref[...] = jnp.transpose(member)[:SEED_ROWS].astype(BF16)
    whole = spread[...]
    high = whole.astype(BF16)
    low = (whole - high.astype(F32)).astype(BF16)
    for out in outs[:-1]:
        out.send()
    back_ref[...] = matmul(member.astype(BF16), high) + matmul(member.astype(BF16), low)
    outs[-1].send()


def first_kernel(fetched_ref, ct_ref, w1_ref, layer_ref, partial_out, wide, partial_ref, sems):
    layers = w1_ref.shape[0]
    layer_out, layer_ref = layer_ref, layer_ref.buffer
    nodes = partial_ref.shape[0]
    fetched = fetched_ref.get()[...].reshape(ct_ref.shape[1], layer_ref.shape[1])
    ct_ref = ct_ref.get()
    ones = jnp.ones((ct_ref.shape[1], LANES), BF16)
    columns = layer_ref.shape[1]
    for k in range(layers):
        span = slice(k * nodes, (k + 1) * nodes)
        summed = matmul(ct_ref[span, :], fetched)
        inverse = 1.0 / jnp.maximum(matmul(ct_ref[span, :], ones)[:, 0:1], 1.0)
        layer = (summed * inverse).astype(BF16)
        layer_ref[span, :] = layer
        wide[:, k * columns : (k + 1) * columns] = layer
    layer_out.send()
    weights = w1_ref.get()[...].reshape(layers * columns, partial_ref.shape[1])
    half = partial_ref.shape[1] // 2
    copies = []
    for i in range(2):
        span = slice(i * half, (i + 1) * half)
        partial_ref[:, span] = matmul(wide[...], weights[:, span])
        copies.append(pltpu.make_async_copy(partial_ref.at[:, span], partial_out.at[:, span], sems.at[i]))
        copies[i].start()
    for copy in copies:
        copy.wait()


def hidden_kernel(place_ref, mine_ref, other_ref, back_ref, e_ref, inv_ref, cot_ref, c_ref, w1_ref, layer_ref, slot_ref, *refs):
    packs, (stage, scaled, sems) = refs[:-3], refs[-3:]
    nodes = mine_ref.shape[0]
    width = stage.shape[2]
    seeds = cot_ref.shape[0]
    layers = inv_ref.shape[0] // nodes
    values = mine_ref.get()[...] + other_ref.get()[...]
    back_ref, e_ref, inv_ref = back_ref.get(), e_ref.get(), inv_ref.get()
    sigma = jax.nn.sigmoid(values)
    hidden = (values * sigma).astype(BF16)
    slope = sigma * (1.0 + values * (1.0 - sigma))
    back = (back_ref[...] * slope).astype(BF16)
    scale = jnp.concatenate(
        [inv_ref[k * nodes : k * nodes + seeds, 0:1] for k in range(layers)]
        + [jnp.zeros((SEED_ROWS - layers * seeds, 1), F32)],
        0,
    )
    second = matmul(e_ref[...], hidden) * scale
    half = second.shape[1] // 2
    second = jnp.where(place_ref[0] == 0, second[:, :half], second[:, half:]).astype(BF16)
    cot = cot_ref[...].astype(F32)
    cot = jnp.concatenate([cot, jnp.zeros((COT_ROWS - seeds, cot.shape[1]), F32)], 0).astype(BF16)
    for j in range(len(packs)):
        span = slice(j * width, (j + 1) * width)
        stage[j, :nodes, :] = back[:, span]
        for part in range(half // width):
            first = nodes + part * SEED_ROWS
            stage[j, first : first + SEED_ROWS, :] = second[:, part * width : (part + 1) * width]
        first = nodes + half // width * SEED_ROWS
        stage[j, first : first + COT_ROWS, :] = cot[:, span]
    moves = []
    for d, pack in enumerate(packs):
        chosen = stage.at[lax.rem(place_ref[1] + d, len(packs))]
        if not is_near(d, len(packs)):
            moves.append((chosen, pack))
            continue
        start = 0
        for source in (chosen, layer_ref.get()):
            rows, wide = source.shape
            for lane in range(0, wide, LANES):
                moves.append((source.at[:, lane : lane + LANES], pack.at[start : start + rows, :]))
                start += rows
    layer_ref.get()
    copies = [pltpu.make_async_copy(source, target, sems.at[i]) for i, (source, target) in enumerate(moves)]
    for copy in copies:
        copy.start()
    columns = w1_ref.shape[1]
    back_in = matmul(back, w1_ref.get()[...].reshape(layers * columns, back.shape[1]), (1, 1))
    for k in range(layers):
        span = slice(k * nodes, (k + 1) * nodes)
        scaled[span, :] = (back_in[:, k * columns : (k + 1) * columns] * inv_ref[span, 0:1]).astype(BF16)
    slot_ref[...] = matmul(c_ref.get()[...], scaled[...]).astype(BF16).reshape(slot_ref.shape)
    for copy in copies:
        copy.wait()


def weight_kernel(count, place_ref, *refs):
    layer_refs, pack_refs = refs[:2], refs[2 : 2 + count]
    own_ref, outs, total = refs[2 + count], refs[3 + count : -1], refs[-1]
    pack_rows, width = pack_refs[0].shape
    layer_rows, columns = layer_refs[0].shape
    layer_parts, packs = [], []
    for d, ref in enumerate(pack_refs):
        if not is_near(d, count):
            packs.append(ref.get()[...])
            layer_parts.append(layer_refs[min(d, 1)].get()[...])
            continue
        near, start = ref.get()[...], 0
        for rows, wide, made in ((pack_rows, width, packs), (layer_rows, columns, layer_parts)):
            lanes = [near[start + i * rows : start + (i + 1) * rows] for i in range(wide // LANES)]
            made.append(jnp.concatenate(lanes, 1))
            start += rows * len(lanes)
    nodes = LANES
    relations = layer_rows // nodes
    rows = own_ref.shape[0]
    left = jnp.concatenate([p[:nodes, :] for p in packs], 0)
    for k in range(relations):
        right = jnp.concatenate([r[k * nodes : (k + 1) * nodes, :] for r in layer_parts], 0)
        total[k] = matmul(left, right, (0, 0))
    pieces = (pack_rows - nodes - COT_ROWS) // SEED_ROWS
    half = pieces * width
    seeds = SEED_ROWS // (relations + 1)
    first = nodes + pieces * SEED_ROWS
    cots = jnp.concatenate([p[first : first + COT_ROWS, :].astype(F32)[:seeds] for p in packs], 0)
    seconds = [
        jnp.concatenate(
            [p[nodes + part * SEED_ROWS : nodes + (part + 1) * SEED_ROWS, :].astype(F32) for part in range(pieces)],
            1,
        )
        for p in packs
    ]
    second = jnp.concatenate(
        [jnp.concatenate([s[k * seeds : (k + 1) * seeds] for s in seconds], 0) for k in range(relations)], 1
    ).astype(BF16)
    group = count * seeds
    per = columns // (group // COT_ROWS)
    tail = relations * rows
    for d, out in enumerate(outs):
        target = lax.rem(place_ref[0] + d, len(outs))
        start = pl.multiple_of(target * rows, rows)
        for k in range(relations):
            block = total[k, pl.ds(start, rows), :]
            if d == 0:
                own_ref[:, k * columns : (k + 1) * columns] = block
            else:
                out[k * rows : (k + 1) * rows, :] = block.astype(BF16)
        for piece in range(relations * half // columns):
            out[tail + piece * group : tail + (piece + 1) * group, :] = second[
                :, piece * columns : (piece + 1) * columns
            ]
        chosen = cots[:, :rows]
        for j in range(1, len(outs)):
            chosen = jnp.where(target == j, cots[:, j * rows : (j + 1) * rows], chosen)
        for piece in range(group // COT_ROWS):
            lanes = slice(piece * per, piece * per + rows)
            out[out.shape[0] - COT_ROWS :, lanes] = chosen[piece * COT_ROWS : (piece + 1) * COT_ROWS].astype(BF16)


def group_kernel(relations, own_ref, *refs):
    packs, out_ref = refs[:-1], refs[-1]
    rows = own_ref.shape[0]
    columns = packs[0].shape[1]
    tail = relations * rows
    wide = out_ref.shape[1] - relations * columns
    pieces = wide // columns
    group = (packs[0].shape[0] - tail - COT_ROWS) // pieces
    per = columns // (group // COT_ROWS)
    for k in range(relations):
        span = slice(k * columns, (k + 1) * columns)
        block = own_ref[:, span]
        for pack in packs[1:]:
            block = block + pack[k * rows : (k + 1) * rows, :].astype(F32)
        out_ref[:, span] = block.astype(BF16)
    cots = jnp.concatenate(
        [
            p[tail + pieces * group :, piece * per : piece * per + rows]
            for p in packs
            for piece in range(group // COT_ROWS)
        ],
        0,
    )
    for piece in range(pieces):
        first = tail + piece * group
        second = jnp.concatenate([p[first : first + group, :] for p in packs], 0)
        start = (relations + piece) * columns
        out_ref[:, start : start + columns] = matmul(cots, second, (0, 0)).astype(BF16)


def sum_kernel(parts_ref, one_ref, two_ref):
    total = jnp.sum(parts_ref[...].astype(F32), axis=0)
    start = 0
    for ref in (one_ref, two_ref):
        wide = ref.shape[2]
        for k in range(ref.shape[0]):
            ref[k] = total[:, start : start + wide]
            start += wide


def row_kernel(serve_ref, arrived_ref, grad_ref, square_ref):
    rows = lax.broadcasted_iota(jnp.int32, (LANES, serve_ref.shape[1]), 0)
    arrived = arrived_ref[...].reshape(serve_ref.shape[1], grad_ref.shape[1])
    for block in range(grad_ref.shape[0] // LANES):
        span = slice(block * LANES, (block + 1) * LANES)
        onehot = jnp.where(serve_ref[...] == rows + block * LANES, 1.0, 0.0).astype(BF16)
        grad = matmul(onehot, arrived)
        grad_ref[span, :] = grad
        square_ref[block : block + 1, :] = column_to_row(jnp.sum(grad * grad, axis=1, keepdims=True))


def update_kernel(columns, table_ref, grad_ref, accum_ref, mine_ref, other_ref, table_out, accum_out):
    accum = accum_ref[...] + (mine_ref[...] + other_ref[...]) / columns
    accum_out[...] = accum
    inverse = lax.rsqrt(accum)
    for block in range(accum.shape[0]):
        span = slice(block * LANES, (block + 1) * LANES)
        scale = row_to_column(inverse[block : block + 1, :])
        table_out[span, :] = table_ref[span, :] - LEARNING_RATE * grad_ref[span, :] * scale


def shift(array, axis, by):
    size = lax.axis_size(axis)
    return lax.ppermute(array, axis, [(i, (i + by) % size) for i in range(size)])


LIMITS = {serve_kernel: 60, index_kernel: 60, first_kernel: 60, hidden_kernel: 60}
COSTS = {update_kernel: 0, group_kernel: 0, row_kernel: 0}


def body(
    table,
    accum,
    serve_rows,
    seed_slot,
    hop1_slot,
    hop2_slot,
    hop1_rel,
    hop2_rel,
    cotangent,
    w_first,
    w_second,
):
    everyone = ("dp", "y", "z")
    owners = lax.axis_size(everyone)
    table_rows, columns = table.shape
    slots = serve_rows.shape[1]
    seeds, fanout = hop1_slot.shape
    fanout_two = hop2_slot.shape[2]
    nodes = seeds + seeds * fanout
    layers, hidden_units = w_second.shape[:2]
    half = hidden_units // 2
    n_x, n_y, n_z = (lax.axis_size(a) for a in everyone)
    x, y = lax.axis_index("dp"), lax.axis_index("y")
    width = hidden_units // n_x

    blocks_shape = (owners, slots // owners, columns)
    chunks = columns // LANES
    outgoing = call(
        serve_kernel,
        [shaped(blocks_shape, BF16)],
        (serve_rows, table),
        scratch=[
            pltpu.VMEM((slots, table_rows), BF16),
            pltpu.VMEM((chunks, table_rows, LANES), F32),
            pltpu.VMEM((chunks, *blocks_shape[:2], LANES), BF16),
            pltpu.SemaphoreType.DMA((2 * chunks,)),
        ],
        hbm_in=(0,),
        raw_in=(1,),
        hbm_raw=(0,),
    )[0]
    fetched = lax.all_to_all(outgoing, everyone, split_axis=0, concat_axis=0, tiled=True)

    key_one = hop1_slot + slots * hop1_rel
    key_two = (hop2_slot + slots * hop2_rel).reshape(seeds * fanout, fanout_two)
    seed_ids = jnp.arange(seeds, dtype=jnp.int32)[:, None]
    group = (seeds * (1 + hop1_rel) + seed_ids).reshape(-1, 1)
    spare = jnp.full((seeds * fanout, fanout - fanout_two), -1, jnp.int32)
    idx = jnp.concatenate(
        [
            jnp.concatenate([seed_slot[:, None], key_one, seed_ids], 1),
            jnp.concatenate([hop1_slot.reshape(-1, 1), key_two, spare, group], 1),
        ],
        0,
    )
    idx, place, y = lax.optimization_barrier((idx, jnp.stack([lax.axis_index("col"), x]), y))
    ct, c, inverse, member, back_hidden = call(
        index_kernel,
        [
            shaped((layers * nodes, slots), BF16),
            shaped((slots, layers * nodes), BF16),
            shaped((layers * nodes, LANES), F32),
            shaped((SEED_ROWS, nodes), BF16),
            shaped((nodes, hidden_units), F32),
        ],
        (idx, cotangent, w_second),
        scratch=[pltpu.VMEM((LANES, hidden_units), F32)],
        hbm_out=range(5),
    )

    layer_in, partial_pre = call(
        first_kernel,
        [shaped((layers * nodes, columns), BF16), shaped((nodes, hidden_units), F32)],
        (fetched, ct, w_first),
        scratch=[
            pltpu.VMEM((nodes, layers * columns), BF16),
            pltpu.VMEM((nodes, hidden_units), F32),
            pltpu.SemaphoreType.DMA((2,)),
        ],
        hbm_in=(0, 1, 2),
        hbm_out=(0,),
        hbm_raw=(1,),
    )
    other_pre = shift(partial_pre, "col", 1)
    layer_parts = [layer_in, shift(layer_in, "dp", n_x // 2)]

    pack_rows = nodes + half // width * SEED_ROWS + COT_ROWS
    pack_shape = (pack_rows, width)
    near_shape = ((pack_rows * width + layers * nodes * columns) // LANES, LANES)
    slot_grad, *packs = call(
        hidden_kernel,
        [shaped(blocks_shape, BF16)] + [shaped(near_shape if is_near(d, n_x) else pack_shape, BF16) for d in range(n_x)],
        (
            place,
            partial_pre,
            other_pre,
            back_hidden,
            member,
            inverse,
            cotangent,
            c,
            w_first,
            layer_in,
        ),
        smem=1,
        scratch=[
            pltpu.VMEM((n_x, *pack_shape), BF16),
            pltpu.VMEM((layers * nodes, columns), BF16),
            pltpu.SemaphoreType.DMA((n_x * (width + columns) // LANES,)),
        ],
        hbm_in=(1, 2, 3, 4, 5, 9, 8, 7),
        hbm_raw=range(1, 1 + n_x),
    )
    packs[n_x // 2], layer_parts = lax.optimization_barrier((packs[n_x // 2], layer_parts))
    packs = [packs[0]] + [shift(packs[d], "dp", d) for d in range(1, n_x)]
    arrived = lax.all_to_all(slot_grad, everyone, split_axis=0, concat_axis=0, tiled=True)

    block_rows = width // n_y
    group_rows = layers * block_rows + (layers * half // columns) * n_x * seeds + COT_ROWS
    own, *blocks = call(
        functools.partial(weight_kernel, n_x),
        [shaped((block_rows, layers * columns), F32)] + [shaped((group_rows, columns), BF16)] * n_y,
        (y.reshape(1), *layer_parts, *packs),
        smem=1,
        hbm_in=range(1, 3 + n_x),
        scratch=[pltpu.VMEM((layers, width, columns), F32)],
    )
    blocks = [blocks[0]] + [shift(blocks[d], "y", d) for d in range(1, n_y)]
    grad_columns = layers * (columns + half)
    grads = call(
        functools.partial(group_kernel, layers),
        [shaped((block_rows, grad_columns), BF16)],
        (own, *blocks),
    )[0]
    grads = grads.reshape(n_z, block_rows // n_z, grad_columns)
    grads = lax.all_to_all(grads, "z", split_axis=0, concat_axis=0, tiled=True)
    grad_one, grad_two = call(
        sum_kernel,
        [shaped((layers, block_rows // n_z, wide), F32) for wide in (columns, half)],
        (grads,),
    )
    grad_one, grad_two = grad_one.transpose(0, 2, 1), grad_two.transpose(0, 2, 1)

    row_grad, squares = call(
        row_kernel,
        [shaped((table_rows, columns), F32), shaped((table_rows // LANES, LANES), F32)],
        (serve_rows, arrived),
    )
    other_squares = shift(squares, "col", 1)
    new_table, new_accum = call(
        functools.partial(update_kernel, 2 * columns),
        [shaped((table_rows, columns), F32), shaped((table_rows // LANES, LANES), F32)],
        (table, row_grad, accum.reshape(-1, LANES), squares, other_squares),
    )
    return (new_table, new_accum.reshape(-1), grad_one, grad_two)


def solution(mesh):
    n_dp, n_table, n_col = (mesh.shape[a] for a in ("dp", "table", "col"))
    n_y = 4 if n_table % 4 == 0 and n_table > 4 else 2
    fine = Mesh(mesh.devices.reshape(n_dp, n_y, n_table // n_y, n_col), ("dp", "y", "z", "col"))
    rows = ("dp", "y", "z")
    placed = (
        P(rows, "col"),
        P(rows),
        P(rows, None),
        P(rows),
        P(rows, None),
        P(rows, None, None),
        P(rows, None),
        P(rows, None, None),
        P(rows, None),
        P(None, "col", None),
        P(),
    )
    return jax.shard_map(
        body,
        mesh=fine,
        in_specs=placed,
        out_specs=(P(rows, "col"), P(rows), P(None, "col", rows), P(None, "col", rows)),
        check_vma=False,
    )
```

```python
import functools
import jax
import jax.numpy as jnp
from jax import lax
from jax.experimental import pallas as pl
from jax.experimental.pallas import tpu as pltpu
from jax.sharding import Mesh
from jax.sharding import PartitionSpec as P

LEARNING_RATE = 0.1
BF16 = jnp.bfloat16
F32 = jnp.float32
LANES = 128
SEED_ROWS = 32
COT_ROWS = 16


def matmul(a, b, contract=(1, 0)):
    dims = (((contract[0],), (contract[1],)), ((), ()))
    return lax.dot_general(a, b, dims, preferred_element_type=F32)


def row_to_column(row):
    return jnp.transpose(jnp.broadcast_to(row, (LANES, LANES)))[:, 0:1]


def column_to_row(column):
    return jnp.transpose(jnp.broadcast_to(column, (LANES, LANES)))[0:1, :]


class Incoming:
    def __init__(self, source, buffer, semaphore):
        self.buffer, self.waiting = buffer, True
        self.shape = buffer.shape
        self.copy = pltpu.make_async_copy(source, buffer, semaphore)
        self.copy.start()

    def get(self):
        if self.waiting:
            self.copy.wait()
        self.waiting = False
        return self.buffer


class Outgoing:
    def __init__(self, target, buffer, semaphore):
        self.buffer = buffer
        self.copy = pltpu.make_async_copy(buffer, target, semaphore)

    def send(self):
        self.copy.start()


def call(kernel, outs, operands, smem=0, scratch=(), hbm_in=(), hbm_out=(), raw_in=(), hbm_raw=()):
    name = getattr(kernel, "func", kernel)
    limit, flops = LIMITS.get(name, 12), COSTS.get(name, 10**12)
    moved = sum(o.size * o.dtype.itemsize for o in list(operands) + list(outs))
    specs = [
        pl.BlockSpec(memory_space=pltpu.SMEM if i < smem else pltpu.HBM if i in hbm_in or i in raw_in else pltpu.VMEM)
        for i in range(len(operands))
    ]
    made = [
        pl.BlockSpec(memory_space=pltpu.HBM if i in hbm_out or i in hbm_raw else pltpu.VMEM)
        for i in range(len(outs))
    ]
    buffers = [pltpu.VMEM(operands[i].shape, operands[i].dtype) for i in hbm_in]
    buffers += [pltpu.VMEM(outs[i].shape, outs[i].dtype) for i in hbm_out]
    semaphores = [pltpu.SemaphoreType.DMA((len(buffers),))] if buffers else []

    def wrapped(*refs):
        refs = list(refs)
        if not buffers:
            kernel(*refs)
            return
        first = len(operands) + len(outs)
        held, sems = refs[first : first + len(buffers)], refs[first + len(buffers)]
        rest = refs[first + len(buffers) + 1 :]
        for j, i in enumerate(hbm_in):
            refs[i] = Incoming(refs[i], held[j], sems.at[j])
        leaving = []
        for j, i in enumerate(hbm_out, len(hbm_in)):
            place = len(operands) + i
            refs[place] = Outgoing(refs[place], held[j], sems.at[j])
            leaving.append(refs[place])
        kernel(*refs[:first], *rest)
        for out in leaving:
            out.copy.wait()

    return pl.pallas_call(
        wrapped,
        out_shape=tuple(outs),
        in_specs=specs,
        out_specs=tuple(made),
        scratch_shapes=buffers + semaphores + list(scratch),
        compiler_params=pltpu.CompilerParams(vmem_limit_bytes=limit * 1024 * 1024),
        cost_estimate=pl.CostEstimate(flops=flops, bytes_accessed=moved, transcendentals=0),
    )(*operands)


def is_near(distance, count):
    return distance not in (0, count // 2)


def shaped(shape, dtype):
    return jax.ShapeDtypeStruct(shape, dtype)


def serve_kernel(serve_ref, table_ref, out_ref, onehot, rows, whole, sems):
    parts = rows.shape[0]
    loads = [pltpu.make_async_copy(table_ref.at[i], rows.at[i], sems.at[i]) for i in range(parts)]
    for load in loads:
        load.start()
    serve = serve_ref.get()[...]
    lanes = lax.broadcasted_iota(jnp.int32, (LANES, onehot.shape[1]), 1)
    for block in range(serve.shape[1] // LANES):
        span = slice(block * LANES, (block + 1) * LANES)
        onehot[span, :] = jnp.where(row_to_column(serve[:, span]) == lanes, 1.0, 0.0).astype(BF16)
    for i, load in enumerate(loads):
        load.wait()
        whole[i * rows.shape[1] : (i + 1) * rows.shape[1], :] = rows[i].astype(BF16)
    out_ref[...] = matmul(onehot[...], whole[...]).astype(BF16).reshape(out_ref.shape)


def index_kernel(idx_ref, cot_ref, w2_ref, *refs):
    outs, spread = refs[:-1], refs[-1]
    ct_ref, c_ref, inv_ref, e_ref, back_ref = (o.buffer for o in outs)
    nodes = idx_ref.shape[0]
    slots = ct_ref.shape[1]
    seeds = cot_ref.shape[0]
    neighbours = idx_ref.shape[1] - 2
    lanes = lax.broadcasted_iota(jnp.int32, (nodes, 2 * slots), 1)
    idx = idx_ref[...]
    counts = jnp.zeros((nodes, 2 * slots), F32)
    for j in range(1, 1 + neighbours):
        counts = counts + jnp.where(idx[:, j : j + 1] == lanes, 1.0, 0.0)
    own = jnp.where(idx[:, 0:1] == lanes[:, :slots], 1.0, 0.0)
    parts = (own, counts[:, :slots], counts[:, slots:])
    spread[...] = jnp.zeros(spread.shape, F32)
    for k, part in enumerate(parts):
        span = slice(k * nodes, (k + 1) * nodes)
        ct_ref[span, :] = part.astype(BF16)
        c_ref[:, span] = jnp.transpose(part).astype(BF16)
        if k == 0:
            inverse = jnp.ones((nodes, 1), F32)
        else:
            inverse = 1.0 / jnp.maximum(jnp.sum(part, axis=1, keepdims=True), 1.0)
        inv_ref[span, :] = jnp.broadcast_to(inverse, (nodes, LANES))
        back = matmul(cot_ref[...], w2_ref[k], (1, 1))
        spread[k * seeds : (k + 1) * seeds, :] = back * inverse[:seeds]
    groups = lax.broadcasted_iota(jnp.int32, (nodes, LANES), 1)
    member = jnp.where(idx[:, neighbours + 1 : neighbours + 2] == groups, 1.0, 0.0)
    e_ref[...] = jnp.transpose(member)[:SEED_ROWS].astype(BF16)
    whole = spread[...]
    high = whole.astype(BF16)
    low = (whole - high.astype(F32)).astype(BF16)
    for out in outs[:-1]:
        out.send()
    back_ref[...] = matmul(member.astype(BF16), high) + matmul(member.astype(BF16), low)
    outs[-1].send()


def first_kernel(fetched_ref, ct_ref, w1_ref, layer_ref, partial_out, wide, partial_ref, sems):
    layers = w1_ref.shape[0]
    layer_out, layer_ref = layer_ref, layer_ref.buffer
    nodes = partial_ref.shape[0]
    fetched = fetched_ref.get()[...].reshape(ct_ref.shape[1], layer_ref.shape[1])
    ct_ref = ct_ref.get()
    ones = jnp.ones((ct_ref.shape[1], LANES), BF16)
    columns = layer_ref.shape[1]
    for k in range(layers):
        span = slice(k * nodes, (k + 1) * nodes)
        summed = matmul(ct_ref[span, :], fetched)
        inverse = 1.0 / jnp.maximum(matmul(ct_ref[span, :], ones)[:, 0:1], 1.0)
        layer = (summed * inverse).astype(BF16)
        layer_ref[span, :] = layer
        wide[:, k * columns : (k + 1) * columns] = layer
    layer_out.send()
    weights = w1_ref.get()[...].reshape(layers * columns, partial_ref.shape[1])
    half = partial_ref.shape[1] // 2
    copies = []
    for i in range(2):
        span = slice(i * half, (i + 1) * half)
        partial_ref[:, span] = matmul(wide[...], weights[:, span])
        copies.append(pltpu.make_async_copy(partial_ref.at[:, span], partial_out.at[:, span], sems.at[i]))
        copies[i].start()
    for copy in copies:
        copy.wait()


def hidden_kernel(place_ref, mine_ref, other_ref, back_ref, e_ref, inv_ref, cot_ref, c_ref, w1_ref, layer_ref, slot_ref, *refs):
    packs, (stage, scaled, sems) = refs[:-3], refs[-3:]
    nodes = mine_ref.shape[0]
    width = stage.shape[2]
    seeds = cot_ref.shape[0]
    layers = inv_ref.shape[0] // nodes
    values = mine_ref.get()[...] + other_ref.get()[...]
    back_ref, e_ref, inv_ref = back_ref.get(), e_ref.get(), inv_ref.get()
    sigma = jax.nn.sigmoid(values)
    hidden = (values * sigma).astype(BF16)
    slope = sigma * (1.0 + values * (1.0 - sigma))
    back = (back_ref[...] * slope).astype(BF16)
    scale = jnp.concatenate(
        [inv_ref[k * nodes : k * nodes + seeds, 0:1] for k in range(layers)]
        + [jnp.zeros((SEED_ROWS - layers * seeds, 1), F32)],
        0,
    )
    second = matmul(e_ref[...], hidden) * scale
    half = second.shape[1] // 2
    second = jnp.where(place_ref[0] == 0, second[:, :half], second[:, half:]).astype(BF16)
    cot = cot_ref[...].astype(F32)
    cot = jnp.concatenate([cot, jnp.zeros((COT_ROWS - seeds, cot.shape[1]), F32)], 0).astype(BF16)
    for j in range(len(packs)):
        span = slice(j * width, (j + 1) * width)
        stage[j, :nodes, :] = back[:, span]
        for part in range(half // width):
            first = nodes + part * SEED_ROWS
            stage[j, first : first + SEED_ROWS, :] = second[:, part * width : (part + 1) * width]
        first = nodes + half // width * SEED_ROWS
        stage[j, first : first + COT_ROWS, :] = cot[:, span]
    moves = []
    for d, pack in enumerate(packs):
        chosen = stage.at[lax.rem(place_ref[1] + d, len(packs))]
        if not is_near(d, len(packs)):
            moves.append((chosen, pack))
            continue
        start = 0
        for source in (chosen, layer_ref.get()):
            rows, wide = source.shape
            for lane in range(0, wide, LANES):
                moves.append((source.at[:, lane : lane + LANES], pack.at[start : start + rows, :]))
                start += rows
    layer_ref.get()
    copies = [pltpu.make_async_copy(source, target, sems.at[i]) for i, (source, target) in enumerate(moves)]
    for copy in copies:
        copy.start()
    columns = w1_ref.shape[1]
    back_in = matmul(back, w1_ref.get()[...].reshape(layers * columns, back.shape[1]), (1, 1))
    for k in range(layers):
        span = slice(k * nodes, (k + 1) * nodes)
        scaled[span, :] = (back_in[:, k * columns : (k + 1) * columns] * inv_ref[span, 0:1]).astype(BF16)
    slot_ref[...] = matmul(c_ref.get()[...], scaled[...]).astype(BF16).reshape(slot_ref.shape)
    for copy in copies:
        copy.wait()


def weight_kernel(count, place_ref, *refs):
    layer_refs, pack_refs = refs[:2], refs[2 : 2 + count]
    own_ref, outs, total = refs[2 + count], refs[3 + count : -1], refs[-1]
    pack_rows, width = pack_refs[0].shape
    layer_rows, columns = layer_refs[0].shape
    layer_parts, packs = [], []
    for d, ref in enumerate(pack_refs):
        if not is_near(d, count):
            packs.append(ref.get()[...])
            layer_parts.append(layer_refs[min(d, 1)].get()[...])
            continue
        near, start = ref.get()[...], 0
        for rows, wide, made in ((pack_rows, width, packs), (layer_rows, columns, layer_parts)):
            lanes = [near[start + i * rows : start + (i + 1) * rows] for i in range(wide // LANES)]
            made.append(jnp.concatenate(lanes, 1))
            start += rows * len(lanes)
    nodes = LANES
    relations = layer_rows // nodes
    rows = own_ref.shape[0]
    left = jnp.concatenate([p[:nodes, :] for p in packs], 0)
    for k in range(relations):
        right = jnp.concatenate([r[k * nodes : (k + 1) * nodes, :] for r in layer_parts], 0)
        total[k] = matmul(left, right, (0, 0))
    pieces = (pack_rows - nodes - COT_ROWS) // SEED_ROWS
    half = pieces * width
    seeds = SEED_ROWS // (relations + 1)
    first = nodes + pieces * SEED_ROWS
    cots = jnp.concatenate([p[first : first + COT_ROWS, :].astype(F32)[:seeds] for p in packs], 0)
    seconds = [
        jnp.concatenate(
            [p[nodes + part * SEED_ROWS : nodes + (part + 1) * SEED_ROWS, :].astype(F32) for part in range(pieces)],
            1,
        )
        for p in packs
    ]
    second = jnp.concatenate(
        [jnp.concatenate([s[k * seeds : (k + 1) * seeds] for s in seconds], 0) for k in range(relations)], 1
    ).astype(BF16)
    group = count * seeds
    per = columns // (group // COT_ROWS)
    tail = relations * rows
    for d, out in enumerate(outs):
        target = lax.rem(place_ref[0] + d, len(outs))
        start = pl.multiple_of(target * rows, rows)
        for k in range(relations):
            block = total[k, pl.ds(start, rows), :]
            if d == 0:
                own_ref[:, k * columns : (k + 1) * columns] = block
            else:
                out[k * rows : (k + 1) * rows, :] = block.astype(BF16)
        for piece in range(relations * half // columns):
            out[tail + piece * group : tail + (piece + 1) * group, :] = second[
                :, piece * columns : (piece + 1) * columns
            ]
        chosen = cots[:, :rows]
        for j in range(1, len(outs)):
            chosen = jnp.where(target == j, cots[:, j * rows : (j + 1) * rows], chosen)
        for piece in range(group // COT_ROWS):
            lanes = slice(piece * per, piece * per + rows)
            out[out.shape[0] - COT_ROWS :, lanes] = chosen[piece * COT_ROWS : (piece + 1) * COT_ROWS].astype(BF16)


def group_kernel(relations, own_ref, *refs):
    packs, out_ref = refs[:-1], refs[-1]
    rows = own_ref.shape[0]
    columns = packs[0].shape[1]
    tail = relations * rows
    wide = out_ref.shape[1] - relations * columns
    pieces = wide // columns
    group = (packs[0].shape[0] - tail - COT_ROWS) // pieces
    per = columns // (group // COT_ROWS)
    for k in range(relations):
        span = slice(k * columns, (k + 1) * columns)
        block = own_ref[:, span]
        for pack in packs[1:]:
            block = block + pack[k * rows : (k + 1) * rows, :].astype(F32)
        out_ref[:, span] = block.astype(BF16)
    cots = jnp.concatenate(
        [
            p[tail + pieces * group :, piece * per : piece * per + rows]
            for p in packs
            for piece in range(group // COT_ROWS)
        ],
        0,
    )
    for piece in range(pieces):
        first = tail + piece * group
        second = jnp.concatenate([p[first : first + group, :] for p in packs], 0)
        start = (relations + piece) * columns
        out_ref[:, start : start + columns] = matmul(cots, second, (0, 0)).astype(BF16)


def sum_kernel(parts_ref, one_ref, two_ref):
    total = jnp.sum(parts_ref[...].astype(F32), axis=0)
    start = 0
    for ref in (one_ref, two_ref):
        wide = ref.shape[2]
        for k in range(ref.shape[0]):
            ref[k] = total[:, start : start + wide]
            start += wide


def row_kernel(serve_ref, arrived_ref, grad_ref, square_ref):
    rows = lax.broadcasted_iota(jnp.int32, (LANES, serve_ref.shape[1]), 0)
    arrived = arrived_ref[...].reshape(serve_ref.shape[1], grad_ref.shape[1])
    for block in range(grad_ref.shape[0] // LANES):
        span = slice(block * LANES, (block + 1) * LANES)
        onehot = jnp.where(serve_ref[...] == rows + block * LANES, 1.0, 0.0).astype(BF16)
        grad = matmul(onehot, arrived)
        grad_ref[span, :] = grad
        square_ref[block : block + 1, :] = column_to_row(jnp.sum(grad * grad, axis=1, keepdims=True))


def update_kernel(columns, table_ref, grad_ref, accum_ref, mine_ref, other_ref, table_out, accum_out):
    accum = accum_ref[...] + (mine_ref[...] + other_ref[...]) / columns
    accum_out[...] = accum
    inverse = lax.rsqrt(accum)
    for block in range(accum.shape[0]):
        span = slice(block * LANES, (block + 1) * LANES)
        scale = row_to_column(inverse[block : block + 1, :])
        table_out[span, :] = table_ref[span, :] - LEARNING_RATE * grad_ref[span, :] * scale


def shift(array, axis, by):
    size = lax.axis_size(axis)
    return lax.ppermute(array, axis, [(i, (i + by) % size) for i in range(size)])


LIMITS = {serve_kernel: 60, index_kernel: 60, first_kernel: 60, hidden_kernel: 60}
COSTS = {update_kernel: 0, group_kernel: 0, row_kernel: 0}


def body(
    table,
    accum,
    serve_rows,
    seed_slot,
    hop1_slot,
    hop2_slot,
    hop1_rel,
    hop2_rel,
    cotangent,
    w_first,
    w_second,
):
    everyone = ("dp", "y", "z")
    owners = lax.axis_size(everyone)
    table_rows, columns = table.shape
    slots = serve_rows.shape[1]
    seeds, fanout = hop1_slot.shape
    fanout_two = hop2_slot.shape[2]
    nodes = seeds + seeds * fanout
    layers, hidden_units = w_second.shape[:2]
    half = hidden_units // 2
    n_x, n_y, n_z = (lax.axis_size(a) for a in everyone)
    x, y = lax.axis_index("dp"), lax.axis_index("y")
    width = hidden_units // n_x

    blocks_shape = (owners, slots // owners, columns)
    parts = 4
    outgoing = call(
        serve_kernel,
        [shaped(blocks_shape, BF16)],
        (serve_rows, table.reshape(parts, table_rows // parts, columns)),
        scratch=[
            pltpu.VMEM((slots, table_rows), BF16),
            pltpu.VMEM((parts, table_rows // parts, columns), F32),
            pltpu.VMEM((table_rows, columns), BF16),
            pltpu.SemaphoreType.DMA((parts,)),
        ],
        hbm_in=(0,),
        raw_in=(1,),
    )[0]
    fetched = lax.all_to_all(outgoing, everyone, split_axis=0, concat_axis=0, tiled=True)

    key_one = hop1_slot + slots * hop1_rel
    key_two = (hop2_slot + slots * hop2_rel).reshape(seeds * fanout, fanout_two)
    seed_ids = jnp.arange(seeds, dtype=jnp.int32)[:, None]
    group = (seeds * (1 + hop1_rel) + seed_ids).reshape(-1, 1)
    spare = jnp.full((seeds * fanout, fanout - fanout_two), -1, jnp.int32)
    idx = jnp.concatenate(
        [
            jnp.concatenate([seed_slot[:, None], key_one, seed_ids], 1),
            jnp.concatenate([hop1_slot.reshape(-1, 1), key_two, spare, group], 1),
        ],
        0,
    )
    idx, place, y = lax.optimization_barrier((idx, jnp.stack([lax.axis_index("col"), x]), y))
    ct, c, inverse, member, back_hidden = call(
        index_kernel,
        [
            shaped((layers * nodes, slots), BF16),
            shaped((slots, layers * nodes), BF16),
            shaped((layers * nodes, LANES), F32),
            shaped((SEED_ROWS, nodes), BF16),
            shaped((nodes, hidden_units), F32),
        ],
        (idx, cotangent, w_second),
        scratch=[pltpu.VMEM((LANES, hidden_units), F32)],
        hbm_out=range(5),
    )

    layer_in, partial_pre = call(
        first_kernel,
        [shaped((layers * nodes, columns), BF16), shaped((nodes, hidden_units), F32)],
        (fetched, ct, w_first),
        scratch=[
            pltpu.VMEM((nodes, layers * columns), BF16),
            pltpu.VMEM((nodes, hidden_units), F32),
            pltpu.SemaphoreType.DMA((2,)),
        ],
        hbm_in=(0, 1, 2),
        hbm_out=(0,),
        hbm_raw=(1,),
    )
    other_pre = shift(partial_pre, "col", 1)
    layer_parts = [layer_in, shift(layer_in, "dp", n_x // 2)]

    pack_rows = nodes + half // width * SEED_ROWS + COT_ROWS
    pack_shape = (pack_rows, width)
    near_shape = ((pack_rows * width + layers * nodes * columns) // LANES, LANES)
    slot_grad, *packs = call(
        hidden_kernel,
        [shaped(blocks_shape, BF16)] + [shaped(near_shape if is_near(d, n_x) else pack_shape, BF16) for d in range(n_x)],
        (
            place,
            partial_pre,
            other_pre,
            back_hidden,
            member,
            inverse,
            cotangent,
            c,
            w_first,
            layer_in,
        ),
        smem=1,
        scratch=[
            pltpu.VMEM((n_x, *pack_shape), BF16),
            pltpu.VMEM((layers * nodes, columns), BF16),
            pltpu.SemaphoreType.DMA((n_x * (width + columns) // LANES,)),
        ],
        hbm_in=(1, 2, 3, 4, 5, 9, 8, 7),
        hbm_raw=range(1, 1 + n_x),
    )
    packs[n_x // 2], layer_parts = lax.optimization_barrier((packs[n_x // 2], layer_parts))
    packs = [packs[0]] + [shift(packs[d], "dp", d) for d in range(1, n_x)]
    arrived = lax.all_to_all(slot_grad, everyone, split_axis=0, concat_axis=0, tiled=True)

    block_rows = width // n_y
    group_rows = layers * block_rows + (layers * half // columns) * n_x * seeds + COT_ROWS
    own, *blocks = call(
        functools.partial(weight_kernel, n_x),
        [shaped((block_rows, layers * columns), F32)] + [shaped((group_rows, columns), BF16)] * n_y,
        (y.reshape(1), *layer_parts, *packs),
        smem=1,
        hbm_in=range(1, 3 + n_x),
        scratch=[pltpu.VMEM((layers, width, columns), F32)],
    )
    blocks = [blocks[0]] + [shift(blocks[d], "y", d) for d in range(1, n_y)]
    grad_columns = layers * (columns + half)
    grads = call(
        functools.partial(group_kernel, layers),
        [shaped((block_rows, grad_columns), BF16)],
        (own, *blocks),
    )[0]
    grads = grads.reshape(n_z, block_rows // n_z, grad_columns)
    grads = lax.all_to_all(grads, "z", split_axis=0, concat_axis=0, tiled=True)
    grad_one, grad_two = call(
        sum_kernel,
        [shaped((layers, block_rows // n_z, wide), F32) for wide in (columns, half)],
        (grads,),
    )
    grad_one, grad_two = grad_one.transpose(0, 2, 1), grad_two.transpose(0, 2, 1)

    row_grad, squares = call(
        row_kernel,
        [shaped((table_rows, columns), F32), shaped((table_rows // LANES, LANES), F32)],
        (serve_rows, arrived),
    )
    other_squares = shift(squares, "col", 1)
    new_table, new_accum = call(
        functools.partial(update_kernel, 2 * columns),
        [shaped((table_rows, columns), F32), shaped((table_rows // LANES, LANES), F32)],
        (table, row_grad, accum.reshape(-1, LANES), squares, other_squares),
    )
    return (new_table, new_accum.reshape(-1), grad_one, grad_two)


def solution(mesh):
    n_dp, n_table, n_col = (mesh.shape[a] for a in ("dp", "table", "col"))
    n_y = 4 if n_table % 4 == 0 and n_table > 4 else 2
    fine = Mesh(mesh.devices.reshape(n_dp, n_y, n_table // n_y, n_col), ("dp", "y", "z", "col"))
    rows = ("dp", "y", "z")
    placed = (
        P(rows, "col"),
        P(rows),
        P(rows, None),
        P(rows),
        P(rows, None),
        P(rows, None, None),
        P(rows, None),
        P(rows, None, None),
        P(rows, None),
        P(None, "col", None),
        P(),
    )
    return jax.shard_map(
        body,
        mesh=fine,
        in_specs=placed,
        out_specs=(P(rows, "col"), P(rows), P(None, "col", rows), P(None, "col", rows)),
        check_vma=False,
    )
```

```python
import functools
import jax
import jax.numpy as jnp
from jax import lax
from jax.experimental import pallas as pl
from jax.experimental.pallas import tpu as pltpu
from jax.sharding import Mesh
from jax.sharding import PartitionSpec as P

LEARNING_RATE = 0.1
BF16 = jnp.bfloat16
F32 = jnp.float32
LANES = 128
SEED_ROWS = 32
COT_ROWS = 16


def matmul(a, b, contract=(1, 0)):
    dims = (((contract[0],), (contract[1],)), ((), ()))
    return lax.dot_general(a, b, dims, preferred_element_type=F32)


def row_to_column(row):
    return jnp.transpose(jnp.broadcast_to(row, (LANES, LANES)))[:, 0:1]


def column_to_row(column):
    return jnp.transpose(jnp.broadcast_to(column, (LANES, LANES)))[0:1, :]


class Incoming:
    def __init__(self, source, buffer, semaphore):
        self.buffer, self.waiting = buffer, True
        self.shape = buffer.shape
        self.copy = pltpu.make_async_copy(source, buffer, semaphore)
        self.copy.start()

    def get(self):
        if self.waiting:
            self.copy.wait()
        self.waiting = False
        return self.buffer


class Outgoing:
    def __init__(self, target, buffer, semaphore):
        self.buffer = buffer
        self.copy = pltpu.make_async_copy(buffer, target, semaphore)

    def send(self):
        self.copy.start()


def call(kernel, outs, operands, smem=0, scratch=(), hbm_in=(), hbm_out=(), raw_in=(), hbm_raw=()):
    name = getattr(kernel, "func", kernel)
    limit, flops = LIMITS.get(name, 12), COSTS.get(name, 10**12)
    moved = sum(o.size * o.dtype.itemsize for o in list(operands) + list(outs))
    specs = [
        pl.BlockSpec(memory_space=pltpu.SMEM if i < smem else pltpu.HBM if i in hbm_in or i in raw_in else pltpu.VMEM)
        for i in range(len(operands))
    ]
    made = [
        pl.BlockSpec(memory_space=pltpu.HBM if i in hbm_out or i in hbm_raw else pltpu.VMEM)
        for i in range(len(outs))
    ]
    buffers = [pltpu.VMEM(operands[i].shape, operands[i].dtype) for i in hbm_in]
    buffers += [pltpu.VMEM(outs[i].shape, outs[i].dtype) for i in hbm_out]
    semaphores = [pltpu.SemaphoreType.DMA((len(buffers),))] if buffers else []

    def wrapped(*refs):
        refs = list(refs)
        if not buffers:
            kernel(*refs)
            return
        first = len(operands) + len(outs)
        held, sems = refs[first : first + len(buffers)], refs[first + len(buffers)]
        rest = refs[first + len(buffers) + 1 :]
        for j, i in enumerate(hbm_in):
            refs[i] = Incoming(refs[i], held[j], sems.at[j])
        leaving = []
        for j, i in enumerate(hbm_out, len(hbm_in)):
            place = len(operands) + i
            refs[place] = Outgoing(refs[place], held[j], sems.at[j])
            leaving.append(refs[place])
        kernel(*refs[:first], *rest)
        for out in leaving:
            out.copy.wait()

    return pl.pallas_call(
        wrapped,
        out_shape=tuple(outs),
        in_specs=specs,
        out_specs=tuple(made),
        scratch_shapes=buffers + semaphores + list(scratch),
        compiler_params=pltpu.CompilerParams(vmem_limit_bytes=limit * 1024 * 1024),
        cost_estimate=pl.CostEstimate(flops=flops, bytes_accessed=moved, transcendentals=0),
    )(*operands)


def shaped(shape, dtype):
    return jax.ShapeDtypeStruct(shape, dtype)


def serve_kernel(serve_ref, table_ref, out_ref, onehot, rows, whole, sems):
    parts = rows.shape[0]
    loads = [pltpu.make_async_copy(table_ref.at[i], rows.at[i], sems.at[i]) for i in range(parts)]
    for load in loads:
        load.start()
    serve = serve_ref.get()[...]
    lanes = lax.broadcasted_iota(jnp.int32, (LANES, onehot.shape[1]), 1)
    for block in range(serve.shape[1] // LANES):
        span = slice(block * LANES, (block + 1) * LANES)
        onehot[span, :] = jnp.where(row_to_column(serve[:, span]) == lanes, 1.0, 0.0).astype(BF16)
    for i, load in enumerate(loads):
        load.wait()
        whole[i * rows.shape[1] : (i + 1) * rows.shape[1], :] = rows[i].astype(BF16)
    out_ref[...] = matmul(onehot[...], whole[...]).astype(BF16).reshape(out_ref.shape)


def index_kernel(idx_ref, cot_ref, w2_ref, *refs):
    outs, spread = refs[:-1], refs[-1]
    ct_ref, c_ref, inv_ref, e_ref, back_ref = (o.buffer for o in outs)
    nodes = idx_ref.shape[0]
    slots = ct_ref.shape[1]
    seeds = cot_ref.shape[0]
    neighbours = idx_ref.shape[1] - 2
    lanes = lax.broadcasted_iota(jnp.int32, (nodes, 2 * slots), 1)
    idx = idx_ref[...]
    counts = jnp.zeros((nodes, 2 * slots), F32)
    for j in range(1, 1 + neighbours):
        counts = counts + jnp.where(idx[:, j : j + 1] == lanes, 1.0, 0.0)
    own = jnp.where(idx[:, 0:1] == lanes[:, :slots], 1.0, 0.0)
    parts = (own, counts[:, :slots], counts[:, slots:])
    spread[...] = jnp.zeros(spread.shape, F32)
    for k, part in enumerate(parts):
        span = slice(k * nodes, (k + 1) * nodes)
        ct_ref[span, :] = part.astype(BF16)
        c_ref[:, span] = jnp.transpose(part).astype(BF16)
        if k == 0:
            inverse = jnp.ones((nodes, 1), F32)
        else:
            inverse = 1.0 / jnp.maximum(jnp.sum(part, axis=1, keepdims=True), 1.0)
        inv_ref[span, :] = jnp.broadcast_to(inverse, (nodes, LANES))
        back = matmul(cot_ref[...], w2_ref[k], (1, 1))
        spread[k * seeds : (k + 1) * seeds, :] = back * inverse[:seeds]
    groups = lax.broadcasted_iota(jnp.int32, (nodes, LANES), 1)
    member = jnp.where(idx[:, neighbours + 1 : neighbours + 2] == groups, 1.0, 0.0)
    e_ref[...] = jnp.transpose(member)[:SEED_ROWS].astype(BF16)
    whole = spread[...]
    high = whole.astype(BF16)
    low = (whole - high.astype(F32)).astype(BF16)
    for out in outs[:-1]:
        out.send()
    back_ref[...] = matmul(member.astype(BF16), high) + matmul(member.astype(BF16), low)
    outs[-1].send()


def first_kernel(fetched_ref, ct_ref, w1_ref, layer_ref, partial_out, wide, partial_ref, sems):
    layers = w1_ref.shape[0]
    layer_out, layer_ref = layer_ref, layer_ref.buffer
    nodes = partial_ref.shape[0]
    fetched = fetched_ref.get()[...].reshape(ct_ref.shape[1], layer_ref.shape[1])
    ct_ref = ct_ref.get()
    ones = jnp.ones((ct_ref.shape[1], LANES), BF16)
    columns = layer_ref.shape[1]
    for k in range(layers):
        span = slice(k * nodes, (k + 1) * nodes)
        summed = matmul(ct_ref[span, :], fetched)
        inverse = 1.0 / jnp.maximum(matmul(ct_ref[span, :], ones)[:, 0:1], 1.0)
        layer = (summed * inverse).astype(BF16)
        layer_ref[span, :] = layer
        wide[:, k * columns : (k + 1) * columns] = layer
    layer_out.send()
    weights = w1_ref.get()[...].reshape(layers * columns, partial_ref.shape[1])
    half = partial_ref.shape[1] // 2
    copies = []
    for i in range(2):
        span = slice(i * half, (i + 1) * half)
        partial_ref[:, span] = matmul(wide[...], weights[:, span])
        copies.append(pltpu.make_async_copy(partial_ref.at[:, span], partial_out.at[:, span], sems.at[i]))
        copies[i].start()
    for copy in copies:
        copy.wait()


def hidden_kernel(place_ref, mine_ref, other_ref, back_ref, e_ref, inv_ref, cot_ref, c_ref, w1_ref, slot_ref, *refs):
    packs, (stage, scaled, sems) = refs[:-3], refs[-3:]
    nodes = mine_ref.shape[0]
    width = stage.shape[2]
    seeds = cot_ref.shape[0]
    layers = inv_ref.shape[0] // nodes
    values = mine_ref.get()[...] + other_ref.get()[...]
    back_ref, e_ref, inv_ref = back_ref.get(), e_ref.get(), inv_ref.get()
    sigma = jax.nn.sigmoid(values)
    hidden = (values * sigma).astype(BF16)
    slope = sigma * (1.0 + values * (1.0 - sigma))
    back = (back_ref[...] * slope).astype(BF16)
    scale = jnp.concatenate(
        [inv_ref[k * nodes : k * nodes + seeds, 0:1] for k in range(layers)]
        + [jnp.zeros((SEED_ROWS - layers * seeds, 1), F32)],
        0,
    )
    second = matmul(e_ref[...], hidden) * scale
    half = second.shape[1] // 2
    second = jnp.where(place_ref[0] == 0, second[:, :half], second[:, half:]).astype(BF16)
    cot = cot_ref[...].astype(F32)
    cot = jnp.concatenate([cot, jnp.zeros((COT_ROWS - seeds, cot.shape[1]), F32)], 0).astype(BF16)
    for j in range(len(packs)):
        span = slice(j * width, (j + 1) * width)
        stage[j, :nodes, :] = back[:, span]
        for part in range(half // width):
            first = nodes + part * SEED_ROWS
            stage[j, first : first + SEED_ROWS, :] = second[:, part * width : (part + 1) * width]
        first = nodes + half // width * SEED_ROWS
        stage[j, first : first + COT_ROWS, :] = cot[:, span]
    copies = [
        pltpu.make_async_copy(stage.at[lax.rem(place_ref[1] + d, len(packs))], pack, sems.at[d])
        for d, pack in enumerate(packs)
    ]
    for copy in copies:
        copy.start()
    columns = w1_ref.shape[1]
    back_in = matmul(back, w1_ref.get()[...].reshape(layers * columns, back.shape[1]), (1, 1))
    for k in range(layers):
        span = slice(k * nodes, (k + 1) * nodes)
        scaled[span, :] = (back_in[:, k * columns : (k + 1) * columns] * inv_ref[span, 0:1]).astype(BF16)
    slot_ref[...] = matmul(c_ref.get()[...], scaled[...]).astype(BF16).reshape(slot_ref.shape)
    for copy in copies:
        copy.wait()


def weight_kernel(count, place_ref, *refs):
    layer_refs, pack_refs = refs[:count], refs[count : 2 * count]
    own_ref, outs, total = refs[2 * count], refs[2 * count + 1 : -1], refs[-1]
    pack_rows, width = pack_refs[0].shape
    layer_rows, columns = layer_refs[0].shape
    layer_parts = [r.get()[...] for r in layer_refs]
    packs = [r.get()[...] for r in pack_refs]
    nodes = LANES
    relations = layer_rows // nodes
    rows = own_ref.shape[0]
    left = jnp.concatenate([p[:nodes, :] for p in packs], 0)
    for k in range(relations):
        right = jnp.concatenate([r[k * nodes : (k + 1) * nodes, :] for r in layer_parts], 0)
        total[k] = matmul(left, right, (0, 0))
    pieces = (pack_rows - nodes - COT_ROWS) // SEED_ROWS
    half = pieces * width
    seeds = SEED_ROWS // (relations + 1)
    first = nodes + pieces * SEED_ROWS
    cots = jnp.concatenate([p[first : first + COT_ROWS, :].astype(F32)[:seeds] for p in packs], 0)
    seconds = [
        jnp.concatenate(
            [p[nodes + part * SEED_ROWS : nodes + (part + 1) * SEED_ROWS, :].astype(F32) for part in range(pieces)],
            1,
        )
        for p in packs
    ]
    second = jnp.concatenate(
        [jnp.concatenate([s[k * seeds : (k + 1) * seeds] for s in seconds], 0) for k in range(relations)], 1
    ).astype(BF16)
    group = count * seeds
    per = columns // (group // COT_ROWS)
    tail = relations * rows
    for d, out in enumerate(outs):
        target = lax.rem(place_ref[0] + d, len(outs))
        start = pl.multiple_of(target * rows, rows)
        for k in range(relations):
            block = total[k, pl.ds(start, rows), :]
            if d == 0:
                own_ref[:, k * columns : (k + 1) * columns] = block
            else:
                out[k * rows : (k + 1) * rows, :] = block.astype(BF16)
        for piece in range(relations * half // columns):
            out[tail + piece * group : tail + (piece + 1) * group, :] = second[
                :, piece * columns : (piece + 1) * columns
            ]
        chosen = cots[:, :rows]
        for j in range(1, len(outs)):
            chosen = jnp.where(target == j, cots[:, j * rows : (j + 1) * rows], chosen)
        for piece in range(group // COT_ROWS):
            lanes = slice(piece * per, piece * per + rows)
            out[out.shape[0] - COT_ROWS :, lanes] = chosen[piece * COT_ROWS : (piece + 1) * COT_ROWS].astype(BF16)


def group_kernel(relations, own_ref, *refs):
    packs, out_ref = refs[:-1], refs[-1]
    rows = own_ref.shape[0]
    columns = packs[0].shape[1]
    tail = relations * rows
    wide = out_ref.shape[1] - relations * columns
    pieces = wide // columns
    group = (packs[0].shape[0] - tail - COT_ROWS) // pieces
    per = columns // (group // COT_ROWS)
    for k in range(relations):
        span = slice(k * columns, (k + 1) * columns)
        block = own_ref[:, span]
        for pack in packs[1:]:
            block = block + pack[k * rows : (k + 1) * rows, :].astype(F32)
        out_ref[:, span] = block.astype(BF16)
    cots = jnp.concatenate(
        [
            p[tail + pieces * group :, piece * per : piece * per + rows]
            for p in packs
            for piece in range(group // COT_ROWS)
        ],
        0,
    )
    for piece in range(pieces):
        first = tail + piece * group
        second = jnp.concatenate([p[first : first + group, :] for p in packs], 0)
        start = (relations + piece) * columns
        out_ref[:, start : start + columns] = matmul(cots, second, (0, 0)).astype(BF16)


def sum_kernel(parts_ref, one_ref, two_ref):
    total = jnp.sum(parts_ref[...].astype(F32), axis=0)
    start = 0
    for ref in (one_ref, two_ref):
        wide = ref.shape[2]
        for k in range(ref.shape[0]):
            ref[k] = total[:, start : start + wide]
            start += wide


def row_kernel(serve_ref, arrived_ref, grad_ref, square_ref):
    rows = lax.broadcasted_iota(jnp.int32, (LANES, serve_ref.shape[1]), 0)
    arrived = arrived_ref[...].reshape(serve_ref.shape[1], grad_ref.shape[1])
    for block in range(grad_ref.shape[0] // LANES):
        span = slice(block * LANES, (block + 1) * LANES)
        onehot = jnp.where(serve_ref[...] == rows + block * LANES, 1.0, 0.0).astype(BF16)
        grad = matmul(onehot, arrived)
        grad_ref[span, :] = grad
        square_ref[block : block + 1, :] = column_to_row(jnp.sum(grad * grad, axis=1, keepdims=True))


def update_kernel(columns, table_ref, grad_ref, accum_ref, mine_ref, other_ref, table_out, accum_out):
    accum = accum_ref[...] + (mine_ref[...] + other_ref[...]) / columns
    accum_out[...] = accum
    inverse = lax.rsqrt(accum)
    for block in range(accum.shape[0]):
        span = slice(block * LANES, (block + 1) * LANES)
        scale = row_to_column(inverse[block : block + 1, :])
        table_out[span, :] = table_ref[span, :] - LEARNING_RATE * grad_ref[span, :] * scale


def shift(array, axis, by):
    size = lax.axis_size(axis)
    return lax.ppermute(array, axis, [(i, (i + by) % size) for i in range(size)])


LIMITS = {serve_kernel: 60, index_kernel: 60, first_kernel: 60, hidden_kernel: 50}
COSTS = {update_kernel: 0, group_kernel: 0, row_kernel: 0}


def body(
    table,
    accum,
    serve_rows,
    seed_slot,
    hop1_slot,
    hop2_slot,
    hop1_rel,
    hop2_rel,
    cotangent,
    w_first,
    w_second,
):
    everyone = ("dp", "y", "z")
    owners = lax.axis_size(everyone)
    table_rows, columns = table.shape
    slots = serve_rows.shape[1]
    seeds, fanout = hop1_slot.shape
    fanout_two = hop2_slot.shape[2]
    nodes = seeds + seeds * fanout
    layers, hidden_units = w_second.shape[:2]
    half = hidden_units // 2
    n_x, n_y, n_z = (lax.axis_size(a) for a in everyone)
    x, y = lax.axis_index("dp"), lax.axis_index("y")
    width = hidden_units // n_x

    blocks_shape = (owners, slots // owners, columns)
    parts = 4
    outgoing = call(
        serve_kernel,
        [shaped(blocks_shape, BF16)],
        (serve_rows, table.reshape(parts, table_rows // parts, columns)),
        scratch=[
            pltpu.VMEM((slots, table_rows), BF16),
            pltpu.VMEM((parts, table_rows // parts, columns), F32),
            pltpu.VMEM((table_rows, columns), BF16),
            pltpu.SemaphoreType.DMA((parts,)),
        ],
        hbm_in=(0,),
        raw_in=(1,),
    )[0]
    fetched = lax.all_to_all(outgoing, everyone, split_axis=0, concat_axis=0, tiled=True)

    key_one = hop1_slot + slots * hop1_rel
    key_two = (hop2_slot + slots * hop2_rel).reshape(seeds * fanout, fanout_two)
    seed_ids = jnp.arange(seeds, dtype=jnp.int32)[:, None]
    group = (seeds * (1 + hop1_rel) + seed_ids).reshape(-1, 1)
    spare = jnp.full((seeds * fanout, fanout - fanout_two), -1, jnp.int32)
    idx = jnp.concatenate(
        [
            jnp.concatenate([seed_slot[:, None], key_one, seed_ids], 1),
            jnp.concatenate([hop1_slot.reshape(-1, 1), key_two, spare, group], 1),
        ],
        0,
    )
    idx, place, y = lax.optimization_barrier((idx, jnp.stack([lax.axis_index("col"), x]), y))
    ct, c, inverse, member, back_hidden = call(
        index_kernel,
        [
            shaped((layers * nodes, slots), BF16),
            shaped((slots, layers * nodes), BF16),
            shaped((layers * nodes, LANES), F32),
            shaped((SEED_ROWS, nodes), BF16),
            shaped((nodes, hidden_units), F32),
        ],
        (idx, cotangent, w_second),
        scratch=[pltpu.VMEM((LANES, hidden_units), F32)],
        hbm_out=range(5),
    )

    layer_in, partial_pre = call(
        first_kernel,
        [shaped((layers * nodes, columns), BF16), shaped((nodes, hidden_units), F32)],
        (fetched, ct, w_first),
        scratch=[
            pltpu.VMEM((nodes, layers * columns), BF16),
            pltpu.VMEM((nodes, hidden_units), F32),
            pltpu.SemaphoreType.DMA((2,)),
        ],
        hbm_in=(0, 1, 2),
        hbm_out=(0,),
        hbm_raw=(1,),
    )
    other_pre = shift(partial_pre, "col", 1)
    layer_parts = [layer_in, shift(layer_in, "dp", 1)]
    if n_x > 2:
        layer_parts.append(shift(layer_in, "dp", n_x - 1))

    pack_rows = nodes + half // width * SEED_ROWS + COT_ROWS
    pack_shape = (pack_rows, width)
    slot_grad, *packs = call(
        hidden_kernel,
        [shaped(blocks_shape, BF16)] + [shaped(pack_shape, BF16)] * n_x,
        (
            place,
            partial_pre,
            other_pre,
            back_hidden,
            member,
            inverse,
            cotangent,
            c,
            w_first,
        ),
        smem=1,
        scratch=[
            pltpu.VMEM((n_x, *pack_shape), BF16),
            pltpu.VMEM((layers * nodes, columns), BF16),
            pltpu.SemaphoreType.DMA((n_x,)),
        ],
        hbm_in=(1, 2, 3, 4, 5, 8, 7),
        hbm_raw=range(1, 1 + n_x),
    )
    packs[n_x // 2], layer_parts = lax.optimization_barrier((packs[n_x // 2], layer_parts))
    if n_x > 2:
        layer_parts.insert(2, shift(layer_parts[2], "dp", n_x - 1))
    packs = [packs[0]] + [shift(packs[d], "dp", d) for d in range(1, n_x)]
    arrived = lax.all_to_all(slot_grad, everyone, split_axis=0, concat_axis=0, tiled=True)

    block_rows = width // n_y
    group_rows = layers * block_rows + (layers * half // columns) * n_x * seeds + COT_ROWS
    own, *blocks = call(
        functools.partial(weight_kernel, n_x),
        [shaped((block_rows, layers * columns), F32)] + [shaped((group_rows, columns), BF16)] * n_y,
        (y.reshape(1), *layer_parts, *packs),
        smem=1,
        hbm_in=range(1, 1 + 2 * n_x),
        scratch=[pltpu.VMEM((layers, width, columns), F32)],
    )
    blocks = [blocks[0]] + [shift(blocks[d], "y", d) for d in range(1, n_y)]
    grad_columns = layers * (columns + half)
    grads = call(
        functools.partial(group_kernel, layers),
        [shaped((block_rows, grad_columns), BF16)],
        (own, *blocks),
    )[0]
    grads = grads.reshape(n_z, block_rows // n_z, grad_columns)
    grads = lax.all_to_all(grads, "z", split_axis=0, concat_axis=0, tiled=True)
    grad_one, grad_two = call(
        sum_kernel,
        [shaped((layers, block_rows // n_z, wide), F32) for wide in (columns, half)],
        (grads,),
    )
    grad_one, grad_two = grad_one.transpose(0, 2, 1), grad_two.transpose(0, 2, 1)

    row_grad, squares = call(
        row_kernel,
        [shaped((table_rows, columns), F32), shaped((table_rows // LANES, LANES), F32)],
        (serve_rows, arrived),
    )
    other_squares = shift(squares, "col", 1)
    new_table, new_accum = call(
        functools.partial(update_kernel, 2 * columns),
        [shaped((table_rows, columns), F32), shaped((table_rows // LANES, LANES), F32)],
        (table, row_grad, accum.reshape(-1, LANES), squares, other_squares),
    )
    return (new_table, new_accum.reshape(-1), grad_one, grad_two)


def solution(mesh):
    n_dp, n_table, n_col = (mesh.shape[a] for a in ("dp", "table", "col"))
    n_y = 4 if n_table % 4 == 0 and n_table > 4 else 2
    fine = Mesh(mesh.devices.reshape(n_dp, n_y, n_table // n_y, n_col), ("dp", "y", "z", "col"))
    rows = ("dp", "y", "z")
    placed = (
        P(rows, "col"),
        P(rows),
        P(rows, None),
        P(rows),
        P(rows, None),
        P(rows, None, None),
        P(rows, None),
        P(rows, None, None),
        P(rows, None),
        P(None, "col", None),
        P(),
    )
    return jax.shard_map(
        body,
        mesh=fine,
        in_specs=placed,
        out_specs=(P(rows, "col"), P(rows), P(None, "col", rows), P(None, "col", rows)),
        check_vma=False,
    )
```

```python
import functools
import jax
import jax.numpy as jnp
from jax import lax
from jax.experimental import pallas as pl
from jax.experimental.pallas import tpu as pltpu
from jax.sharding import Mesh
from jax.sharding import PartitionSpec as P

LEARNING_RATE = 0.1
BF16 = jnp.bfloat16
F32 = jnp.float32
LANES = 128
SEED_ROWS = 32
COT_ROWS = 16


def matmul(a, b, contract=(1, 0)):
    dims = (((contract[0],), (contract[1],)), ((), ()))
    return lax.dot_general(a, b, dims, preferred_element_type=F32)


def row_to_column(row):
    return jnp.transpose(jnp.broadcast_to(row, (LANES, LANES)))[:, 0:1]


def column_to_row(column):
    return jnp.transpose(jnp.broadcast_to(column, (LANES, LANES)))[0:1, :]


class Incoming:
    def __init__(self, source, buffer, semaphore):
        self.buffer, self.waiting = buffer, True
        self.shape = buffer.shape
        self.copy = pltpu.make_async_copy(source, buffer, semaphore)
        self.copy.start()

    def get(self):
        if self.waiting:
            self.copy.wait()
        self.waiting = False
        return self.buffer


class Outgoing:
    def __init__(self, target, buffer, semaphore):
        self.buffer = buffer
        self.copy = pltpu.make_async_copy(buffer, target, semaphore)

    def send(self):
        self.copy.start()


def call(kernel, outs, operands, smem=0, scratch=(), hbm_in=(), hbm_out=(), raw_in=(), hbm_raw=()):
    name = getattr(kernel, "func", kernel)
    limit, flops = LIMITS.get(name, 12), COSTS.get(name, 10**12)
    moved = sum(o.size * o.dtype.itemsize for o in list(operands) + list(outs))
    specs = [
        pl.BlockSpec(memory_space=pltpu.SMEM if i < smem else pltpu.HBM if i in hbm_in or i in raw_in else pltpu.VMEM)
        for i in range(len(operands))
    ]
    made = [
        pl.BlockSpec(memory_space=pltpu.HBM if i in hbm_out or i in hbm_raw else pltpu.VMEM)
        for i in range(len(outs))
    ]
    buffers = [pltpu.VMEM(operands[i].shape, operands[i].dtype) for i in hbm_in]
    buffers += [pltpu.VMEM(outs[i].shape, outs[i].dtype) for i in hbm_out]
    semaphores = [pltpu.SemaphoreType.DMA((len(buffers),))] if buffers else []

    def wrapped(*refs):
        refs = list(refs)
        if not buffers:
            kernel(*refs)
            return
        first = len(operands) + len(outs)
        held, sems = refs[first : first + len(buffers)], refs[first + len(buffers)]
        rest = refs[first + len(buffers) + 1 :]
        for j, i in enumerate(hbm_in):
            refs[i] = Incoming(refs[i], held[j], sems.at[j])
        leaving = []
        for j, i in enumerate(hbm_out, len(hbm_in)):
            place = len(operands) + i
            refs[place] = Outgoing(refs[place], held[j], sems.at[j])
            leaving.append(refs[place])
        kernel(*refs[:first], *rest)
        for out in leaving:
            out.copy.wait()

    return pl.pallas_call(
        wrapped,
        out_shape=tuple(outs),
        in_specs=specs,
        out_specs=tuple(made),
        scratch_shapes=buffers + semaphores + list(scratch),
        compiler_params=pltpu.CompilerParams(vmem_limit_bytes=int(limit * 1024 * 1024)),
        cost_estimate=pl.CostEstimate(flops=flops, bytes_accessed=moved, transcendentals=0),
    )(*operands)


def is_near(distance, count):
    return distance not in (0, count // 2)


def shaped(shape, dtype):
    return jax.ShapeDtypeStruct(shape, dtype)


def serve_kernel(serve_ref, table_ref, out_ref, onehot, rows, whole, sems):
    parts = rows.shape[0]
    loads = [pltpu.make_async_copy(table_ref.at[i], rows.at[i], sems.at[i]) for i in range(parts)]
    for load in loads:
        load.start()
    serve = serve_ref.get()[...]
    lanes = lax.broadcasted_iota(jnp.int32, (LANES, onehot.shape[1]), 1)
    for block in range(serve.shape[1] // LANES):
        span = slice(block * LANES, (block + 1) * LANES)
        onehot[span, :] = jnp.where(row_to_column(serve[:, span]) == lanes, 1.0, 0.0).astype(BF16)
    for i, load in enumerate(loads):
        load.wait()
        whole[i * rows.shape[1] : (i + 1) * rows.shape[1], :] = rows[i].astype(BF16)
    out_ref[...] = matmul(onehot[...], whole[...]).astype(BF16).reshape(out_ref.shape)


def index_kernel(idx_ref, cot_ref, w2_ref, *refs):
    outs, spread = refs[:-1], refs[-1]
    ct_ref, c_ref, inv_ref, e_ref, back_ref = (o.buffer for o in outs)
    nodes = idx_ref.shape[0]
    slots = ct_ref.shape[1]
    seeds = cot_ref.shape[0]
    neighbours = idx_ref.shape[1] - 2
    lanes = lax.broadcasted_iota(jnp.int32, (nodes, 2 * slots), 1)
    idx = idx_ref[...]
    counts = jnp.zeros((nodes, 2 * slots), F32)
    for j in range(1, 1 + neighbours):
        counts = counts + jnp.where(idx[:, j : j + 1] == lanes, 1.0, 0.0)
    own = jnp.where(idx[:, 0:1] == lanes[:, :slots], 1.0, 0.0)
    parts = (own, counts[:, :slots], counts[:, slots:])
    spread[...] = jnp.zeros(spread.shape, F32)
    for k, part in enumerate(parts):
        span = slice(k * nodes, (k + 1) * nodes)
        ct_ref[span, :] = part.astype(BF16)
        c_ref[:, span] = jnp.transpose(part).astype(BF16)
        if k == 0:
            inverse = jnp.ones((nodes, 1), F32)
        else:
            inverse = 1.0 / jnp.maximum(jnp.sum(part, axis=1, keepdims=True), 1.0)
        inv_ref[span, :] = jnp.broadcast_to(inverse, (nodes, LANES))
        back = matmul(cot_ref[...], w2_ref[k], (1, 1))
        spread[k * seeds : (k + 1) * seeds, :] = back * inverse[:seeds]
    groups = lax.broadcasted_iota(jnp.int32, (nodes, LANES), 1)
    member = jnp.where(idx[:, neighbours + 1 : neighbours + 2] == groups, 1.0, 0.0)
    e_ref[...] = jnp.transpose(member)[:SEED_ROWS].astype(BF16)
    whole = spread[...]
    high = whole.astype(BF16)
    low = (whole - high.astype(F32)).astype(BF16)
    for out in outs[:-1]:
        out.send()
    back_ref[...] = matmul(member.astype(BF16), high) + matmul(member.astype(BF16), low)
    outs[-1].send()


def first_kernel(fetched_ref, ct_ref, w1_ref, layer_ref, partial_out, wide, partial_ref, sems):
    layers = w1_ref.shape[0]
    layer_out, layer_ref = layer_ref, layer_ref.buffer
    nodes = partial_ref.shape[0]
    fetched = fetched_ref.get()[...].reshape(ct_ref.shape[1], layer_ref.shape[1])
    ct_ref = ct_ref.get()
    ones = jnp.ones((ct_ref.shape[1], LANES), BF16)
    columns = layer_ref.shape[1]
    for k in range(layers):
        span = slice(k * nodes, (k + 1) * nodes)
        summed = matmul(ct_ref[span, :], fetched)
        inverse = 1.0 / jnp.maximum(matmul(ct_ref[span, :], ones)[:, 0:1], 1.0)
        layer = (summed * inverse).astype(BF16)
        layer_ref[span, :] = layer
        wide[:, k * columns : (k + 1) * columns] = layer
    layer_out.send()
    weights = w1_ref.get()[...].reshape(layers * columns, partial_ref.shape[1])
    half = partial_ref.shape[1] // 2
    copies = []
    for i in range(2):
        span = slice(i * half, (i + 1) * half)
        partial_ref[:, span] = matmul(wide[...], weights[:, span])
        copies.append(pltpu.make_async_copy(partial_ref.at[:, span], partial_out.at[:, span], sems.at[i]))
        copies[i].start()
    for copy in copies:
        copy.wait()


def hidden_kernel(place_ref, mine_ref, other_ref, back_ref, e_ref, inv_ref, cot_ref, c_ref, w1_ref, layer_ref, slot_ref, *refs):
    packs, (stage, scaled, sems) = refs[:-3], refs[-3:]
    nodes = mine_ref.shape[0]
    width = stage.shape[2]
    seeds = cot_ref.shape[0]
    layers = inv_ref.shape[0] // nodes
    values = mine_ref.get()[...] + other_ref.get()[...]
    back_ref, e_ref, inv_ref = back_ref.get(), e_ref.get(), inv_ref.get()
    sigma = jax.nn.sigmoid(values)
    hidden = (values * sigma).astype(BF16)
    slope = sigma * (1.0 + values * (1.0 - sigma))
    back = (back_ref[...] * slope).astype(BF16)
    scale = jnp.concatenate(
        [inv_ref[k * nodes : k * nodes + seeds, 0:1] for k in range(layers)]
        + [jnp.zeros((SEED_ROWS - layers * seeds, 1), F32)],
        0,
    )
    second = matmul(e_ref[...], hidden) * scale
    half = second.shape[1] // 2
    second = jnp.where(place_ref[0] == 0, second[:, :half], second[:, half:]).astype(BF16)
    cot = cot_ref[...].astype(F32)
    cot = jnp.concatenate([cot, jnp.zeros((COT_ROWS - seeds, cot.shape[1]), F32)], 0).astype(BF16)
    for j in range(len(packs)):
        span = slice(j * width, (j + 1) * width)
        stage[j, :nodes, :] = back[:, span]
        for part in range(half // width):
            first = nodes + part * SEED_ROWS
            stage[j, first : first + SEED_ROWS, :] = second[:, part * width : (part + 1) * width]
        first = nodes + half // width * SEED_ROWS
        stage[j, first : first + COT_ROWS, :] = cot[:, span]
    moves = []
    for d, pack in enumerate(packs):
        chosen = stage.at[lax.rem(place_ref[1] + d, len(packs))]
        if not is_near(d, len(packs)):
            moves.append((chosen, pack))
            continue
        start = 0
        for source in (chosen, layer_ref.get()):
            rows, wide = source.shape
            for lane in range(0, wide, LANES):
                moves.append((source.at[:, lane : lane + LANES], pack.at[start : start + rows, :]))
                start += rows
    layer_ref.get()
    copies = [pltpu.make_async_copy(source, target, sems.at[i]) for i, (source, target) in enumerate(moves)]
    for copy in copies:
        copy.start()
    columns = w1_ref.shape[1]
    back_in = matmul(back, w1_ref.get()[...].reshape(layers * columns, back.shape[1]), (1, 1))
    for k in range(layers):
        span = slice(k * nodes, (k + 1) * nodes)
        scaled[span, :] = (back_in[:, k * columns : (k + 1) * columns] * inv_ref[span, 0:1]).astype(BF16)
    slot_ref[...] = matmul(c_ref.get()[...], scaled[...]).astype(BF16).reshape(slot_ref.shape)
    for copy in copies:
        copy.wait()


def weight_kernel(count, place_ref, *refs):
    layer_refs, pack_refs = refs[:2], refs[2 : 2 + count]
    own_ref, second_ref, outs, total = refs[2 + count], refs[3 + count], refs[4 + count : -1], refs[-1]
    pack_rows, width = pack_refs[0].shape
    layer_rows, columns = layer_refs[0].shape
    layer_parts, packs = [], []
    for d, ref in enumerate(pack_refs):
        if not is_near(d, count):
            packs.append(ref.get()[...])
            layer_parts.append(layer_refs[min(d, 1)].get()[...])
            continue
        near, start = ref.get()[...], 0
        for rows, wide, made in ((pack_rows, width, packs), (layer_rows, columns, layer_parts)):
            lanes = [near[start + i * rows : start + (i + 1) * rows] for i in range(wide // LANES)]
            made.append(jnp.concatenate(lanes, 1))
            start += rows * len(lanes)
    nodes = LANES
    relations = layer_rows // nodes
    rows = own_ref.shape[0]
    left = jnp.concatenate([p[:nodes, :] for p in packs], 0)
    for k in range(relations):
        right = jnp.concatenate([r[k * nodes : (k + 1) * nodes, :] for r in layer_parts], 0)
        total[k] = matmul(left, right, (0, 0))
    pieces = (pack_rows - nodes - COT_ROWS) // SEED_ROWS
    half = pieces * width
    seeds = SEED_ROWS // (relations + 1)
    first = nodes + pieces * SEED_ROWS
    cots = jnp.concatenate([p[first : first + COT_ROWS, :].astype(F32)[:seeds] for p in packs], 0)
    seconds = [
        jnp.concatenate(
            [p[nodes + part * SEED_ROWS : nodes + (part + 1) * SEED_ROWS, :].astype(F32) for part in range(pieces)],
            1,
        )
        for p in packs
    ]
    second = jnp.concatenate(
        [jnp.concatenate([s[k * seeds : (k + 1) * seeds] for s in seconds], 0) for k in range(relations)], 1
    ).astype(BF16)
    group = count * seeds
    per = columns // (group // COT_ROWS)
    for piece in range(relations * half // columns):
        second_ref[piece * group : (piece + 1) * group, :] = second[:, piece * columns : (piece + 1) * columns]
    for d, out in enumerate(outs):
        target = lax.rem(place_ref[0] + d, len(outs))
        start = pl.multiple_of(target * rows, rows)
        for k in range(relations):
            block = total[k, pl.ds(start, rows), :]
            if d == 0:
                own_ref[:, k * columns : (k + 1) * columns] = block
            else:
                out[k * rows : (k + 1) * rows, :] = block.astype(BF16)
        chosen = cots[:, :rows]
        for j in range(1, len(outs)):
            chosen = jnp.where(target == j, cots[:, j * rows : (j + 1) * rows], chosen)
        for piece in range(group // COT_ROWS):
            lanes = slice(piece * per, piece * per + rows)
            out[out.shape[0] - COT_ROWS :, lanes] = chosen[piece * COT_ROWS : (piece + 1) * COT_ROWS].astype(BF16)


def group_kernel(relations, own_ref, *refs):
    count = len(refs) // 2
    packs, seconds, out_ref = refs[:count], refs[count:-1], refs[-1]
    rows = own_ref.shape[0]
    columns = packs[0].shape[1]
    tail = relations * rows
    wide = out_ref.shape[1] - relations * columns
    pieces = wide // columns
    group = seconds[0].shape[0] // pieces
    per = columns // (group // COT_ROWS)
    for k in range(relations):
        span = slice(k * columns, (k + 1) * columns)
        block = own_ref[:, span]
        for pack in packs[1:]:
            block = block + pack[k * rows : (k + 1) * rows, :].astype(F32)
        out_ref[:, span] = block.astype(BF16)
    cots = jnp.concatenate(
        [
            p[tail:, piece * per : piece * per + rows]
            for p in packs
            for piece in range(group // COT_ROWS)
        ],
        0,
    )
    for piece in range(pieces):
        first = piece * group
        second = jnp.concatenate([p[first : first + group, :] for p in seconds], 0)
        start = (relations + piece) * columns
        out_ref[:, start : start + columns] = matmul(cots, second, (0, 0)).astype(BF16)


def sum_kernel(parts_ref, one_ref, two_ref):
    total = jnp.sum(parts_ref[...].astype(F32), axis=0)
    start = 0
    for ref in (one_ref, two_ref):
        wide = ref.shape[2]
        for k in range(ref.shape[0]):
            ref[k] = total[:, start : start + wide]
            start += wide


def row_kernel(serve_ref, arrived_ref, grad_ref, square_ref):
    rows = lax.broadcasted_iota(jnp.int32, (LANES, serve_ref.shape[1]), 0)
    arrived = arrived_ref[...].reshape(serve_ref.shape[1], grad_ref.shape[1])
    for block in range(grad_ref.shape[0] // LANES):
        span = slice(block * LANES, (block + 1) * LANES)
        onehot = jnp.where(serve_ref[...] == rows + block * LANES, 1.0, 0.0).astype(BF16)
        grad = matmul(onehot, arrived)
        grad_ref[span, :] = grad
        square_ref[block : block + 1, :] = column_to_row(jnp.sum(grad * grad, axis=1, keepdims=True))


def update_kernel(columns, table_ref, grad_ref, accum_ref, mine_ref, other_ref, table_out, accum_out):
    accum = accum_ref[...] + (mine_ref[...] + other_ref[...]) / columns
    accum_out[...] = accum
    inverse = lax.rsqrt(accum)
    for block in range(accum.shape[0]):
        span = slice(block * LANES, (block + 1) * LANES)
        scale = row_to_column(inverse[block : block + 1, :])
        table_out[span, :] = table_ref[span, :] - LEARNING_RATE * grad_ref[span, :] * scale


def shift(array, axis, by):
    size = lax.axis_size(axis)
    return lax.ppermute(array, axis, [(i, (i + by) % size) for i in range(size)])


LIMITS = {serve_kernel: 60, index_kernel: 60, first_kernel: 60, hidden_kernel: 51.5}
COSTS = {update_kernel: 0, group_kernel: 0, row_kernel: 0}


def body(
    table,
    accum,
    serve_rows,
    seed_slot,
    hop1_slot,
    hop2_slot,
    hop1_rel,
    hop2_rel,
    cotangent,
    w_first,
    w_second,
):
    everyone = ("dp", "y", "z")
    owners = lax.axis_size(everyone)
    table_rows, columns = table.shape
    slots = serve_rows.shape[1]
    seeds, fanout = hop1_slot.shape
    fanout_two = hop2_slot.shape[2]
    nodes = seeds + seeds * fanout
    layers, hidden_units = w_second.shape[:2]
    half = hidden_units // 2
    n_x, n_y, n_z = (lax.axis_size(a) for a in everyone)
    x, y = lax.axis_index("dp"), lax.axis_index("y")
    width = hidden_units // n_x

    blocks_shape = (owners, slots // owners, columns)
    parts = 4
    outgoing = call(
        serve_kernel,
        [shaped(blocks_shape, BF16)],
        (serve_rows, table.reshape(parts, table_rows // parts, columns)),
        scratch=[
            pltpu.VMEM((slots, table_rows), BF16),
            pltpu.VMEM((parts, table_rows // parts, columns), F32),
            pltpu.VMEM((table_rows, columns), BF16),
            pltpu.SemaphoreType.DMA((parts,)),
        ],
        hbm_in=(0,),
        raw_in=(1,),
    )[0]
    fetched = lax.all_to_all(outgoing, everyone, split_axis=0, concat_axis=0, tiled=True)

    key_one = hop1_slot + slots * hop1_rel
    key_two = (hop2_slot + slots * hop2_rel).reshape(seeds * fanout, fanout_two)
    seed_ids = jnp.arange(seeds, dtype=jnp.int32)[:, None]
    group = (seeds * (1 + hop1_rel) + seed_ids).reshape(-1, 1)
    spare = jnp.full((seeds * fanout, fanout - fanout_two), -1, jnp.int32)
    idx = jnp.concatenate(
        [
            jnp.concatenate([seed_slot[:, None], key_one, seed_ids], 1),
            jnp.concatenate([hop1_slot.reshape(-1, 1), key_two, spare, group], 1),
        ],
        0,
    )
    idx, place, y = lax.optimization_barrier((idx, jnp.stack([lax.axis_index("col"), x]), y))
    ct, c, inverse, member, back_hidden = call(
        index_kernel,
        [
            shaped((layers * nodes, slots), BF16),
            shaped((slots, layers * nodes), BF16),
            shaped((layers * nodes, LANES), F32),
            shaped((SEED_ROWS, nodes), BF16),
            shaped((nodes, hidden_units), F32),
        ],
        (idx, cotangent, w_second),
        scratch=[pltpu.VMEM((LANES, hidden_units), F32)],
        hbm_out=range(5),
    )

    layer_in, partial_pre = call(
        first_kernel,
        [shaped((layers * nodes, columns), BF16), shaped((nodes, hidden_units), F32)],
        (fetched, ct, w_first),
        scratch=[
            pltpu.VMEM((nodes, layers * columns), BF16),
            pltpu.VMEM((nodes, hidden_units), F32),
            pltpu.SemaphoreType.DMA((2,)),
        ],
        hbm_in=(0, 1, 2),
        hbm_out=(0,),
        hbm_raw=(1,),
    )
    other_pre = shift(partial_pre, "col", 1)
    layer_parts = [layer_in, shift(layer_in, "dp", n_x // 2)]

    pack_rows = nodes + half // width * SEED_ROWS + COT_ROWS
    pack_shape = (pack_rows, width)
    near_shape = ((pack_rows * width + layers * nodes * columns) // LANES, LANES)
    slot_grad, *packs = call(
        hidden_kernel,
        [shaped(blocks_shape, BF16)] + [shaped(near_shape if is_near(d, n_x) else pack_shape, BF16) for d in range(n_x)],
        (
            place,
            partial_pre,
            other_pre,
            back_hidden,
            member,
            inverse,
            cotangent,
            c,
            w_first,
            layer_in,
        ),
        smem=1,
        scratch=[
            pltpu.VMEM((n_x, *pack_shape), BF16),
            pltpu.VMEM((layers * nodes, columns), BF16),
            pltpu.SemaphoreType.DMA((n_x * (width + columns) // LANES,)),
        ],
        hbm_in=(1, 2, 3, 4, 5, 9, 8, 7),
        hbm_raw=range(1, 1 + n_x),
    )
    packs[n_x // 2], layer_parts = lax.optimization_barrier((packs[n_x // 2], layer_parts))
    packs = [packs[0]] + [shift(packs[d], "dp", d) for d in range(1, n_x)]
    arrived = lax.all_to_all(slot_grad, everyone, split_axis=0, concat_axis=0, tiled=True)

    block_rows = width // n_y
    group_rows = layers * block_rows + COT_ROWS
    second_rows = (layers * half // columns) * n_x * seeds
    own, second, *blocks = call(
        functools.partial(weight_kernel, n_x),
        [shaped((block_rows, layers * columns), F32), shaped((second_rows, columns), BF16)]
        + [shaped((group_rows, columns), BF16)] * n_y,
        (y.reshape(1), *layer_parts, *packs),
        smem=1,
        hbm_in=range(1, 3 + n_x),
        scratch=[pltpu.VMEM((layers, width, columns), F32)],
    )
    seconds = [second, shift(second, "y", 1)]
    if n_y > 2:
        last = shift(second, "y", n_y - 1)
        seconds += [shift(last, "y", n_y - 1), last]
    blocks = [blocks[0]] + [shift(blocks[d], "y", d) for d in range(1, n_y)]
    grad_columns = layers * (columns + half)
    grads = call(
        functools.partial(group_kernel, layers),
        [shaped((block_rows, grad_columns), BF16)],
        (own, *blocks, *seconds),
    )[0]
    grads = grads.reshape(n_z, block_rows // n_z, grad_columns)
    grads = lax.all_to_all(grads, "z", split_axis=0, concat_axis=0, tiled=True)
    grad_one, grad_two = call(
        sum_kernel,
        [shaped((layers, block_rows // n_z, wide), F32) for wide in (columns, half)],
        (grads,),
    )
    grad_one, grad_two = grad_one.transpose(0, 2, 1), grad_two.transpose(0, 2, 1)

    row_grad, squares = call(
        row_kernel,
        [shaped((table_rows, columns), F32), shaped((table_rows // LANES, LANES), F32)],
        (serve_rows, arrived),
    )
    other_squares = shift(squares, "col", 1)
    new_table, new_accum = call(
        functools.partial(update_kernel, 2 * columns),
        [shaped((table_rows, columns), F32), shaped((table_rows // LANES, LANES), F32)],
        (table, row_grad, accum.reshape(-1, LANES), squares, other_squares),
    )
    return (new_table, new_accum.reshape(-1), grad_one, grad_two)


def solution(mesh):
    n_dp, n_table, n_col = (mesh.shape[a] for a in ("dp", "table", "col"))
    n_y = 4 if n_table % 4 == 0 and n_table > 4 else 2
    fine = Mesh(mesh.devices.reshape(n_dp, n_y, n_table // n_y, n_col), ("dp", "y", "z", "col"))
    rows = ("dp", "y", "z")
    placed = (
        P(rows, "col"),
        P(rows),
        P(rows, None),
        P(rows),
        P(rows, None),
        P(rows, None, None),
        P(rows, None),
        P(rows, None, None),
        P(rows, None),
        P(None, "col", None),
        P(),
    )
    return jax.shard_map(
        body,
        mesh=fine,
        in_specs=placed,
        out_specs=(P(rows, "col"), P(rows), P(None, "col", rows), P(None, "col", rows)),
        check_vma=False,
    )
```

```python
import functools
import jax
import jax.numpy as jnp
from jax import lax
from jax.experimental import pallas as pl
from jax.experimental.pallas import tpu as pltpu
from jax.sharding import Mesh
from jax.sharding import PartitionSpec as P

LEARNING_RATE = 0.1
BF16 = jnp.bfloat16
F32 = jnp.float32
LANES = 128
SEED_ROWS = 32
COT_ROWS = 16


def matmul(a, b, contract=(1, 0)):
    dims = (((contract[0],), (contract[1],)), ((), ()))
    return lax.dot_general(a, b, dims, preferred_element_type=F32)


def row_to_column(row):
    return jnp.transpose(jnp.broadcast_to(row, (LANES, LANES)))[:, 0:1]


def column_to_row(column):
    return jnp.transpose(jnp.broadcast_to(column, (LANES, LANES)))[0:1, :]


class Incoming:
    def __init__(self, source, buffer, semaphore):
        self.buffer, self.waiting = buffer, True
        self.shape = buffer.shape
        self.copy = pltpu.make_async_copy(source, buffer, semaphore)
        self.copy.start()

    def get(self):
        if self.waiting:
            self.copy.wait()
        self.waiting = False
        return self.buffer


class Outgoing:
    def __init__(self, target, buffer, semaphore):
        self.buffer = buffer
        self.copy = pltpu.make_async_copy(buffer, target, semaphore)

    def send(self):
        self.copy.start()


def call(kernel, outs, operands, smem=0, scratch=(), hbm_in=(), hbm_out=(), raw_in=(), hbm_raw=()):
    name = getattr(kernel, "func", kernel)
    limit, flops = LIMITS.get(name, 12), COSTS.get(name, 10**12)
    moved = sum(o.size * o.dtype.itemsize for o in list(operands) + list(outs))
    specs = [
        pl.BlockSpec(memory_space=pltpu.SMEM if i < smem else pltpu.HBM if i in hbm_in or i in raw_in else pltpu.VMEM)
        for i in range(len(operands))
    ]
    made = [
        pl.BlockSpec(memory_space=pltpu.HBM if i in hbm_out or i in hbm_raw else pltpu.VMEM)
        for i in range(len(outs))
    ]
    buffers = [pltpu.VMEM(operands[i].shape, operands[i].dtype) for i in hbm_in]
    buffers += [pltpu.VMEM(outs[i].shape, outs[i].dtype) for i in hbm_out]
    semaphores = [pltpu.SemaphoreType.DMA((len(buffers),))] if buffers else []

    def wrapped(*refs):
        refs = list(refs)
        if not buffers:
            kernel(*refs)
            return
        first = len(operands) + len(outs)
        held, sems = refs[first : first + len(buffers)], refs[first + len(buffers)]
        rest = refs[first + len(buffers) + 1 :]
        for j, i in enumerate(hbm_in):
            refs[i] = Incoming(refs[i], held[j], sems.at[j])
        leaving = []
        for j, i in enumerate(hbm_out, len(hbm_in)):
            place = len(operands) + i
            refs[place] = Outgoing(refs[place], held[j], sems.at[j])
            leaving.append(refs[place])
        kernel(*refs[:first], *rest)
        for out in leaving:
            out.copy.wait()

    return pl.pallas_call(
        wrapped,
        out_shape=tuple(outs),
        in_specs=specs,
        out_specs=tuple(made),
        scratch_shapes=buffers + semaphores + list(scratch),
        compiler_params=pltpu.CompilerParams(vmem_limit_bytes=int(limit * 1024 * 1024)),
        cost_estimate=pl.CostEstimate(flops=flops, bytes_accessed=moved, transcendentals=0),
    )(*operands)


def is_near(distance, count):
    return distance > count // 2


def shaped(shape, dtype):
    return jax.ShapeDtypeStruct(shape, dtype)


def serve_kernel(serve_ref, table_ref, out_ref, onehot, rows, whole, sems):
    parts = rows.shape[0]
    loads = [pltpu.make_async_copy(table_ref.at[i], rows.at[i], sems.at[i]) for i in range(parts)]
    for load in loads:
        load.start()
    serve = serve_ref.get()[...]
    lanes = lax.broadcasted_iota(jnp.int32, (LANES, onehot.shape[1]), 1)
    for block in range(serve.shape[1] // LANES):
        span = slice(block * LANES, (block + 1) * LANES)
        onehot[span, :] = jnp.where(row_to_column(serve[:, span]) == lanes, 1.0, 0.0).astype(BF16)
    for i, load in enumerate(loads):
        load.wait()
        whole[i * rows.shape[1] : (i + 1) * rows.shape[1], :] = rows[i].astype(BF16)
    out_ref[...] = matmul(onehot[...], whole[...]).astype(BF16).reshape(out_ref.shape)


def index_kernel(idx_ref, cot_ref, w2_ref, *refs):
    outs, spread = refs[:-1], refs[-1]
    ct_ref, c_ref, inv_ref, e_ref, back_ref = (o.buffer for o in outs)
    nodes = idx_ref.shape[0]
    slots = ct_ref.shape[1]
    seeds = cot_ref.shape[0]
    neighbours = idx_ref.shape[1] - 2
    lanes = lax.broadcasted_iota(jnp.int32, (nodes, 2 * slots), 1)
    idx = idx_ref[...]
    counts = jnp.zeros((nodes, 2 * slots), F32)
    for j in range(1, 1 + neighbours):
        counts = counts + jnp.where(idx[:, j : j + 1] == lanes, 1.0, 0.0)
    own = jnp.where(idx[:, 0:1] == lanes[:, :slots], 1.0, 0.0)
    parts = (own, counts[:, :slots], counts[:, slots:])
    spread[...] = jnp.zeros(spread.shape, F32)
    for k, part in enumerate(parts):
        span = slice(k * nodes, (k + 1) * nodes)
        ct_ref[span, :] = part.astype(BF16)
        c_ref[:, span] = jnp.transpose(part).astype(BF16)
        if k == 0:
            inverse = jnp.ones((nodes, 1), F32)
        else:
            inverse = 1.0 / jnp.maximum(jnp.sum(part, axis=1, keepdims=True), 1.0)
        inv_ref[span, :] = jnp.broadcast_to(inverse, (nodes, LANES))
        back = matmul(cot_ref[...], w2_ref[k], (1, 1))
        spread[k * seeds : (k + 1) * seeds, :] = back * inverse[:seeds]
    groups = lax.broadcasted_iota(jnp.int32, (nodes, LANES), 1)
    member = jnp.where(idx[:, neighbours + 1 : neighbours + 2] == groups, 1.0, 0.0)
    e_ref[...] = jnp.transpose(member)[:SEED_ROWS].astype(BF16)
    whole = spread[...]
    high = whole.astype(BF16)
    low = (whole - high.astype(F32)).astype(BF16)
    for out in outs[:-1]:
        out.send()
    back_ref[...] = matmul(member.astype(BF16), high) + matmul(member.astype(BF16), low)
    outs[-1].send()


def first_kernel(fetched_ref, ct_ref, w1_ref, layer_ref, partial_out, wide, partial_ref, sems):
    layers = w1_ref.shape[0]
    layer_out, layer_ref = layer_ref, layer_ref.buffer
    nodes = partial_ref.shape[0]
    fetched = fetched_ref.get()[...].reshape(ct_ref.shape[1], layer_ref.shape[1])
    ct_ref = ct_ref.get()
    ones = jnp.ones((ct_ref.shape[1], LANES), BF16)
    columns = layer_ref.shape[1]
    for k in range(layers):
        span = slice(k * nodes, (k + 1) * nodes)
        summed = matmul(ct_ref[span, :], fetched)
        inverse = 1.0 / jnp.maximum(matmul(ct_ref[span, :], ones)[:, 0:1], 1.0)
        layer = (summed * inverse).astype(BF16)
        layer_ref[span, :] = layer
        wide[:, k * columns : (k + 1) * columns] = layer
    layer_out.send()
    weights = w1_ref.get()[...].reshape(layers * columns, partial_ref.shape[1])
    half = partial_ref.shape[1] // 2
    copies = []
    for i in range(2):
        span = slice(i * half, (i + 1) * half)
        partial_ref[:, span] = matmul(wide[...], weights[:, span])
        copies.append(pltpu.make_async_copy(partial_ref.at[:, span], partial_out.at[:, span], sems.at[i]))
        copies[i].start()
    for copy in copies:
        copy.wait()


def hidden_kernel(place_ref, mine_ref, other_ref, back_ref, e_ref, inv_ref, cot_ref, c_ref, w1_ref, layer_ref, slot_ref, *refs):
    packs, (stage, scaled, sems) = refs[:-3], refs[-3:]
    nodes = mine_ref.shape[0]
    width = stage.shape[2]
    seeds = cot_ref.shape[0]
    layers = inv_ref.shape[0] // nodes
    values = mine_ref.get()[...] + other_ref.get()[...]
    back_ref, e_ref, inv_ref = back_ref.get(), e_ref.get(), inv_ref.get()
    sigma = jax.nn.sigmoid(values)
    hidden = (values * sigma).astype(BF16)
    slope = sigma * (1.0 + values * (1.0 - sigma))
    back = (back_ref[...] * slope).astype(BF16)
    scale = jnp.concatenate(
        [inv_ref[k * nodes : k * nodes + seeds, 0:1] for k in range(layers)]
        + [jnp.zeros((SEED_ROWS - layers * seeds, 1), F32)],
        0,
    )
    second = matmul(e_ref[...], hidden) * scale
    half = second.shape[1] // 2
    second = jnp.where(place_ref[0] == 0, second[:, :half], second[:, half:]).astype(BF16)
    cot = cot_ref[...].astype(F32)
    cot = jnp.concatenate([cot, jnp.zeros((COT_ROWS - seeds, cot.shape[1]), F32)], 0).astype(BF16)
    for j in range(len(packs)):
        span = slice(j * width, (j + 1) * width)
        stage[j, :nodes, :] = back[:, span]
        for part in range(half // width):
            first = nodes + part * SEED_ROWS
            stage[j, first : first + SEED_ROWS, :] = second[:, part * width : (part + 1) * width]
        first = nodes + half // width * SEED_ROWS
        stage[j, first : first + COT_ROWS, :] = cot[:, span]
    moves = []
    for d, pack in enumerate(packs):
        chosen = stage.at[lax.rem(place_ref[1] + d, len(packs))]
        if not is_near(d, len(packs)):
            moves.append((chosen, pack))
            continue
        start = 0
        for source in (chosen, layer_ref.get()):
            rows, wide = source.shape
            for lane in range(0, wide, LANES):
                moves.append((source.at[:, lane : lane + LANES], pack.at[start : start + rows, :]))
                start += rows
    layer_ref.get()
    copies = [pltpu.make_async_copy(source, target, sems.at[i]) for i, (source, target) in enumerate(moves)]
    for copy in copies:
        copy.start()
    columns = w1_ref.shape[1]
    back_in = matmul(back, w1_ref.get()[...].reshape(layers * columns, back.shape[1]), (1, 1))
    for k in range(layers):
        span = slice(k * nodes, (k + 1) * nodes)
        scaled[span, :] = (back_in[:, k * columns : (k + 1) * columns] * inv_ref[span, 0:1]).astype(BF16)
    slot_ref[...] = matmul(c_ref.get()[...], scaled[...]).astype(BF16).reshape(slot_ref.shape)
    for copy in copies:
        copy.wait()


def weight_kernel(count, place_ref, *refs):
    early = count // 2 + 1
    layer_refs, pack_refs = refs[:early], refs[early : early + count]
    refs = refs[early + count :]
    own_ref, second_ref, outs, total = refs[0], refs[1], refs[2:-1], refs[-1]
    pack_rows, width = pack_refs[0].shape
    layer_rows, columns = layer_refs[0].shape
    layer_parts, packs = [], []
    for d, ref in enumerate(pack_refs):
        if not is_near(d, count):
            packs.append(ref.get()[...])
            layer_parts.append(layer_refs[d].get()[...])
            continue
        near, start = ref.get()[...], 0
        for rows, wide, made in ((pack_rows, width, packs), (layer_rows, columns, layer_parts)):
            lanes = [near[start + i * rows : start + (i + 1) * rows] for i in range(wide // LANES)]
            made.append(jnp.concatenate(lanes, 1))
            start += rows * len(lanes)
    nodes = LANES
    relations = layer_rows // nodes
    rows = own_ref.shape[0]
    left = jnp.concatenate([p[:nodes, :] for p in packs], 0)
    for k in range(relations):
        right = jnp.concatenate([r[k * nodes : (k + 1) * nodes, :] for r in layer_parts], 0)
        total[k] = matmul(left, right, (0, 0))
    pieces = (pack_rows - nodes - COT_ROWS) // SEED_ROWS
    half = pieces * width
    seeds = SEED_ROWS // (relations + 1)
    first = nodes + pieces * SEED_ROWS
    cots = jnp.concatenate([p[first : first + COT_ROWS, :].astype(F32)[:seeds] for p in packs], 0)
    seconds = [
        jnp.concatenate(
            [p[nodes + part * SEED_ROWS : nodes + (part + 1) * SEED_ROWS, :].astype(F32) for part in range(pieces)],
            1,
        )
        for p in packs
    ]
    second = jnp.concatenate(
        [jnp.concatenate([s[k * seeds : (k + 1) * seeds] for s in seconds], 0) for k in range(relations)], 1
    ).astype(BF16)
    group = count * seeds
    per = columns // (group // COT_ROWS)
    for piece in range(relations * half // columns):
        second_ref[piece * group : (piece + 1) * group, :] = second[:, piece * columns : (piece + 1) * columns]
    for d, out in enumerate(outs):
        target = lax.rem(place_ref[0] + d, len(outs))
        start = pl.multiple_of(target * rows, rows)
        for k in range(relations):
            block = total[k, pl.ds(start, rows), :]
            if d == 0:
                own_ref[:, k * columns : (k + 1) * columns] = block
            else:
                out[k * rows : (k + 1) * rows, :] = block.astype(BF16)
        chosen = cots[:, :rows]
        for j in range(1, len(outs)):
            chosen = jnp.where(target == j, cots[:, j * rows : (j + 1) * rows], chosen)
        for piece in range(group // COT_ROWS):
            lanes = slice(piece * per, piece * per + rows)
            out[out.shape[0] - COT_ROWS :, lanes] = chosen[piece * COT_ROWS : (piece + 1) * COT_ROWS].astype(BF16)


def group_kernel(relations, own_ref, *refs):
    count = len(refs) // 2
    packs, seconds, out_ref = refs[:count], refs[count:-1], refs[-1]
    rows = own_ref.shape[0]
    columns = packs[0].shape[1]
    tail = relations * rows
    wide = out_ref.shape[1] - relations * columns
    pieces = wide // columns
    group = seconds[0].shape[0] // pieces
    per = columns // (group // COT_ROWS)
    for k in range(relations):
        span = slice(k * columns, (k + 1) * columns)
        block = own_ref[:, span]
        for pack in packs[1:]:
            block = block + pack[k * rows : (k + 1) * rows, :].astype(F32)
        out_ref[:, span] = block.astype(BF16)
    cots = jnp.concatenate(
        [
            p[tail:, piece * per : piece * per + rows]
            for p in packs
            for piece in range(group // COT_ROWS)
        ],
        0,
    )
    for piece in range(pieces):
        first = piece * group
        second = jnp.concatenate([p[first : first + group, :] for p in seconds], 0)
        start = (relations + piece) * columns
        out_ref[:, start : start + columns] = matmul(cots, second, (0, 0)).astype(BF16)


def sum_kernel(parts_ref, one_ref, two_ref):
    total = jnp.sum(parts_ref[...].astype(F32), axis=0)
    start = 0
    for ref in (one_ref, two_ref):
        wide = ref.shape[2]
        for k in range(ref.shape[0]):
            ref[k] = total[:, start : start + wide]
            start += wide


def row_kernel(serve_ref, arrived_ref, grad_ref, square_ref):
    rows = lax.broadcasted_iota(jnp.int32, (LANES, serve_ref.shape[1]), 0)
    arrived = arrived_ref[...].reshape(serve_ref.shape[1], grad_ref.shape[1])
    for block in range(grad_ref.shape[0] // LANES):
        span = slice(block * LANES, (block + 1) * LANES)
        onehot = jnp.where(serve_ref[...] == rows + block * LANES, 1.0, 0.0).astype(BF16)
        grad = matmul(onehot, arrived)
        grad_ref[span, :] = grad
        square_ref[block : block + 1, :] = column_to_row(jnp.sum(grad * grad, axis=1, keepdims=True))


def update_kernel(columns, table_ref, grad_ref, accum_ref, mine_ref, other_ref, table_out, accum_out):
    accum = accum_ref[...] + (mine_ref[...] + other_ref[...]) / columns
    accum_out[...] = accum
    inverse = lax.rsqrt(accum)
    for block in range(accum.shape[0]):
        span = slice(block * LANES, (block + 1) * LANES)
        scale = row_to_column(inverse[block : block + 1, :])
        table_out[span, :] = table_ref[span, :] - LEARNING_RATE * grad_ref[span, :] * scale


def shift(array, axis, by):
    size = lax.axis_size(axis)
    return lax.ppermute(array, axis, [(i, (i + by) % size) for i in range(size)])


LIMITS = {serve_kernel: 60, index_kernel: 60, first_kernel: 60, hidden_kernel: 60}
COSTS = {update_kernel: 0, group_kernel: 0, row_kernel: 0}


def body(
    table,
    accum,
    serve_rows,
    seed_slot,
    hop1_slot,
    hop2_slot,
    hop1_rel,
    hop2_rel,
    cotangent,
    w_first,
    w_second,
):
    everyone = ("dp", "y", "z")
    owners = lax.axis_size(everyone)
    table_rows, columns = table.shape
    slots = serve_rows.shape[1]
    seeds, fanout = hop1_slot.shape
    fanout_two = hop2_slot.shape[2]
    nodes = seeds + seeds * fanout
    layers, hidden_units = w_second.shape[:2]
    half = hidden_units // 2
    n_x, n_y, n_z = (lax.axis_size(a) for a in everyone)
    x, y = lax.axis_index("dp"), lax.axis_index("y")
    width = hidden_units // n_x

    blocks_shape = (owners, slots // owners, columns)
    parts = 4
    outgoing = call(
        serve_kernel,
        [shaped(blocks_shape, BF16)],
        (serve_rows, table.reshape(parts, table_rows // parts, columns)),
        scratch=[
            pltpu.VMEM((slots, table_rows), BF16),
            pltpu.VMEM((parts, table_rows // parts, columns), F32),
            pltpu.VMEM((table_rows, columns), BF16),
            pltpu.SemaphoreType.DMA((parts,)),
        ],
        hbm_in=(0,),
        raw_in=(1,),
    )[0]
    fetched = lax.all_to_all(outgoing, everyone, split_axis=0, concat_axis=0, tiled=True)

    key_one = hop1_slot + slots * hop1_rel
    key_two = (hop2_slot + slots * hop2_rel).reshape(seeds * fanout, fanout_two)
    seed_ids = jnp.arange(seeds, dtype=jnp.int32)[:, None]
    group = (seeds * (1 + hop1_rel) + seed_ids).reshape(-1, 1)
    spare = jnp.full((seeds * fanout, fanout - fanout_two), -1, jnp.int32)
    idx = jnp.concatenate(
        [
            jnp.concatenate([seed_slot[:, None], key_one, seed_ids], 1),
            jnp.concatenate([hop1_slot.reshape(-1, 1), key_two, spare, group], 1),
        ],
        0,
    )
    idx, place, y = lax.optimization_barrier((idx, jnp.stack([lax.axis_index("col"), x]), y))
    ct, c, inverse, member, back_hidden = call(
        index_kernel,
        [
            shaped((layers * nodes, slots), BF16),
            shaped((slots, layers * nodes), BF16),
            shaped((layers * nodes, LANES), F32),
            shaped((SEED_ROWS, nodes), BF16),
            shaped((nodes, hidden_units), F32),
        ],
        (idx, cotangent, w_second),
        scratch=[pltpu.VMEM((LANES, hidden_units), F32)],
        hbm_out=range(5),
    )

    layer_in, partial_pre = call(
        first_kernel,
        [shaped((layers * nodes, columns), BF16), shaped((nodes, hidden_units), F32)],
        (fetched, ct, w_first),
        scratch=[
            pltpu.VMEM((nodes, layers * columns), BF16),
            pltpu.VMEM((nodes, hidden_units), F32),
            pltpu.SemaphoreType.DMA((2,)),
        ],
        hbm_in=(0, 1, 2),
        hbm_out=(0,),
        hbm_raw=(1,),
    )
    other_pre = shift(partial_pre, "col", 1)
    layer_parts = [layer_in] + [shift(layer_in, "dp", d) for d in range(1, n_x // 2 + 1)]

    pack_rows = nodes + half // width * SEED_ROWS + COT_ROWS
    pack_shape = (pack_rows, width)
    near_shape = ((pack_rows * width + layers * nodes * columns) // LANES, LANES)
    slot_grad, *packs = call(
        hidden_kernel,
        [shaped(blocks_shape, BF16)] + [shaped(near_shape if is_near(d, n_x) else pack_shape, BF16) for d in range(n_x)],
        (
            place,
            partial_pre,
            other_pre,
            back_hidden,
            member,
            inverse,
            cotangent,
            c,
            w_first,
            layer_in,
        ),
        smem=1,
        scratch=[
            pltpu.VMEM((n_x, *pack_shape), BF16),
            pltpu.VMEM((layers * nodes, columns), BF16),
            pltpu.SemaphoreType.DMA((n_x * (width + columns) // LANES,)),
        ],
        hbm_in=(1, 2, 3, 4, 5, 9, 8, 7),
        hbm_raw=range(1, 1 + n_x),
    )
    packs[n_x // 2], layer_parts = lax.optimization_barrier((packs[n_x // 2], layer_parts))
    packs = [packs[0]] + [shift(packs[d], "dp", d) for d in range(1, n_x)]
    arrived = lax.all_to_all(slot_grad, everyone, split_axis=0, concat_axis=0, tiled=True)

    block_rows = width // n_y
    group_rows = layers * block_rows + COT_ROWS
    second_rows = (layers * half // columns) * n_x * seeds
    own, second, *blocks = call(
        functools.partial(weight_kernel, n_x),
        [shaped((block_rows, layers * columns), F32), shaped((second_rows, columns), BF16)]
        + [shaped((group_rows, columns), BF16)] * n_y,
        (y.reshape(1), *layer_parts, *packs),
        smem=1,
        hbm_in=range(1, 2 + n_x // 2 + n_x),
        scratch=[pltpu.VMEM((layers, width, columns), F32)],
    )
    seconds = [second, shift(second, "y", 1)]
    if n_y > 2:
        last = shift(second, "y", n_y - 1)
        seconds += [shift(last, "y", n_y - 1), last]
    blocks = [blocks[0]] + [shift(blocks[d], "y", d) for d in range(1, n_y)]
    grad_columns = layers * (columns + half)
    grads = call(
        functools.partial(group_kernel, layers),
        [shaped((block_rows, grad_columns), BF16)],
        (own, *blocks, *seconds),
    )[0]
    grads = grads.reshape(n_z, block_rows // n_z, grad_columns)
    grads = lax.all_to_all(grads, "z", split_axis=0, concat_axis=0, tiled=True)
    grad_one, grad_two = call(
        sum_kernel,
        [shaped((layers, block_rows // n_z, wide), F32) for wide in (columns, half)],
        (grads,),
    )
    grad_one, grad_two = grad_one.transpose(0, 2, 1), grad_two.transpose(0, 2, 1)

    row_grad, squares = call(
        row_kernel,
        [shaped((table_rows, columns), F32), shaped((table_rows // LANES, LANES), F32)],
        (serve_rows, arrived),
    )
    other_squares = shift(squares, "col", 1)
    new_table, new_accum = call(
        functools.partial(update_kernel, 2 * columns),
        [shaped((table_rows, columns), F32), shaped((table_rows // LANES, LANES), F32)],
        (table, row_grad, accum.reshape(-1, LANES), squares, other_squares),
    )
    return (new_table, new_accum.reshape(-1), grad_one, grad_two)


def solution(mesh):
    n_dp, n_table, n_col = (mesh.shape[a] for a in ("dp", "table", "col"))
    n_y = 4 if n_table % 4 == 0 and n_table > 4 else 2
    fine = Mesh(mesh.devices.reshape(n_dp, n_y, n_table // n_y, n_col), ("dp", "y", "z", "col"))
    rows = ("dp", "y", "z")
    placed = (
        P(rows, "col"),
        P(rows),
        P(rows, None),
        P(rows),
        P(rows, None),
        P(rows, None, None),
        P(rows, None),
        P(rows, None, None),
        P(rows, None),
        P(None, "col", None),
        P(),
    )
    return jax.shard_map(
        body,
        mesh=fine,
        in_specs=placed,
        out_specs=(P(rows, "col"), P(rows), P(None, "col", rows), P(None, "col", rows)),
        check_vma=False,
    )
```

```python
import functools
import jax
import jax.numpy as jnp
from jax import lax
from jax.experimental import pallas as pl
from jax.experimental.pallas import tpu as pltpu
from jax.sharding import Mesh
from jax.sharding import PartitionSpec as P

LEARNING_RATE = 0.1
BF16 = jnp.bfloat16
F32 = jnp.float32
LANES = 128
SEED_ROWS = 32
COT_ROWS = 16


def matmul(a, b, contract=(1, 0)):
    dims = (((contract[0],), (contract[1],)), ((), ()))
    return lax.dot_general(a, b, dims, preferred_element_type=F32)


def row_to_column(row):
    return jnp.transpose(jnp.broadcast_to(row, (LANES, LANES)))[:, 0:1]


def column_to_row(column):
    return jnp.transpose(jnp.broadcast_to(column, (LANES, LANES)))[0:1, :]


class Incoming:
    def __init__(self, source, buffer, semaphore):
        self.buffer, self.waiting = buffer, True
        self.shape = buffer.shape
        self.copy = pltpu.make_async_copy(source, buffer, semaphore)
        self.copy.start()

    def get(self):
        if self.waiting:
            self.copy.wait()
        self.waiting = False
        return self.buffer


class Outgoing:
    def __init__(self, target, buffer, semaphore):
        self.buffer = buffer
        self.copy = pltpu.make_async_copy(buffer, target, semaphore)

    def send(self):
        self.copy.start()


def call(kernel, outs, operands, smem=0, scratch=(), hbm_in=(), hbm_out=(), raw_in=(), hbm_raw=()):
    name = getattr(kernel, "func", kernel)
    limit, flops = LIMITS.get(name, 12), COSTS.get(name, 10**12)
    moved = sum(o.size * o.dtype.itemsize for o in list(operands) + list(outs))
    specs = [
        pl.BlockSpec(memory_space=pltpu.SMEM if i < smem else pltpu.HBM if i in hbm_in or i in raw_in else pltpu.VMEM)
        for i in range(len(operands))
    ]
    made = [
        pl.BlockSpec(memory_space=pltpu.HBM if i in hbm_out or i in hbm_raw else pltpu.VMEM)
        for i in range(len(outs))
    ]
    buffers = [pltpu.VMEM(operands[i].shape, operands[i].dtype) for i in hbm_in]
    buffers += [pltpu.VMEM(outs[i].shape, outs[i].dtype) for i in hbm_out]
    semaphores = [pltpu.SemaphoreType.DMA((len(buffers),))] if buffers else []

    def wrapped(*refs):
        refs = list(refs)
        if not buffers:
            kernel(*refs)
            return
        first = len(operands) + len(outs)
        held, sems = refs[first : first + len(buffers)], refs[first + len(buffers)]
        rest = refs[first + len(buffers) + 1 :]
        for j, i in enumerate(hbm_in):
            refs[i] = Incoming(refs[i], held[j], sems.at[j])
        leaving = []
        for j, i in enumerate(hbm_out, len(hbm_in)):
            place = len(operands) + i
            refs[place] = Outgoing(refs[place], held[j], sems.at[j])
            leaving.append(refs[place])
        kernel(*refs[:first], *rest)
        for out in leaving:
            out.copy.wait()

    return pl.pallas_call(
        wrapped,
        out_shape=tuple(outs),
        in_specs=specs,
        out_specs=tuple(made),
        scratch_shapes=buffers + semaphores + list(scratch),
        compiler_params=pltpu.CompilerParams(vmem_limit_bytes=int(limit * 1024 * 1024)),
        cost_estimate=pl.CostEstimate(flops=flops, bytes_accessed=moved, transcendentals=0),
    )(*operands)


def is_near(distance, count):
    return distance not in (0, count // 2)


def shaped(shape, dtype):
    return jax.ShapeDtypeStruct(shape, dtype)


def serve_kernel(serve_ref, table_ref, out_ref, onehot, rows, whole, sems):
    parts = rows.shape[0]
    loads = [pltpu.make_async_copy(table_ref.at[i], rows.at[i], sems.at[i]) for i in range(parts)]
    for load in loads:
        load.start()
    serve = serve_ref.get()[...]
    lanes = lax.broadcasted_iota(jnp.int32, (LANES, onehot.shape[1]), 1)
    for block in range(serve.shape[1] // LANES):
        span = slice(block * LANES, (block + 1) * LANES)
        onehot[span, :] = jnp.where(row_to_column(serve[:, span]) == lanes, 1.0, 0.0).astype(BF16)
    for i, load in enumerate(loads):
        load.wait()
        whole[i * rows.shape[1] : (i + 1) * rows.shape[1], :] = rows[i].astype(BF16)
    out_ref[...] = matmul(onehot[...], whole[...]).astype(BF16).reshape(out_ref.shape)


def index_kernel(idx_ref, cot_ref, w2_ref, *refs):
    outs, spread = refs[:-1], refs[-1]
    ct_ref, c_ref, inv_ref, e_ref, back_ref = (o.buffer for o in outs)
    nodes = idx_ref.shape[0]
    slots = ct_ref.shape[1]
    seeds = cot_ref.shape[0]
    neighbours = idx_ref.shape[1] - 2
    lanes = lax.broadcasted_iota(jnp.int32, (nodes, 2 * slots), 1)
    idx = idx_ref[...]
    counts = jnp.zeros((nodes, 2 * slots), F32)
    for j in range(1, 1 + neighbours):
        counts = counts + jnp.where(idx[:, j : j + 1] == lanes, 1.0, 0.0)
    own = jnp.where(idx[:, 0:1] == lanes[:, :slots], 1.0, 0.0)
    parts = (own, counts[:, :slots], counts[:, slots:])
    spread[...] = jnp.zeros(spread.shape, F32)
    for k, part in enumerate(parts):
        span = slice(k * nodes, (k + 1) * nodes)
        ct_ref[span, :] = part.astype(BF16)
        c_ref[:, span] = jnp.transpose(part).astype(BF16)
        if k == 0:
            inverse = jnp.ones((nodes, 1), F32)
        else:
            inverse = 1.0 / jnp.maximum(jnp.sum(part, axis=1, keepdims=True), 1.0)
        inv_ref[span, :] = jnp.broadcast_to(inverse, (nodes, LANES))
        back = matmul(cot_ref[...], w2_ref[k], (1, 1))
        spread[k * seeds : (k + 1) * seeds, :] = back * inverse[:seeds]
    groups = lax.broadcasted_iota(jnp.int32, (nodes, LANES), 1)
    member = jnp.where(idx[:, neighbours + 1 : neighbours + 2] == groups, 1.0, 0.0)
    e_ref[...] = jnp.transpose(member)[:SEED_ROWS].astype(BF16)
    whole = spread[...]
    high = whole.astype(BF16)
    low = (whole - high.astype(F32)).astype(BF16)
    for out in outs[:-1]:
        out.send()
    back_ref[...] = matmul(member.astype(BF16), high) + matmul(member.astype(BF16), low)
    outs[-1].send()


def first_kernel(fetched_ref, ct_ref, w1_ref, layer_ref, partial_out, wide, partial_ref, sems):
    layers = w1_ref.shape[0]
    layer_out, layer_ref = layer_ref, layer_ref.buffer
    nodes = partial_ref.shape[0]
    fetched = fetched_ref.get()[...].reshape(ct_ref.shape[1], layer_ref.shape[1])
    ct_ref = ct_ref.get()
    ones = jnp.ones((ct_ref.shape[1], LANES), BF16)
    columns = layer_ref.shape[1]
    for k in range(layers):
        span = slice(k * nodes, (k + 1) * nodes)
        summed = matmul(ct_ref[span, :], fetched)
        inverse = 1.0 / jnp.maximum(matmul(ct_ref[span, :], ones)[:, 0:1], 1.0)
        layer = (summed * inverse).astype(BF16)
        layer_ref[span, :] = layer
        wide[:, k * columns : (k + 1) * columns] = layer
    layer_out.send()
    weights = w1_ref.get()[...].reshape(layers * columns, partial_ref.shape[1])
    half = partial_ref.shape[1] // 2
    copies = []
    for i in range(2):
        span = slice(i * half, (i + 1) * half)
        partial_ref[:, span] = matmul(wide[...], weights[:, span])
        copies.append(pltpu.make_async_copy(partial_ref.at[:, span], partial_out.at[:, span], sems.at[i]))
        copies[i].start()
    for copy in copies:
        copy.wait()


def hidden_kernel(place_ref, mine_ref, other_ref, back_ref, e_ref, inv_ref, cot_ref, layer_ref, out_ref, *refs):
    packs, (stage, sems) = refs[:-2], refs[-2:]
    nodes = mine_ref.shape[0]
    width = stage.shape[2]
    seeds = cot_ref.shape[0]
    layers = inv_ref.shape[0] // nodes
    values = mine_ref.get()[...] + other_ref.get()[...]
    back_ref, e_ref, inv_ref = back_ref.get(), e_ref.get(), inv_ref.get()
    sigma = jax.nn.sigmoid(values)
    hidden = (values * sigma).astype(BF16)
    slope = sigma * (1.0 + values * (1.0 - sigma))
    back = (back_ref[...] * slope).astype(BF16)
    out_ref[...] = back
    scale = jnp.concatenate(
        [inv_ref[k * nodes : k * nodes + seeds, 0:1] for k in range(layers)]
        + [jnp.zeros((SEED_ROWS - layers * seeds, 1), F32)],
        0,
    )
    second = matmul(e_ref[...], hidden) * scale
    half = second.shape[1] // 2
    second = jnp.where(place_ref[0] == 0, second[:, :half], second[:, half:]).astype(BF16)
    cot = cot_ref[...].astype(F32)
    cot = jnp.concatenate([cot, jnp.zeros((COT_ROWS - seeds, cot.shape[1]), F32)], 0).astype(BF16)
    for j in range(len(packs)):
        span = slice(j * width, (j + 1) * width)
        stage[j, :nodes, :] = back[:, span]
        for part in range(half // width):
            first = nodes + part * SEED_ROWS
            stage[j, first : first + SEED_ROWS, :] = second[:, part * width : (part + 1) * width]
        first = nodes + half // width * SEED_ROWS
        stage[j, first : first + COT_ROWS, :] = cot[:, span]
    moves = []
    for d, pack in enumerate(packs):
        chosen = stage.at[lax.rem(place_ref[1] + d, len(packs))]
        if not is_near(d, len(packs)):
            moves.append((chosen, pack))
            continue
        start = 0
        for source in (chosen, layer_ref.get()):
            rows, wide = source.shape
            for lane in range(0, wide, LANES):
                moves.append((source.at[:, lane : lane + LANES], pack.at[start : start + rows, :]))
                start += rows
    layer_ref.get()
    copies = [pltpu.make_async_copy(source, target, sems.at[i]) for i, (source, target) in enumerate(moves)]
    for copy in copies:
        copy.start()
    for copy in copies:
        copy.wait()


def slot_kernel(back_ref, inv_ref, c_ref, w1_ref, slot_ref, scaled):
    layers, columns, hidden = w1_ref.shape
    nodes = back_ref.shape[0]
    back_in = matmul(back_ref.get()[...], w1_ref.get()[...].reshape(layers * columns, hidden), (1, 1))
    for k in range(layers):
        span = slice(k * nodes, (k + 1) * nodes)
        scaled[span, :] = (back_in[:, k * columns : (k + 1) * columns] * inv_ref.get()[span, 0:1]).astype(BF16)
    slot_ref[...] = matmul(c_ref.get()[...], scaled[...]).astype(BF16).reshape(slot_ref.shape)


def weight_kernel(count, place_ref, *refs):
    layer_refs, pack_refs = refs[:2], refs[2 : 2 + count]
    own_ref, second_ref, outs, total = refs[2 + count], refs[3 + count], refs[4 + count : -1], refs[-1]
    pack_rows, width = pack_refs[0].shape
    layer_rows, columns = layer_refs[0].shape
    layer_parts, packs = [], []
    for d, ref in enumerate(pack_refs):
        if not is_near(d, count):
            packs.append(ref.get()[...])
            layer_parts.append(layer_refs[min(d, 1)].get()[...])
            continue
        near, start = ref.get()[...], 0
        for rows, wide, made in ((pack_rows, width, packs), (layer_rows, columns, layer_parts)):
            lanes = [near[start + i * rows : start + (i + 1) * rows] for i in range(wide // LANES)]
            made.append(jnp.concatenate(lanes, 1))
            start += rows * len(lanes)
    nodes = LANES
    relations = layer_rows // nodes
    rows = own_ref.shape[0]
    left = jnp.concatenate([p[:nodes, :] for p in packs], 0)
    for k in range(relations):
        right = jnp.concatenate([r[k * nodes : (k + 1) * nodes, :] for r in layer_parts], 0)
        total[k] = matmul(left, right, (0, 0))
    pieces = (pack_rows - nodes - COT_ROWS) // SEED_ROWS
    half = pieces * width
    seeds = SEED_ROWS // (relations + 1)
    first = nodes + pieces * SEED_ROWS
    cots = jnp.concatenate([p[first : first + COT_ROWS, :].astype(F32)[:seeds] for p in packs], 0)
    seconds = [
        jnp.concatenate(
            [p[nodes + part * SEED_ROWS : nodes + (part + 1) * SEED_ROWS, :].astype(F32) for part in range(pieces)],
            1,
        )
        for p in packs
    ]
    second = jnp.concatenate(
        [jnp.concatenate([s[k * seeds : (k + 1) * seeds] for s in seconds], 0) for k in range(relations)], 1
    ).astype(BF16)
    group = count * seeds
    per = columns // (group // COT_ROWS)
    for piece in range(relations * half // columns):
        second_ref[piece * group : (piece + 1) * group, :] = second[:, piece * columns : (piece + 1) * columns]
    for d, out in enumerate(outs):
        target = lax.rem(place_ref[0] + d, len(outs))
        start = pl.multiple_of(target * rows, rows)
        for k in range(relations):
            block = total[k, pl.ds(start, rows), :]
            if d == 0:
                own_ref[:, k * columns : (k + 1) * columns] = block
            else:
                out[k * rows : (k + 1) * rows, :] = block.astype(BF16)
        chosen = cots[:, :rows]
        for j in range(1, len(outs)):
            chosen = jnp.where(target == j, cots[:, j * rows : (j + 1) * rows], chosen)
        for piece in range(group // COT_ROWS):
            lanes = slice(piece * per, piece * per + rows)
            out[out.shape[0] - COT_ROWS :, lanes] = chosen[piece * COT_ROWS : (piece + 1) * COT_ROWS].astype(BF16)


def group_kernel(relations, own_ref, *refs):
    count = len(refs) // 2
    packs, seconds, out_ref = refs[:count], refs[count:-1], refs[-1]
    rows = own_ref.shape[0]
    columns = packs[0].shape[1]
    tail = relations * rows
    wide = out_ref.shape[1] - relations * columns
    pieces = wide // columns
    group = seconds[0].shape[0] // pieces
    per = columns // (group // COT_ROWS)
    for k in range(relations):
        span = slice(k * columns, (k + 1) * columns)
        block = own_ref[:, span]
        for pack in packs[1:]:
            block = block + pack[k * rows : (k + 1) * rows, :].astype(F32)
        out_ref[:, span] = block.astype(BF16)
    cots = jnp.concatenate(
        [
            p[tail:, piece * per : piece * per + rows]
            for p in packs
            for piece in range(group // COT_ROWS)
        ],
        0,
    )
    for piece in range(pieces):
        first = piece * group
        second = jnp.concatenate([p[first : first + group, :] for p in seconds], 0)
        start = (relations + piece) * columns
        out_ref[:, start : start + columns] = matmul(cots, second, (0, 0)).astype(BF16)


def sum_kernel(parts_ref, one_ref, two_ref):
    total = jnp.sum(parts_ref[...].astype(F32), axis=0)
    start = 0
    for ref in (one_ref, two_ref):
        wide = ref.shape[2]
        for k in range(ref.shape[0]):
            ref[k] = total[:, start : start + wide]
            start += wide


def row_kernel(serve_ref, arrived_ref, grad_ref, square_ref):
    rows = lax.broadcasted_iota(jnp.int32, (LANES, serve_ref.shape[1]), 0)
    arrived = arrived_ref[...].reshape(serve_ref.shape[1], grad_ref.shape[1])
    for block in range(grad_ref.shape[0] // LANES):
        span = slice(block * LANES, (block + 1) * LANES)
        onehot = jnp.where(serve_ref[...] == rows + block * LANES, 1.0, 0.0).astype(BF16)
        grad = matmul(onehot, arrived)
        grad_ref[span, :] = grad
        square_ref[block : block + 1, :] = column_to_row(jnp.sum(grad * grad, axis=1, keepdims=True))


def update_kernel(columns, table_ref, grad_ref, accum_ref, mine_ref, other_ref, table_out, accum_out):
    accum = accum_ref[...] + (mine_ref[...] + other_ref[...]) / columns
    accum_out[...] = accum
    inverse = lax.rsqrt(accum)
    for block in range(accum.shape[0]):
        span = slice(block * LANES, (block + 1) * LANES)
        scale = row_to_column(inverse[block : block + 1, :])
        table_out[span, :] = table_ref[span, :] - LEARNING_RATE * grad_ref[span, :] * scale


def shift(array, axis, by):
    size = lax.axis_size(axis)
    return lax.ppermute(array, axis, [(i, (i + by) % size) for i in range(size)])


LIMITS = {serve_kernel: 60, index_kernel: 60, first_kernel: 60, hidden_kernel: 60, slot_kernel: 60}
COSTS = {update_kernel: 0, group_kernel: 0, row_kernel: 0}


def body(
    table,
    accum,
    serve_rows,
    seed_slot,
    hop1_slot,
    hop2_slot,
    hop1_rel,
    hop2_rel,
    cotangent,
    w_first,
    w_second,
):
    everyone = ("dp", "y", "z")
    owners = lax.axis_size(everyone)
    table_rows, columns = table.shape
    slots = serve_rows.shape[1]
    seeds, fanout = hop1_slot.shape
    fanout_two = hop2_slot.shape[2]
    nodes = seeds + seeds * fanout
    layers, hidden_units = w_second.shape[:2]
    half = hidden_units // 2
    n_x, n_y, n_z = (lax.axis_size(a) for a in everyone)
    x, y = lax.axis_index("dp"), lax.axis_index("y")
    width = hidden_units // n_x

    blocks_shape = (owners, slots // owners, columns)
    parts = 4
    outgoing = call(
        serve_kernel,
        [shaped(blocks_shape, BF16)],
        (serve_rows, table.reshape(parts, table_rows // parts, columns)),
        scratch=[
            pltpu.VMEM((slots, table_rows), BF16),
            pltpu.VMEM((parts, table_rows // parts, columns), F32),
            pltpu.VMEM((table_rows, columns), BF16),
            pltpu.SemaphoreType.DMA((parts,)),
        ],
        hbm_in=(0,),
        raw_in=(1,),
    )[0]
    fetched = lax.all_to_all(outgoing, everyone, split_axis=0, concat_axis=0, tiled=True)

    key_one = hop1_slot + slots * hop1_rel
    key_two = (hop2_slot + slots * hop2_rel).reshape(seeds * fanout, fanout_two)
    seed_ids = jnp.arange(seeds, dtype=jnp.int32)[:, None]
    group = (seeds * (1 + hop1_rel) + seed_ids).reshape(-1, 1)
    spare = jnp.full((seeds * fanout, fanout - fanout_two), -1, jnp.int32)
    idx = jnp.concatenate(
        [
            jnp.concatenate([seed_slot[:, None], key_one, seed_ids], 1),
            jnp.concatenate([hop1_slot.reshape(-1, 1), key_two, spare, group], 1),
        ],
        0,
    )
    idx, place, y = lax.optimization_barrier((idx, jnp.stack([lax.axis_index("col"), x]), y))
    ct, c, inverse, member, back_hidden = call(
        index_kernel,
        [
            shaped((layers * nodes, slots), BF16),
            shaped((slots, layers * nodes), BF16),
            shaped((layers * nodes, LANES), F32),
            shaped((SEED_ROWS, nodes), BF16),
            shaped((nodes, hidden_units), F32),
        ],
        (idx, cotangent, w_second),
        scratch=[pltpu.VMEM((LANES, hidden_units), F32)],
        hbm_out=range(5),
    )

    layer_in, partial_pre = call(
        first_kernel,
        [shaped((layers * nodes, columns), BF16), shaped((nodes, hidden_units), F32)],
        (fetched, ct, w_first),
        scratch=[
            pltpu.VMEM((nodes, layers * columns), BF16),
            pltpu.VMEM((nodes, hidden_units), F32),
            pltpu.SemaphoreType.DMA((2,)),
        ],
        hbm_in=(0, 1, 2),
        hbm_out=(0,),
        hbm_raw=(1,),
    )
    other_pre = shift(partial_pre, "col", 1)
    layer_parts = [layer_in, shift(layer_in, "dp", n_x // 2)]

    pack_rows = nodes + half // width * SEED_ROWS + COT_ROWS
    pack_shape = (pack_rows, width)
    near_shape = ((pack_rows * width + layers * nodes * columns) // LANES, LANES)
    back, *packs = call(
        hidden_kernel,
        [shaped((nodes, hidden_units), BF16)] + [shaped(near_shape if is_near(d, n_x) else pack_shape, BF16) for d in range(n_x)],
        (
            place,
            partial_pre,
            other_pre,
            back_hidden,
            member,
            inverse,
            cotangent,
            layer_in,
        ),
        smem=1,
        scratch=[
            pltpu.VMEM((n_x, *pack_shape), BF16),
            pltpu.SemaphoreType.DMA((n_x * (width + columns) // LANES,)),
        ],
        hbm_in=(1, 2, 3, 4, 5, 7),
        hbm_raw=range(1, 1 + n_x),
    )
    packs = [packs[0]] + [shift(packs[d], "dp", d) for d in range(1, n_x)]
    slot_grad = call(
        slot_kernel,
        [shaped(blocks_shape, BF16)],
        (back, inverse, c, w_first),
        scratch=[pltpu.VMEM((layers * nodes, columns), BF16)],
        hbm_in=(0, 3, 1, 2),
    )[0]
    slot_grad, layer_parts = lax.optimization_barrier((slot_grad, layer_parts))
    arrived = lax.all_to_all(slot_grad, everyone, split_axis=0, concat_axis=0, tiled=True)

    block_rows = width // n_y
    group_rows = layers * block_rows + COT_ROWS
    second_rows = (layers * half // columns) * n_x * seeds
    own, second, *blocks = call(
        functools.partial(weight_kernel, n_x),
        [shaped((block_rows, layers * columns), F32), shaped((second_rows, columns), BF16)]
        + [shaped((group_rows, columns), BF16)] * n_y,
        (y.reshape(1), *layer_parts, *packs),
        smem=1,
        hbm_in=range(1, 3 + n_x),
        scratch=[pltpu.VMEM((layers, width, columns), F32)],
    )
    seconds = [second, shift(second, "y", 1)]
    if n_y > 2:
        last = shift(second, "y", n_y - 1)
        seconds += [shift(last, "y", n_y - 1), last]
    blocks = [blocks[0]] + [shift(blocks[d], "y", d) for d in range(1, n_y)]
    grad_columns = layers * (columns + half)
    grads = call(
        functools.partial(group_kernel, layers),
        [shaped((block_rows, grad_columns), BF16)],
        (own, *blocks, *seconds),
    )[0]
    grads = grads.reshape(n_z, block_rows // n_z, grad_columns)
    grads = lax.all_to_all(grads, "z", split_axis=0, concat_axis=0, tiled=True)
    grad_one, grad_two = call(
        sum_kernel,
        [shaped((layers, block_rows // n_z, wide), F32) for wide in (columns, half)],
        (grads,),
    )
    grad_one, grad_two = grad_one.transpose(0, 2, 1), grad_two.transpose(0, 2, 1)

    row_grad, squares = call(
        row_kernel,
        [shaped((table_rows, columns), F32), shaped((table_rows // LANES, LANES), F32)],
        (serve_rows, arrived),
    )
    other_squares = shift(squares, "col", 1)
    new_table, new_accum = call(
        functools.partial(update_kernel, 2 * columns),
        [shaped((table_rows, columns), F32), shaped((table_rows // LANES, LANES), F32)],
        (table, row_grad, accum.reshape(-1, LANES), squares, other_squares),
    )
    return (new_table, new_accum.reshape(-1), grad_one, grad_two)


def solution(mesh):
    n_dp, n_table, n_col = (mesh.shape[a] for a in ("dp", "table", "col"))
    n_y = 4 if n_table % 4 == 0 and n_table > 4 else 2
    fine = Mesh(mesh.devices.reshape(n_dp, n_y, n_table // n_y, n_col), ("dp", "y", "z", "col"))
    rows = ("dp", "y", "z")
    placed = (
        P(rows, "col"),
        P(rows),
        P(rows, None),
        P(rows),
        P(rows, None),
        P(rows, None, None),
        P(rows, None),
        P(rows, None, None),
        P(rows, None),
        P(None, "col", None),
        P(),
    )
    return jax.shard_map(
        body,
        mesh=fine,
        in_specs=placed,
        out_specs=(P(rows, "col"), P(rows), P(None, "col", rows), P(None, "col", rows)),
        check_vma=False,
    )
```
